512 devices in a mesh: lat: 32 (over y, z_hi), lon: 16 (over x, z_lo, core).
Axes of the slice: x: 4, y: 8, z: 8 (z_hi: 4, z_lo: 2; z = z_hi * 2 + z_lo), core: 2. Of those that a mesh axis runs over, the one named last changes fastest.
Arguments:
- tokens: bfloat16 [128, 512, 384], P('lat', 'lon'), may hold values from -6 to 6
- w_qkv: bfloat16 [384, 1152], replicated, may hold values from -0.3125 to 0.3125
- w_out: bfloat16 [384, 384], replicated, may hold values from -0.3125 to 0.3125
- w_disco: bfloat16 [768, 384], replicated, may hold values from -0.21875 to 0.21875
- psi: float32 [128, 18], P('lat'), may hold values from -2 to 2
- reach: int32 [128], P('lat'), may hold values from 1 to 32, as said below
- key_bias: float32 [128, 8], replicated, may hold values from -4 to 300
- cotangent: bfloat16 [128, 512, 384], P('lat', 'lon'), may hold values from -6 to 6
Outputs:
- mixed_out: bfloat16 [128, 512, 384], P('lat', 'lon')
- input_grad: bfloat16 [128, 512, 384], P('lat', 'lon')
- weight_grads: float32 [884736], P(('lat', 'lon'))
The draws below stay inside these ranges and needn't reach their ends.
Inputs may be any that keep to these rules, and one draw needn't show every extreme that they name: `reach`: at most 32 in the first and last 8 rows, where some row reaches 32; at most 8 in all other rows, where some row reaches 8.
All inputs are finite; a program needn't handle non-finite values.
Results may differ from the reference program's by a relative error of at most 0.0073.
Values may be sent and summed in bfloat16 or wider, within the bound.
A program may use at most 64 MiB of HBM per device.

```python
import jax
import jax.numpy as jnp
from jax import lax

C = 384
HEADS = 8
BASIS = 2
LAT_DEV = 4
LON_DEV = 32
NLAT = 128
NLON = 512
N_LAT = 32
N_LON = 16


def draw_reach(key, part):
    key = jax.random.fold_in(key, 11)
    wide_key, narrow_key = jax.random.split(key)
    all_rows = jnp.arange(NLAT, dtype=jnp.int32)
    polar_rows = (all_rows < 2 * LAT_DEV) | (all_rows >= NLAT - 2 * LAT_DEV)
    wide_steps = jax.random.randint(wide_key, (NLAT,), LON_DEV // 2, LON_DEV + 1)
    narrow_steps = jax.random.randint(narrow_key, (NLAT,), 1, LON_DEV // 4 + 1)
    picked = jnp.where(polar_rows, wide_steps, narrow_steps)
    picked = picked.at[0].set(LON_DEV)
    picked = picked.at[NLAT // 2].set(LON_DEV // 4)
    return picked.astype(jnp.int32)


def draw_key_bias(key, part):
    key = jax.random.fold_in(key, 23)
    base_key = jax.random.fold_in(key, 0)
    return jax.random.uniform(base_key, (NLAT, HEADS), jnp.float32, -2.0, 2.0)


def block_levels(stream_key, extent, shards, low, largest):
    loudness, own = 1.0, jax.random.fold_in(stream_key, 6)
    for position, parts in shards:
        heights = jnp.exp(jax.random.uniform(jax.random.fold_in(own, position), (parts,), jnp.float32, low / len(shards), largest / len(shards)))
        loudness = loudness * jnp.repeat(heights, extent[position] // parts).reshape([-1 if axis == position else 1 for axis in range(len(extent))])
    return loudness


def normal_values(own_key, shape, deviation, most, cuts=(), kind=jnp.bfloat16):
    values = jax.random.normal(own_key, shape, jnp.float32) * deviation
    if len(cuts) > 0:
        values = block_levels(own_key, shape, cuts, -0.22, 0.18) * values
    return jnp.clip(values, min=-most, max=most).astype(kind)


def setup_inputs(seed: int = 0) -> dict:
    keys = jax.random.split(jax.random.key(seed), 9)
    tokens = normal_values(keys[0], (NLAT, NLON, C), 1.0, 6.0, ((0, 32), (1, 16)))
    w_qkv = normal_values(keys[1], (C, 3 * C), C ** -0.5, 0.3125)
    w_out = normal_values(keys[2], (C, C), C ** -0.5, 0.3125)
    w_disco = normal_values(keys[3], (BASIS * C, C), (BASIS * C) ** -0.5, 0.21875)
    psi = normal_values(keys[4], (NLAT, 9 * BASIS), 0.33, 2.0, ((0, 32),), jnp.float32)
    reach = draw_reach(jax.random.fold_in(keys[8], 71), 0)
    key_bias = draw_key_bias(jax.random.fold_in(keys[8], 71), 0)
    cotangent = normal_values(keys[7], (NLAT, NLON, C), 1.0, 6.0, ((0, 32), (1, 16)))
    return {"tokens": tokens, "w_qkv": w_qkv, "w_out": w_out, "w_disco": w_disco, "psi": psi, "reach": reach, "key_bias": key_bias, "cotangent": cotangent}


def disco_forward(canvas_in, psi_rows):
    row_count = psi_rows.shape[0]
    col_count = canvas_in.shape[1] - 2
    shifted = [canvas_in[row_off:row_off + row_count, col_off:col_off + col_count].astype(jnp.float32) for row_off in range(3) for col_off in range(3)]
    pieces = []
    for basis_idx in range(psi_rows.shape[1] // 9):
        summed = jnp.zeros(shifted[0].shape, jnp.float32)
        for tap_idx in range(9):
            summed = summed + psi_rows[:, basis_idx * 9 + tap_idx][:, None, None] * shifted[tap_idx]
        pieces.append(summed)
    return jnp.concatenate(pieces, axis=-1).astype(jnp.bfloat16)


def disco_backward(grad_s, psi_rows):
    row_count, col_count, all_channels = grad_s.shape
    basis_count = psi_rows.shape[1] // 9
    channels = all_channels // basis_count
    pieces = [grad_s[:, :, basis_idx * channels:(basis_idx + 1) * channels].astype(jnp.float32) for basis_idx in range(basis_count)]
    canvas = jnp.zeros((row_count + 2, col_count + 2, channels), jnp.float32)
    for row_off in range(3):
        for col_off in range(3):
            tap_idx = row_off * 3 + col_off
            summed = jnp.zeros(pieces[0].shape, jnp.float32)
            for basis_idx in range(basis_count):
                summed = summed + psi_rows[:, basis_idx * 9 + tap_idx][:, None, None] * pieces[basis_idx]
            canvas = canvas + jnp.pad(summed, ((row_off, 2 - row_off), (col_off, 2 - col_off), (0, 0)))
    return canvas.astype(jnp.bfloat16)


def attend(queries, kv_frame, bias_rows, reach_rows, row_ok, upstream, key_start, key_span):
    row_count, col_count, channels = queries.shape
    head_dim = channels // HEADS
    scaling = head_dim ** -0.5
    key_part = kv_frame[:, key_start:key_start + key_span, :channels].astype(jnp.float32).reshape(row_count + 2, key_span, HEADS, head_dim)
    value_part = kv_frame[:, key_start:key_start + key_span, channels:].astype(jnp.float32).reshape(row_count + 2, key_span, HEADS, head_dim)

    def three_rows(source):
        return jnp.stack([source[row_off:row_off + row_count] for row_off in range(3)], axis=1)

    key_rows = three_rows(key_part)
    value_rows = three_rows(value_part)
    heads_q = queries.astype(jnp.float32).reshape(row_count, col_count, HEADS, head_dim)
    heads_up = upstream.astype(jnp.float32).reshape(row_count, col_count, HEADS, head_dim)
    bias_three = three_rows(bias_rows).transpose(0, 2, 1)[:, :, None, :, None]
    valid_three = three_rows(row_ok)[:, None, None, :, None]
    offsets = jnp.arange(key_span, dtype=jnp.int32)[None, :] + (key_start - col_count) - jnp.arange(col_count, dtype=jnp.int32)[:, None]
    in_reach = jnp.abs(offsets)[None] <= reach_rows[:, None, None]
    allowed = in_reach[:, None, :, None, :] & valid_three
    logits = jnp.einsum('rqhd,rakhd->rhqak', heads_q, key_rows) * scaling + bias_three
    logits = jnp.where(allowed, logits, -jnp.inf)
    attn_probs = jax.nn.softmax(logits.reshape(row_count, HEADS, col_count, 3 * key_span), axis=-1).reshape(logits.shape)
    probs_low = lax.optimization_barrier(attn_probs.astype(jnp.bfloat16)).astype(jnp.float32)
    attended = jnp.einsum('rhqak,rakhd->rqhd', probs_low, value_rows).astype(jnp.bfloat16).reshape(queries.shape)
    grad_prob = jnp.einsum('rqhd,rakhd->rhqak', heads_up, value_rows).astype(jnp.bfloat16)
    grad_prob = lax.optimization_barrier(grad_prob).astype(jnp.float32)
    grad_logit = attn_probs * (grad_prob - jnp.sum(attn_probs * grad_prob, axis=(-2, -1), keepdims=True))
    grad_logit = lax.optimization_barrier(grad_logit.astype(jnp.bfloat16)).astype(jnp.float32)
    grad_query = (jnp.einsum('rhqak,rakhd->rqhd', grad_logit, key_rows) * scaling).astype(jnp.bfloat16).reshape(queries.shape)
    grad_key = jnp.einsum('rhqak,rqhd->rakhd', grad_logit, heads_q) * scaling
    grad_value = jnp.einsum('rhqak,rqhd->rakhd', probs_low, heads_up)
    grad_both = jnp.concatenate([grad_key.reshape(row_count, 3, key_span, channels), grad_value.reshape(row_count, 3, key_span, channels)], axis=-1)
    canvas = jnp.zeros((row_count + 2, key_span, 2 * channels), jnp.float32)
    for row_off in range(3):
        canvas = canvas + jnp.pad(grad_both[:, row_off], ((row_off, 2 - row_off), (0, 0), (0, 0)))
    canvas = jnp.pad(canvas, ((0, 0), (key_start, 3 * col_count - key_start - key_span), (0, 0)))
    return attended, grad_query, canvas


def reference(tokens, w_qkv, w_out, w_disco, psi, reach, key_bias, cotangent):
    w_query = w_qkv[:, :C]
    w_keyval = w_qkv[:, C:]
    padded_x = jnp.pad(tokens, ((1, 1), (0, 0), (0, 0)))
    padded_bias = jnp.pad(key_bias, ((1, 1), (0, 0)))
    stencil_width = w_disco.shape[0]

    def frames(band_rows):
        blocks = band_rows.reshape(band_rows.shape[0], N_LON, LON_DEV, band_rows.shape[-1])
        joined = jnp.concatenate([jnp.roll(blocks, 1, axis=1), blocks, jnp.roll(blocks, -1, axis=1)], axis=2)
        return joined.transpose(1, 0, 2, 3)

    def split_blocks(band_rows):
        return band_rows.reshape(band_rows.shape[0], N_LON, LON_DEV, band_rows.shape[-1]).transpose(1, 0, 2, 3)

    def join_blocks(blocks):
        return blocks.transpose(1, 0, 2, 3).reshape(blocks.shape[1], NLON, blocks.shape[-1])

    def finish(pending, prev_dq, prev_x):
        kv_grad = pending[..., :2 * C]
        disco_grad = pending[..., 2 * C:]
        flat_kv = kv_grad.reshape(-1, 2 * C)
        grads_in = jnp.dot(prev_dq.reshape(-1, C), w_query.T, preferred_element_type=jnp.float32)
        grads_in = grads_in + jnp.dot(flat_kv, w_keyval.T.astype(jnp.float32), precision=lax.Precision.HIGHEST)
        grads_in = grads_in.reshape(pending.shape[0], NLON, C) + disco_grad
        kv_weight = jnp.dot(prev_x.reshape(-1, C).astype(jnp.float32).T, flat_kv, precision=lax.Precision.HIGHEST)
        return grads_in.astype(jnp.bfloat16), kv_weight

    def band_step(state_carry, band_idx):
        pending, rim_row, prev_dq, prev_x, query_w, keyval_w, out_w, disco_w = state_carry
        start_row = band_idx * LAT_DEV
        x_band = lax.dynamic_slice_in_dim(padded_x, start_row, LAT_DEV + 2, 0)
        cot_band = lax.dynamic_slice_in_dim(cotangent, start_row, LAT_DEV, 0)
        inner_x = x_band[1:LAT_DEV + 1]
        queries = jnp.dot(inner_x.reshape(-1, C), w_query, preferred_element_type=jnp.float32).astype(jnp.bfloat16).reshape(LAT_DEV, NLON, C)
        keyval = jnp.dot(x_band.reshape(-1, C), w_keyval, preferred_element_type=jnp.float32).astype(jnp.bfloat16).reshape(LAT_DEV + 2, NLON, 2 * C)
        upstream = jnp.dot(cot_band.reshape(-1, C), w_out.T, preferred_element_type=jnp.float32).astype(jnp.bfloat16).reshape(LAT_DEV, NLON, C)
        bias_rows = lax.dynamic_slice_in_dim(padded_bias, start_row, LAT_DEV + 2, 0)
        global_rows = start_row - 1 + jnp.arange(LAT_DEV + 2, dtype=jnp.int32)
        row_ok = (global_rows >= 0) & (global_rows < NLAT)
        reach_rows = lax.dynamic_slice_in_dim(reach, start_row, LAT_DEV, 0)
        psi_rows = lax.dynamic_slice_in_dim(psi, start_row, LAT_DEV, 0)

        def one_block(query_blk, kv_blk, x_blk, up_blk, cot_blk):
            attended, grad_query, kv_canvas = attend(query_blk, kv_blk, bias_rows, reach_rows, row_ok, up_blk, 0, 3 * LON_DEV)
            stencil = disco_forward(x_blk[:, LON_DEV - 1:2 * LON_DEV + 1], psi_rows)
            flat_cot = cot_blk.reshape(-1, C)
            flat_att = attended.reshape(-1, C)
            flat_sten = stencil.reshape(-1, stencil_width)
            mixed_blk = jnp.dot(flat_att, w_out, preferred_element_type=jnp.float32) + jnp.dot(flat_sten, w_disco, preferred_element_type=jnp.float32)
            grad_s = jnp.dot(flat_cot, w_disco.T, preferred_element_type=jnp.float32).astype(jnp.bfloat16).reshape(stencil.shape)
            disco_canvas = jnp.pad(disco_backward(grad_s, psi_rows), ((0, 0), (LON_DEV - 1, LON_DEV - 1), (0, 0)))
            partial_sum = jnp.concatenate([kv_canvas.astype(jnp.bfloat16), disco_canvas], axis=-1)
            out_term = jnp.dot(flat_att.T, flat_cot, preferred_element_type=jnp.float32)
            disco_term = jnp.dot(flat_sten.T, flat_cot, preferred_element_type=jnp.float32)
            return mixed_blk.astype(jnp.bfloat16).reshape(cot_blk.shape), grad_query, partial_sum, out_term, disco_term

        mixed_b, grad_query, partial_sum, out_term, disco_term = jax.vmap(one_block)(split_blocks(queries), frames(keyval), frames(x_band), split_blocks(upstream), split_blocks(cot_band))
        widened = partial_sum.astype(jnp.float32)
        lon_sum = widened[:, :, LON_DEV:2 * LON_DEV] + jnp.roll(widened[:, :, :LON_DEV], -1, axis=0) + jnp.roll(widened[:, :, 2 * LON_DEV:], 1, axis=0)
        band_sum = join_blocks(lon_sum)
        pending = pending.at[LAT_DEV - 1].add(band_sum[0])
        done_dx, kv_weight = finish(pending, prev_dq, prev_x)
        grad_q_band = join_blocks(grad_query)
        new_pending = band_sum[1:LAT_DEV + 1].at[0].add(rim_row)
        query_w = query_w + jnp.dot(inner_x.reshape(-1, C).T, grad_q_band.reshape(-1, C), preferred_element_type=jnp.float32)
        keyval_w = keyval_w + kv_weight
        out_w = out_w + jnp.sum(out_term, axis=0)
        disco_w = disco_w + jnp.sum(disco_term, axis=0)
        next_carry = (new_pending, band_sum[LAT_DEV + 1], grad_q_band, inner_x, query_w, keyval_w, out_w, disco_w)
        return next_carry, (join_blocks(mixed_b), done_dx)

    start_carry = (jnp.zeros((LAT_DEV, NLON, 3 * C), jnp.float32), jnp.zeros((NLON, 3 * C), jnp.float32), jnp.zeros((LAT_DEV, NLON, C), jnp.bfloat16), jnp.zeros((LAT_DEV, NLON, C), jnp.bfloat16), jnp.zeros((C, C), jnp.float32), jnp.zeros((C, 2 * C), jnp.float32), jnp.zeros((C, C), jnp.float32), jnp.zeros((stencil_width, C), jnp.float32))
    final_carry, outputs = lax.scan(band_step, start_carry, jnp.arange(N_LAT, dtype=jnp.int32))
    pending, rim_row, prev_dq, prev_x, query_w, keyval_w, out_w, disco_w = final_carry
    last_dx, last_kv = finish(pending, prev_dq, prev_x)
    keyval_w = keyval_w + last_kv
    mixed_out = outputs[0].reshape(NLAT, NLON, C)
    input_grad = jnp.concatenate([outputs[1][1:], last_dx[None]], axis=0).reshape(NLAT, NLON, C)
    weight_grads = jnp.concatenate([jnp.concatenate([query_w, keyval_w], axis=1).reshape(-1), out_w.reshape(-1), disco_w.reshape(-1)])
    return mixed_out, input_grad, weight_grads
```

```python
import jax
import jax.numpy as jnp
from jax import lax
from jax.experimental import pallas as pl
from jax.experimental.pallas import tpu as pltpu
from jax.sharding import PartitionSpec as P

HEADS = 8
HEAD_DIM = 48
C = 384
ROWS = 4
COLS = 32
SPAN = 3 * COLS
FRAME = (ROWS + 2) * SPAN
CELLS = ROWS * COLS
LATS = 32
LONS = 16
CHUNK = 144
SCALING = HEAD_DIM ** (-0.5)
FAR = -1e30
MESH = pl.DeviceIdType.MESH
BF16 = jnp.bfloat16
F32 = jnp.float32
VMEM = pltpu.VMEM
LIMIT = 56 * 1024 * 1024


def nn(left, right):
    return lax.dot_general(left, right, (((1,), (0,)), ((), ())), preferred_element_type=F32)


def nt(left, right):
    return lax.dot_general(left, right, (((1,), (1,)), ((), ())), preferred_element_type=F32)


def tn(left, right):
    return lax.dot_general(left, right, (((0,), (0,)), ((), ())), preferred_element_type=F32)


def place():
    return lax.axis_index("lat"), lax.axis_index("lon")


def neighbours(lat, lon):
    found = []
    for row_step in (-1, 0, 1):
        for col_step in (-1, 0, 1):
            if row_step or col_step:
                target = (
                    lax.rem(lat + row_step + LATS, LATS),
                    lax.rem(lon + col_step + LONS, LONS),
                )
                found.append((row_step, col_step, target))
    return found


def greet(targets, count):
    barrier = pltpu.get_barrier_semaphore()
    for target in targets:
        pl.semaphore_signal(barrier, inc=1, device_id=target, device_id_type=MESH)
    pl.semaphore_wait(barrier, count)


def halo_kernel(tokens_ref, frame_ref, send_sem, recv_sem):
    lat, lon = place()
    around = neighbours(lat, lon)
    greet([target for _, _, target in around], len(around))
    copies = []
    for idx, (row_step, col_step, target) in enumerate(around):
        if row_step == -1:
            src, dst_rows = tokens_ref.at[pl.ds(0, 1)], pl.ds(ROWS + 1, 1)
        elif row_step == 1:
            src, dst_rows = tokens_ref.at[pl.ds(ROWS - 1, 1)], pl.ds(0, 1)
        else:
            src, dst_rows = tokens_ref, pl.ds(1, ROWS)
        copy = pltpu.make_async_remote_copy(
            src_ref=src,
            dst_ref=frame_ref.at[dst_rows, pl.ds((1 - col_step) * COLS, COLS)],
            send_sem=send_sem.at[idx],
            recv_sem=recv_sem.at[idx],
            device_id=target,
            device_id_type=MESH,
        )
        copy.start()
        copies.append(copy)
    frame_ref[1 : ROWS + 1, COLS : 2 * COLS] = tokens_ref[...]
    for copy in copies:
        copy.wait()

    @pl.when(lat == 0)
    def _():
        frame_ref[0] = jnp.zeros((SPAN, C), BF16)

    @pl.when(lat == LATS - 1)
    def _():
        frame_ref[ROWS + 1] = jnp.zeros((SPAN, C), BF16)


def halo(tokens):
    return pl.pallas_call(
        halo_kernel,
        out_shape=jax.ShapeDtypeStruct((ROWS + 2, SPAN, C), BF16),
        in_specs=[pl.BlockSpec(memory_space=VMEM)],
        out_specs=pl.BlockSpec(memory_space=VMEM),
        scratch_shapes=[pltpu.SemaphoreType.DMA((8,)), pltpu.SemaphoreType.DMA((8,))],
        compiler_params=pltpu.CompilerParams(
            collective_id=0, has_side_effects=True, vmem_limit_bytes=LIMIT
        ),
    )(tokens)


def block_kernel(
    frame_ref,
    cot_ref,
    w_qkv_ref,
    w_out_ref,
    w_disco_ref,
    psi_ref,
    reach_ref,
    bias_ref,
    mixed_ref,
    own_ref,
    rim_ref,
    grads_ref,
    kv_ref,
    canvas_ref,
    shifted_ref,
    stencil_ref,
    att_ref,
    dq_ref,
    gs_ref,
):
    lat, _ = place()
    x_own = jnp.concatenate(
        [frame_ref[(r + 1) * SPAN + COLS : (r + 1) * SPAN + 2 * COLS] for r in range(ROWS)], axis=0
    )
    cot = cot_ref[...].reshape(CELLS, C)
    queries = nn(x_own, w_qkv_ref[:, :C]).astype(BF16)
    upstream = nt(cot, w_out_ref[...]).astype(BF16)
    gs_ref[...] = nt(cot, w_disco_ref[...]).astype(BF16).astype(F32)
    for r in range(ROWS + 2):
        rows = slice(r * SPAN, (r + 1) * SPAN)
        kv_ref[rows] = nn(frame_ref[rows], w_qkv_ref[:, C:]).astype(BF16)
    canvas_ref[...] = jnp.zeros_like(canvas_ref)

    for r in range(ROWS + 2):
        wide = frame_ref[r * SPAN + 16 : r * SPAN + 80].astype(F32)
        shifted_ref[0, r] = pltpu.roll(wide, 1, 0)[16:48]
        shifted_ref[1, r] = wide[16:48]
        shifted_ref[2, r] = pltpu.roll(wide, 63, 0)[16:48]
    for r in range(ROWS):
        for k in range(2):
            total = jnp.zeros((COLS, C), F32)
            for a in range(3):
                for b in range(3):
                    total = total + psi_ref[r, 9 * k + 3 * a + b] * shifted_ref[b, r + a]
            stencil_ref[r * COLS : (r + 1) * COLS, k * C : (k + 1) * C] = total.astype(BF16)

    stack = HEADS * COLS
    head_mask = (
        lax.broadcasted_iota(jnp.int32, (stack, C), 0) // COLS
        == lax.broadcasted_iota(jnp.int32, (stack, C), 1) // HEAD_DIM
    )
    head_mask = jnp.where(head_mask, 1.0, 0.0).astype(BF16)
    lane_head = lax.broadcasted_iota(jnp.int32, (COLS, C), 1) // HEAD_DIM
    distance = jnp.abs(
        lax.broadcasted_iota(jnp.int32, (SPAN, stack), 0)
        - COLS
        - lax.rem(lax.broadcasted_iota(jnp.int32, (SPAN, stack), 1), COLS)
    )
    stack_head = lax.broadcasted_iota(jnp.int32, (1, stack), 1) // COLS
    bias_rows = []
    for k in range(ROWS + 2):
        global_row = lat * ROWS - 1 + k
        clamped = jnp.clip(global_row, 0, LATS * ROWS - 1)
        line = jnp.zeros((1, stack), F32)
        for h in range(HEADS):
            line = jnp.where(stack_head == h, bias_ref[clamped, h], line)
        valid = (global_row >= 0) & (global_row < LATS * ROWS)
        bias_rows.append(jnp.where(valid, line, FAR))

    def fold_heads(wide):
        total = jnp.zeros((COLS, C), F32)
        for h in range(HEADS):
            total = jnp.where(lane_head == h, wide[h * COLS : (h + 1) * COLS], total)
        return total

    for r in range(ROWS):
        cells = slice(r * COLS, (r + 1) * COLS)
        keys_at = slice(r * SPAN, (r + 3) * SPAN)
        keys, values = kv_ref[keys_at, :C], kv_ref[keys_at, C:]
        q_heads = jnp.concatenate([queries[cells]] * HEADS, axis=0) * head_mask
        u_heads = jnp.concatenate([upstream[cells]] * HEADS, axis=0) * head_mask
        outside = jnp.where(distance <= reach_ref[r], 0.0, FAR)
        added = jnp.concatenate([outside + bias_rows[r + a] for a in range(3)], axis=0)
        logits = nt(keys, q_heads) * SCALING + added
        logits = logits - jnp.max(logits, axis=0, keepdims=True)
        probs = jnp.exp(logits)
        probs = probs * (1.0 / jnp.sum(probs, axis=0, keepdims=True))
        probs_low = probs.astype(BF16)
        grad_prob = nt(values, u_heads).astype(BF16).astype(F32)
        mean = jnp.sum(probs * grad_prob, axis=0, keepdims=True)
        grad_logit = (probs * (grad_prob - mean)).astype(BF16)
        att_ref[cells] = fold_heads(tn(probs_low, values)).astype(BF16)
        dq_ref[cells] = (fold_heads(tn(grad_logit, keys)) * SCALING).astype(BF16)
        canvas_ref[keys_at, :C] += nn(grad_logit, q_heads) * SCALING
        canvas_ref[keys_at, C:] += nn(probs_low, u_heads)

    attended = att_ref[...]
    grad_query = dq_ref[...]
    stencil = stencil_ref[...]
    mixed = nn(attended, w_out_ref[...]) + nn(stencil, w_disco_ref[...])
    mixed_ref[...] = mixed.astype(BF16).reshape(ROWS, COLS, C)
    grads_ref[1, :C] = tn(attended, cot).astype(BF16)
    grads_ref[1, C:] = tn(stencil, cot).astype(BF16)

    kv_part = canvas_ref[...].astype(BF16)
    query_weight = tn(x_own, grad_query).astype(BF16)
    kv_weight = tn(frame_ref[...], kv_part).astype(BF16)
    for c in range(8):
        lines = slice(48 * c, 48 * (c + 1))
        grads_ref[0, CHUNK * c : CHUNK * c + 48] = query_weight[lines]
        grads_ref[0, CHUNK * c + 48 : CHUNK * c + 96] = kv_weight[lines, :C]
        grads_ref[0, CHUNK * c + 96 : CHUNK * c + 144] = kv_weight[lines, C:]

    canvas_ref[:, :C] = nt(kv_part, w_qkv_ref[:, C:])
    query_part = nt(grad_query, w_qkv_ref[:, :C])
    margin = jnp.zeros((16, C), F32)
    for row in range(ROWS + 2):
        spread = jnp.zeros((64, C), F32)
        for b in range(3):
            total = jnp.zeros((COLS, C), F32)
            for a in range(3):
                r = row - a
                if 0 <= r < ROWS:
                    for k in range(2):
                        total = total + (
                            psi_ref[r, 9 * k + 3 * a + b]
                            * gs_ref[r * COLS : (r + 1) * COLS, k * C : (k + 1) * C]
                        )
            total = jnp.concatenate([margin, total, margin], axis=0)
            spread = spread + (total if b == 1 else pltpu.roll(total, 63 if b == 0 else 1, 0))
        canvas_ref[row * SPAN + 16 : row * SPAN + 80, :C] += spread
    for r in range(ROWS):
        at = (r + 1) * SPAN + COLS
        own_ref[r] = canvas_ref[at : at + COLS, :C] + query_part[r * COLS : (r + 1) * COLS]
    rim_ref[...] = canvas_ref[:, :C].astype(BF16).reshape(ROWS + 2, SPAN, C)


def block(frame, cotangent, w_qkv, w_out, w_disco, psi, reach, key_bias):
    vmem = pl.BlockSpec(memory_space=VMEM)
    smem = pl.BlockSpec(memory_space=pltpu.SMEM)
    return pl.pallas_call(
        block_kernel,
        out_shape=(
            jax.ShapeDtypeStruct((ROWS, COLS, C), BF16),
            jax.ShapeDtypeStruct((ROWS, COLS, C), F32),
            jax.ShapeDtypeStruct((ROWS + 2, SPAN, C), BF16),
            jax.ShapeDtypeStruct((2, 8 * CHUNK, C), BF16),
        ),
        in_specs=[vmem] * 5 + [smem] * 3,
        out_specs=(vmem,) * 4,
        scratch_shapes=[
            VMEM((FRAME, 2 * C), BF16),
            VMEM((FRAME, 2 * C), F32),
            VMEM((3, ROWS + 2, COLS, C), F32),
            VMEM((CELLS, 2 * C), BF16),
            VMEM((CELLS, C), BF16),
            VMEM((CELLS, C), BF16),
            VMEM((CELLS, 2 * C), F32),
        ],
        compiler_params=pltpu.CompilerParams(vmem_limit_bytes=LIMIT),
    )(frame, cotangent, w_qkv, w_out, w_disco, psi, reach, key_bias)


def sum_kernel(
    grads_ref,
    own_ref,
    rim_ref,
    input_ref,
    weight_ref,
    pair_in,
    x_out,
    x_in,
    total_ref,
    z_out,
    z_in,
    last_out,
    last_in,
    rim_in,
    line_in,
    order_ref,
    pair_send,
    pair_recv,
    x_send,
    x_recv,
    z_send,
    z_recv,
    last_send,
    last_recv,
    rim_send,
    rim_recv,
):
    lat, lon = place()
    y, z_high = lat // 4, lax.rem(lat, 4)
    x, z_low, core = lon // 4, lax.rem(lon, 4) // 2, lax.rem(lon, 2)
    z = z_high * 2 + z_low
    other = 1 - core
    pair_peer = (lat, lon + 1 - 2 * core)
    x_peers = []
    for d in range(1, 4):
        peer_x = lax.rem(x + d, 4)
        peer_back = lax.rem(x + 4 - d, 4)
        x_peers.append((peer_x, (lat, peer_x * 4 + lax.rem(lon, 4)), (lat, peer_back * 4 + lax.rem(lon, 4))))

    def at_z(where):
        return (y * 4 + where // 2, x * 4 + lax.rem(where, 2) * 2 + core)

    z_peers = []
    for d in range(1, 8):
        peer_z, back = lax.rem(z + d, 8), lax.rem(z + 8 - d, 8)
        z_peers.append((peer_z, at_z(peer_z), at_z(back)))
    around = neighbours(lat, lon)
    owners = []
    for job in range(2):
        for o in range(4):
            owners.append((job * 16 + 2 * (core * 4 + x) + z // 4, 4 * lax.rem(z, 4) + o))
    piece = lax.rem(lat, 16) * 16 + lon
    chunk = piece // 32
    from_x, from_core = lax.rem(chunk, 4), chunk // 4
    from_z = lax.rem(piece, 32) // 4
    sources = []
    for k in range(8):
        sources.append((k * 4 + from_z // 2, from_x * 4 + lax.rem(from_z, 2) * 2 + from_core))

    barrier = pltpu.get_barrier_semaphore()

    def hail(target):
        pl.semaphore_signal(barrier, inc=1, device_id=target, device_id_type=MESH)

    hail(pair_peer)
    for _, _, back in x_peers:
        hail(back)
    for _, _, back in z_peers:
        hail(back)
    for _, _, target in around:
        hail(target)
    expected = 1 + 3 + 7 + 8 + 8
    for source in sources:
        same = (source[0] == lat) & (source[1] == lon)

        @pl.when(jnp.logical_not(same))
        def _():
            hail(source)

    for owner in owners:
        same = (owner[0] == lat) & (owner[1] == lon)
        expected = expected - jnp.where(same, 1, 0)
    pl.semaphore_wait(barrier, expected)

    def remote(src, dst, send, recv, target):
        return pltpu.make_async_remote_copy(
            src_ref=src,
            dst_ref=dst,
            send_sem=send,
            recv_sem=recv,
            device_id=target,
            device_id_type=MESH,
        )

    jobs = (1, 0)
    pending = []
    pair_copies = {}
    for job in jobs:
        copy = remote(
            grads_ref.at[job, pl.ds(other * 4, 4)],
            pair_in.at[job],
            pair_send.at[job],
            pair_recv.at[job],
            pair_peer,
        )
        copy.start()
        pair_copies[job] = copy
    rim_copies = []
    for idx, (row_step, col_step, target) in enumerate(around):
        if row_step == 0:
            src = rim_ref.at[pl.ds(1, ROWS), pl.ds((1 + col_step) * COLS, COLS)]
            dst = rim_in.at[0 if col_step == -1 else 1]
        else:
            row = 0 if row_step == -1 else ROWS + 1
            src = rim_ref.at[row, pl.ds((1 + col_step) * COLS, COLS)]
            dst = line_in.at[(0 if row_step == -1 else 3) + col_step + 1]
        copy = remote(src, dst, rim_send.at[idx], rim_recv.at[idx], target)
        copy.start()
        rim_copies.append(copy)

    x_copies = {}
    for job in jobs:
        pair_copies[job].wait()
        x_copies[job] = []
        for d, (peer_x, target, _) in enumerate(x_peers):
            added = grads_ref[job, core * 4 + peer_x].astype(F32) + pair_in[job, peer_x].astype(F32)
            x_out[job, d] = added.astype(BF16)
            copy = remote(
                x_out.at[job, d], x_in.at[job, d], x_send.at[job, d], x_recv.at[job, d], target
            )
            copy.start()
            x_copies[job].append(copy)

    row_ids = lax.broadcasted_iota(jnp.int32, (16, C), 0)
    z_copies = {}
    for job in jobs:
        total = grads_ref[job, core * 4 + x].astype(F32) + pair_in[job, x].astype(F32)
        for d in range(3):
            x_copies[job][d].wait()
            total = total + x_in[job, d].astype(F32)
        total_ref[job, 0:8] = jnp.zeros((8, C), F32)
        total_ref[job, 8 : 8 + CHUNK] = total
        total_ref[job, 8 + CHUNK : 32 + CHUNK] = jnp.zeros((24, C), F32)
        for k in range(8):
            for half in range(2):
                if job == 1:
                    first = 8 + 18 * k + 9 * half
                    lines = total_ref[job, first : first + 16]
                else:
                    first = 8 + 6 * k + 3 * half
                    parts = [
                        total_ref[job, first + 48 * m - 3 * m : first + 48 * m - 3 * m + 16]
                        for m in range(3)
                    ]
                    lines = jnp.where(row_ids < 3, parts[0], jnp.where(row_ids < 6, parts[1], parts[2]))
                z_out[job, k, half * 16 : half * 16 + 16] = lines.astype(BF16)
        z_copies[job] = []
        for d, (peer_z, target, _) in enumerate(z_peers):
            copy = remote(
                z_out.at[job, peer_z], z_in.at[job, d], z_send.at[job, d], z_recv.at[job, d], target
            )
            copy.start()
            z_copies[job].append(copy)

    for idx, copy in enumerate(rim_copies):
        copy.wait()
    above = jnp.where(lat > 0, 1.0, 0.0)
    below = jnp.where(lat < LATS - 1, 1.0, 0.0)
    for r in range(ROWS):
        summed = own_ref[r] + rim_in[0, r].astype(F32) + rim_in[1, r].astype(F32)
        for side in range(3):
            if r == 0:
                summed = summed + above * line_in[3 + side].astype(F32)
            if r == ROWS - 1:
                summed = summed + below * line_in[side].astype(F32)
        input_ref[r] = summed.astype(BF16)

    for job in jobs:
        total = z_out[job, z].astype(F32)
        for d in range(7):
            z_copies[job][d].wait()
            total = total + z_in[job, d].astype(F32)
        last_out[job] = total.astype(BF16)
        for o in range(4):
            owner = owners[job * 4 + o]
            same = (owner[0] == lat) & (owner[1] == lon)
            src = last_out.at[job, pl.ds((o // 2) * 16, 16)]

            @pl.when(jnp.logical_not(same))
            def _():
                remote(src, last_in.at[y], last_send.at[job, o], last_recv.at[y], owner).start()

            @pl.when(same)
            def _():
                last_in[y] = src[...]

    final = jnp.zeros((16, C), F32)
    for k in range(8):
        same = (sources[k][0] == lat) & (sources[k][1] == lon)

        @pl.when(jnp.logical_not(same))
        def _():
            remote(
                last_out.at[0, pl.ds(0, 16)],
                last_in.at[k],
                last_send.at[0, 0],
                last_recv.at[k],
                sources[k],
            ).wait_recv()

        final = final + last_in[k].astype(F32)
    for job in jobs:
        for o in range(4):
            owner = owners[job * 4 + o]
            same = (owner[0] == lat) & (owner[1] == lon)

            @pl.when(jnp.logical_not(same))
            def _():
                remote(
                    last_out.at[job, pl.ds((o // 2) * 16, 16)],
                    last_in.at[y],
                    last_send.at[job, o],
                    last_recv.at[y],
                    owner,
                ).wait_send()

    order_ref[0:16] = jnp.zeros((16, C), F32)
    order_ref[16:32] = final
    order_ref[32:48] = jnp.zeros((16, C), F32)
    mixed = final
    for i in range(3):
        for m in range(3):
            target, origin = 3 * i + m, 3 * m + i
            first = 16 + origin - target
            mixed = jnp.where(row_ids == target, order_ref[first : first + 16], mixed)
    weight_ref[...] = jnp.where(lat < 16, mixed, final)


def sums(grads, own, rim):
    vmem = pl.BlockSpec(memory_space=VMEM)
    dma = pltpu.SemaphoreType.DMA
    return pl.pallas_call(
        sum_kernel,
        out_shape=(
            jax.ShapeDtypeStruct((ROWS, COLS, C), BF16),
            jax.ShapeDtypeStruct((16, C), F32),
        ),
        in_specs=[vmem] * 3,
        out_specs=(vmem,) * 2,
        scratch_shapes=[
            VMEM((2, 4, CHUNK, C), BF16),
            VMEM((2, 3, CHUNK, C), BF16),
            VMEM((2, 3, CHUNK, C), BF16),
            VMEM((2, CHUNK + 32, C), F32),
            VMEM((2, 8, 32, C), BF16),
            VMEM((2, 7, 32, C), BF16),
            VMEM((2, 32, C), BF16),
            VMEM((8, 16, C), BF16),
            VMEM((2, ROWS, COLS, C), BF16),
            VMEM((6, COLS, C), BF16),
            VMEM((48, C), F32),
            dma((2,)),
            dma((2,)),
            dma((2, 3)),
            dma((2, 3)),
            dma((2, 7)),
            dma((2, 7)),
            dma((2, 4)),
            dma((8,)),
            dma((8,)),
            dma((8,)),
        ],
        compiler_params=pltpu.CompilerParams(
            collective_id=1, has_side_effects=True, vmem_limit_bytes=LIMIT
        ),
    )(grads.reshape(2, 8, CHUNK, C), own, rim)


def on_device(tokens, w_qkv, w_out, w_disco, psi, reach, key_bias, cotangent):
    frame = halo(tokens)
    mixed_out, own, rim, grads = block(
        frame.reshape(FRAME, C), cotangent, w_qkv, w_out, w_disco, psi, reach, key_bias
    )
    input_grad, lines = sums(grads, own, rim)
    size = 9 * C // 2
    first = lax.rem(lax.axis_index("lon"), 2) * size
    weight_grads = lax.dynamic_slice_in_dim(lines[:9].reshape(-1), first, size, 0)
    return (mixed_out, input_grad, weight_grads)


def solution(mesh):
    placed = (
        P("lat", "lon", None),
        P(),
        P(),
        P(),
        P("lat", None),
        P("lat"),
        P(),
        P("lat", "lon", None),
    )
    return jax.shard_map(
        on_device,
        mesh=mesh,
        in_specs=placed,
        out_specs=(P("lat", "lon", None), P("lat", "lon", None), P(("lat", "lon"))),
        check_vma=False,
    )
```

```python
import jax
import jax.numpy as jnp
from jax import lax
from jax.experimental import pallas as pl
from jax.experimental.pallas import tpu as pltpu
from jax.sharding import PartitionSpec as P

HEADS = 8
HEAD_DIM = 48
C = 384
ROWS = 4
COLS = 32
SPAN = 3 * COLS
FRAME = (ROWS + 2) * SPAN
CELLS = ROWS * COLS
LATS = 32
LONS = 16
CHUNK = 144
SCALING = HEAD_DIM ** (-0.5)
FAR = -1e30
MESH = pl.DeviceIdType.MESH
BF16 = jnp.bfloat16
F32 = jnp.float32
VMEM = pltpu.VMEM
LIMIT = 56 * 1024 * 1024


def nn(left, right):
    return lax.dot_general(left, right, (((1,), (0,)), ((), ())), preferred_element_type=F32)


def nt(left, right):
    return lax.dot_general(left, right, (((1,), (1,)), ((), ())), preferred_element_type=F32)


def tn(left, right):
    return lax.dot_general(left, right, (((0,), (0,)), ((), ())), preferred_element_type=F32)


def place():
    return lax.axis_index("lat"), lax.axis_index("lon")


def neighbours(lat, lon):
    found = []
    for row_step in (-1, 0, 1):
        for col_step in (-1, 0, 1):
            if row_step or col_step:
                target = (
                    lax.rem(lat + row_step + LATS, LATS),
                    lax.rem(lon + col_step + LONS, LONS),
                )
                found.append((row_step, col_step, target))
    return found


def to_chip(y, z, x, core):
    return (y * 4 + z // 2, x * 4 + lax.rem(z, 2) * 2 + core)


def remote(src, dst, send, recv, target):
    return pltpu.make_async_remote_copy(
        src_ref=src,
        dst_ref=dst,
        send_sem=send,
        recv_sem=recv,
        device_id=target,
        device_id_type=MESH,
    )


def whole_kernel(
    tokens_hbm,
    cot_hbm,
    w_qkv_hbm,
    w_out_hbm,
    w_disco_hbm,
    psi_ref,
    reach_ref,
    bias_ref,
    mixed_ref,
    input_ref,
    last_in,
    frame,
    cot_ref,
    w_qkv,
    w_out,
    w_disco,
    perm_x,
    perm_a,
    perm_b,
    kv_ref,
    canvas,
    probs_ref,
    shifted,
    mix_in,
    dq_ref,
    gs_ref,
    grads,
    own_ref,
    rim_ref,
    pair_in,
    x_out,
    x_in,
    total_ref,
    z_out,
    z_in,
    last_out,
    rim_in,
    line_in,
    load_sem,
    halo_send,
    halo_recv,
    pair_send,
    pair_recv,
    x_send,
    x_recv,
    z_send,
    z_recv,
    last_send,
    last_recv,
    rim_send,
    rim_recv,
):
    lat, lon = place()
    y, x, core = lat // 4, lon // 4, lax.rem(lon, 2)
    z = lax.rem(lat, 4) * 2 + lax.rem(lon, 4) // 2
    other = 1 - core

    loads = [
        pltpu.make_async_copy(tokens_hbm, frame.at[pl.ds(1, ROWS), pl.ds(COLS, COLS)], load_sem.at[0]),
        pltpu.make_async_copy(w_qkv_hbm, w_qkv, load_sem.at[1]),
        pltpu.make_async_copy(cot_hbm, cot_ref, load_sem.at[2]),
        pltpu.make_async_copy(w_out_hbm, w_out, load_sem.at[3]),
        pltpu.make_async_copy(w_disco_hbm, w_disco, load_sem.at[4]),
    ]
    for load in loads:
        load.start()

    around = neighbours(lat, lon)
    pair_peer = (lat, lon + 1 - 2 * core)
    x_peers = []
    for d in range(1, 4):
        there, back = lax.rem(x + d, 4), lax.rem(x + 4 - d, 4)
        x_peers.append((there, to_chip(y, z, there, core), to_chip(y, z, back, core)))
    z_peers = []
    for d in range(1, 8):
        there, back = lax.rem(z + d, 8), lax.rem(z + 8 - d, 8)
        z_peers.append((there, to_chip(y, there, x, core), to_chip(y, back, x, core)))
    owners = {}
    for job in range(2):
        for half in range(2):
            for to_core in range(2):
                row = (4 * job + half) + 2 * core
                mine = (row == y) & (core == to_core)
                owners[job, half, to_core] = (to_chip(row, z, x, to_core), mine)
    from_core = lax.rem(y, 4) // 2
    sources = []
    for k in range(8):
        mine = (y == k) & (core == from_core)
        sources.append((to_chip(k, z, x, from_core), mine))

    barrier = pltpu.get_barrier_semaphore()

    def hail(target):
        pl.semaphore_signal(barrier, inc=1, device_id=target, device_id_type=MESH)

    for _, _, target in around:
        hail(target)
    hail(pair_peer)
    for _, _, back in x_peers + z_peers:
        hail(back)
    for target, mine in sources:

        @pl.when(jnp.logical_not(mine))
        def _():
            hail(target)

    expected = 8 + 1 + 3 + 7 + 8 - jnp.where(core == from_core, 1, 0)
    pl.semaphore_wait(barrier, expected)

    halo_copies = []
    for idx, (row_step, col_step, target) in enumerate(around):
        if row_step == -1:
            src, dst_rows = tokens_hbm.at[pl.ds(0, 1)], pl.ds(ROWS + 1, 1)
        elif row_step == 1:
            src, dst_rows = tokens_hbm.at[pl.ds(ROWS - 1, 1)], pl.ds(0, 1)
        else:
            src, dst_rows = tokens_hbm, pl.ds(1, ROWS)
        copy = remote(
            src,
            frame.at[dst_rows, pl.ds((1 - col_step) * COLS, COLS)],
            halo_send.at[idx],
            halo_recv.at[idx],
            target,
        )
        copy.start()
        halo_copies.append(copy)

    def ones_where(equal):
        return jnp.where(equal, 1.0, 0.0).astype(BF16)

    pos = lax.broadcasted_iota(jnp.int32, (C, 128), 0)
    lane = lax.broadcasted_iota(jnp.int32, (C, 128), 1)
    pos_z = lax.rem(pos // 6, 8)
    pos_y = (pos // 192) * 2 + lax.rem(pos // 3, 2)
    origin = 3 * (
        pos_y * 32 + (pos_z // 2) * 8 + lax.rem(pos // 48, 4) * 2 + lax.rem(pos_z, 2)
    ) + lax.rem(pos, 3)
    for t in range(3):
        perm_x[:, 128 * t : 128 * (t + 1)] = ones_where(lane + 128 * t == origin)
    pos = lax.broadcasted_iota(jnp.int32, (4 * CHUNK, 128), 0)
    lane = lax.broadcasted_iota(jnp.int32, (4 * CHUNK, 128), 1)
    pos_z = lax.rem(pos // 18, 8)
    origin = (
        288 * lax.rem(pos // 9, 2)
        + 72 * (pos_z // 2)
        + 18 * (pos // 144)
        + 9 * lax.rem(pos_z, 2)
        + lax.rem(pos, 9)
    )
    for t in range(5):
        perm_a[:, 128 * t : 128 * (t + 1)] = ones_where(lane + 128 * t == origin)
        perm_b[:, 128 * t : 128 * (t + 1)] = ones_where(lane + 128 * t - 64 == origin)

    stack = HEADS * COLS
    head_mask = ones_where(
        lax.broadcasted_iota(jnp.int32, (stack, C), 0) // COLS
        == lax.broadcasted_iota(jnp.int32, (stack, C), 1) // HEAD_DIM
    )
    lane_head = lax.broadcasted_iota(jnp.int32, (COLS, C), 1) // HEAD_DIM
    distance = jnp.abs(
        lax.broadcasted_iota(jnp.int32, (SPAN, stack), 0)
        - COLS
        - lax.rem(lax.broadcasted_iota(jnp.int32, (SPAN, stack), 1), COLS)
    )
    stack_head = lax.broadcasted_iota(jnp.int32, (1, stack), 1) // COLS
    bias_lane = lax.broadcasted_iota(jnp.int32, (HEADS, LATS * ROWS), 1)
    bias_rows = []
    for k in range(ROWS + 2):
        global_row = lat * ROWS - 1 + k
        clamped = jnp.clip(global_row, 0, LATS * ROWS - 1)
        biases = jnp.sum(
            jnp.where(bias_lane == clamped, bias_ref[...], 0.0), axis=1, keepdims=True
        )
        line = jnp.zeros((1, stack), F32)
        for h in range(HEADS):
            line = jnp.where(stack_head == h, biases[h : h + 1], line)
        valid = (global_row >= 0) & (global_row < LATS * ROWS)
        bias_rows.append(jnp.where(valid, line, FAR))

    for load in loads:
        load.wait()
    x_own = frame[1 : ROWS + 1, COLS : 2 * COLS].reshape(CELLS, C)
    cot = cot_ref[...].reshape(CELLS, C)
    queries = nn(x_own, w_qkv[:, :C]).astype(BF16)
    upstream = nt(cot, w_out[...]).astype(BF16)
    gs_ref[...] = nt(cot, w_disco[...]).astype(BF16).astype(F32)
    own_turned = nt(perm_x[...], x_own).astype(BF16)
    canvas[...] = jnp.zeros_like(canvas)

    for copy in halo_copies:
        copy.wait()

    @pl.when(lat == 0)
    def _():
        frame[0] = jnp.zeros((SPAN, C), BF16)

    @pl.when(lat == LATS - 1)
    def _():
        frame[ROWS + 1] = jnp.zeros((SPAN, C), BF16)

    for r in range(ROWS + 2):
        kv_ref[r * SPAN : (r + 1) * SPAN] = nn(frame[r], w_qkv[:, C:]).astype(BF16)

    for r in range(ROWS + 2):
        wide = frame[r, 16:80].astype(F32)
        shifted[0, r] = pltpu.roll(wide, 1, 0)[16:48]
        shifted[1, r] = wide[16:48]
        shifted[2, r] = pltpu.roll(wide, 63, 0)[16:48]
    for r in range(ROWS):
        for k in range(2):
            total = jnp.zeros((COLS, C), F32)
            for a in range(3):
                for b in range(3):
                    total = total + psi_ref[r, 9 * k + 3 * a + b] * shifted[b, r + a]
            mix_in[r * COLS : (r + 1) * COLS, (k + 1) * C : (k + 2) * C] = total.astype(BF16)

    def fold_heads(wide):
        total = jnp.zeros((COLS, C), F32)
        for h in range(HEADS):
            total = jnp.where(lane_head == h, wide[h * COLS : (h + 1) * COLS], total)
        return total

    def all_heads(source, r):
        return jnp.concatenate([source[r * COLS : (r + 1) * COLS]] * HEADS, axis=0) * head_mask

    for r in range(ROWS):
        keys_at = slice(r * SPAN, (r + 3) * SPAN)
        keys, values = kv_ref[keys_at, :C], kv_ref[keys_at, C:]
        outside = jnp.where(distance <= reach_ref[r], 0.0, FAR)
        added = jnp.concatenate([outside + bias_rows[r + a] for a in range(3)], axis=0)
        logits = nt(keys, all_heads(queries, r)) * SCALING + added
        logits = logits - jnp.max(logits, axis=0, keepdims=True)
        probs = jnp.exp(logits)
        probs = probs * (1.0 / jnp.sum(probs, axis=0, keepdims=True))
        probs_ref[r] = probs
        attended = fold_heads(tn(probs.astype(BF16), values))
        mix_in[r * COLS : (r + 1) * COLS, :C] = attended.astype(BF16)

    turned = nt(perm_a[...], mix_in[:, :640]).astype(BF16)
    grads[1, 0:4] = nn(turned, cot).astype(BF16).reshape(4, CHUNK, C)
    turned = nt(perm_b[...], mix_in[:, 512:]).astype(BF16)
    grads[1, 4:8] = nn(turned, cot).astype(BF16).reshape(4, CHUNK, C)

    def pair_copy(job):
        return remote(
            grads.at[job, pl.ds(other * 4, 4)],
            pair_in.at[job],
            pair_send.at[job],
            pair_recv.at[job],
            pair_peer,
        )

    def x_copy(job, d):
        return remote(
            x_out.at[job, d], x_in.at[job, d], x_send.at[job, d], x_recv.at[job, d], x_peers[d][1]
        )

    def z_copies(job):
        return [
            remote(
                z_out.at[job, there],
                z_in.at[job, d],
                z_send.at[job, d],
                z_recv.at[job, d],
                target,
            )
            for d, (there, target, _) in enumerate(z_peers)
        ]

    def last_copy(job, half, to_core):
        return remote(
            last_out.at[job, pl.ds(half * 16, 16)],
            last_in.at[y],
            last_send.at[job, 2 * half + to_core],
            last_recv.at[y],
            owners[job, half, to_core][0],
        )

    def send_x(job):
        pair_copy(job).wait()
        for d, (there, _, _) in enumerate(x_peers):
            added = grads[job, core * 4 + there].astype(F32) + pair_in[job, there].astype(F32)
            x_out[job, d] = added.astype(BF16)
            x_copy(job, d).start()

    row_ids = lax.broadcasted_iota(jnp.int32, (16, C), 0)

    def send_z(job):
        total = grads[job, core * 4 + x].astype(F32) + pair_in[job, x].astype(F32)
        for d in range(3):
            x_copy(job, d).wait()
            total = total + x_in[job, d].astype(F32)
        total_ref[job, 0:8] = jnp.zeros((8, C), F32)
        total_ref[job, 8 : 8 + CHUNK] = total
        total_ref[job, 8 + CHUNK : 32 + CHUNK] = jnp.zeros((24, C), F32)
        for k in range(8):
            for half in range(2):
                if job == 1:
                    first = 8 + 18 * k + 9 * half
                    lines = total_ref[job, first : first + 16]
                else:
                    first = 8 + 6 * k + 3 * half
                    parts = [total_ref[job, first + 45 * m : first + 45 * m + 16] for m in range(3)]
                    lines = jnp.where(row_ids < 3, parts[0], jnp.where(row_ids < 6, parts[1], parts[2]))
                z_out[job, k, half * 16 : half * 16 + 16] = lines.astype(BF16)
        for copy in z_copies(job):
            copy.start()

    def send_last(job):
        total = z_out[job, z].astype(F32)
        for d, copy in enumerate(z_copies(job)):
            copy.wait()
            total = total + z_in[job, d].astype(F32)
        last_out[job] = total.astype(BF16)
        for half in range(2):
            for to_core in range(2):
                mine = owners[job, half, to_core][1]

                @pl.when(jnp.logical_not(mine))
                def _():
                    last_copy(job, half, to_core).start()

                @pl.when(mine)
                def _():
                    last_in[y] = last_out[job, half * 16 : half * 16 + 16]

    pair_copy(1).start()

    def backward(r):
        keys_at = slice(r * SPAN, (r + 3) * SPAN)
        keys, values = kv_ref[keys_at, :C], kv_ref[keys_at, C:]
        q_heads, u_heads = all_heads(queries, r), all_heads(upstream, r)
        probs = probs_ref[r]
        grad_prob = nt(values, u_heads).astype(BF16).astype(F32)
        mean = jnp.sum(probs * grad_prob, axis=0, keepdims=True)
        grad_logit = (probs * (grad_prob - mean)).astype(BF16)
        cells = slice(r * COLS, (r + 1) * COLS)
        dq_ref[cells] = (fold_heads(tn(grad_logit, keys)) * SCALING).astype(BF16)
        canvas[keys_at, :C] += nn(grad_logit, q_heads) * SCALING
        canvas[keys_at, C:] += nn(probs.astype(BF16), u_heads)

    backward(0)
    backward(1)
    send_x(1)
    backward(2)
    backward(3)

    grad_query = dq_ref[...]
    kv_part = canvas[...].astype(BF16)
    query_weight = nn(own_turned, grad_query).astype(BF16)
    frame_turned = nt(perm_x[...], frame[...].reshape(FRAME, C)).astype(BF16)
    kv_weight = nn(frame_turned, kv_part).astype(BF16)
    for c in range(8):
        lines = slice(48 * c, 48 * (c + 1))
        grads[0, c, 0:48] = query_weight[lines]
        grads[0, c, 48:96] = kv_weight[lines, :C]
        grads[0, c, 96:144] = kv_weight[lines, C:]
    pair_copy(0).start()

    canvas[:, :C] = nt(kv_part, w_qkv[:, C:])
    send_x(0)
    query_part = nt(grad_query, w_qkv[:, :C])
    margin = jnp.zeros((16, C), F32)
    for row in range(ROWS + 2):
        spread = jnp.zeros((64, C), F32)
        for b in range(3):
            total = jnp.zeros((COLS, C), F32)
            for a in range(3):
                r = row - a
                if 0 <= r < ROWS:
                    for k in range(2):
                        total = total + (
                            psi_ref[r, 9 * k + 3 * a + b]
                            * gs_ref[r * COLS : (r + 1) * COLS, k * C : (k + 1) * C]
                        )
            total = jnp.concatenate([margin, total, margin], axis=0)
            spread = spread + (total if b == 1 else pltpu.roll(total, 63 if b == 0 else 1, 0))
        canvas[row * SPAN + 16 : row * SPAN + 80, :C] += spread
    rim_ref[...] = canvas[:, :C].astype(BF16).reshape(ROWS + 2, SPAN, C)
    rim_copies = []
    for idx, (row_step, col_step, target) in enumerate(around):
        if row_step == 0:
            src = rim_ref.at[pl.ds(1, ROWS), pl.ds((1 + col_step) * COLS, COLS)]
            dst = rim_in.at[0 if col_step == -1 else 1]
        else:
            row = 0 if row_step == -1 else ROWS + 1
            src = rim_ref.at[row, pl.ds((1 + col_step) * COLS, COLS)]
            dst = line_in.at[(0 if row_step == -1 else 3) + col_step + 1]
        copy = remote(src, dst, rim_send.at[idx], rim_recv.at[idx], target)
        copy.start()
        rim_copies.append(copy)
    for r in range(ROWS):
        at = (r + 1) * SPAN + COLS
        own_ref[r] = canvas[at : at + COLS, :C] + query_part[r * COLS : (r + 1) * COLS]

    send_z(1)
    mixed = nn(mix_in[:, :C], w_out[...]) + nn(mix_in[:, C:], w_disco[...])
    mixed_ref[...] = mixed.astype(BF16).reshape(ROWS, COLS, C)
    send_z(0)
    send_last(1)

    for copy in rim_copies:
        copy.wait()
    above = jnp.where(lat > 0, 1.0, 0.0)
    below = jnp.where(lat < LATS - 1, 1.0, 0.0)
    for r in range(ROWS):
        summed = own_ref[r] + rim_in[0, r].astype(F32) + rim_in[1, r].astype(F32)
        for side in range(3):
            if r == 0:
                summed = summed + above * line_in[3 + side].astype(F32)
            if r == ROWS - 1:
                summed = summed + below * line_in[side].astype(F32)
        input_ref[r] = summed.astype(BF16)

    send_last(0)
    for k, (source, mine) in enumerate(sources):

        @pl.when(jnp.logical_not(mine))
        def _():
            remote(
                last_out.at[0, pl.ds(0, 16)],
                last_in.at[k],
                last_send.at[0, 0],
                last_recv.at[k],
                source,
            ).wait_recv()

    for (job, half, to_core), (_, mine) in owners.items():

        @pl.when(jnp.logical_not(mine))
        def _():
            last_copy(job, half, to_core).wait_send()


def whole(tokens, cotangent, w_qkv, w_out, w_disco, psi, reach, key_bias):
    vmem = pl.BlockSpec(memory_space=VMEM)
    smem = pl.BlockSpec(memory_space=pltpu.SMEM)
    anywhere = pl.BlockSpec(memory_space=pl.ANY)
    dma = pltpu.SemaphoreType.DMA
    return pl.pallas_call(
        whole_kernel,
        out_shape=(
            jax.ShapeDtypeStruct((ROWS, COLS, C), BF16),
            jax.ShapeDtypeStruct((ROWS, COLS, C), BF16),
            jax.ShapeDtypeStruct((8, 16, C), BF16),
        ),
        in_specs=[anywhere] * 5 + [smem] * 2 + [vmem],
        out_specs=(vmem,) * 3,
        scratch_shapes=[
            VMEM((ROWS + 2, SPAN, C), BF16),
            VMEM((ROWS, COLS, C), BF16),
            VMEM((C, 3 * C), BF16),
            VMEM((C, C), BF16),
            VMEM((2 * C, C), BF16),
            VMEM((C, C), BF16),
            VMEM((4 * CHUNK, 640), BF16),
            VMEM((4 * CHUNK, 640), BF16),
            VMEM((FRAME, 2 * C), BF16),
            VMEM((FRAME, 2 * C), F32),
            VMEM((ROWS, 3 * SPAN, HEADS * COLS), F32),
            VMEM((3, ROWS + 2, COLS, C), F32),
            VMEM((CELLS, 3 * C), BF16),
            VMEM((CELLS, C), BF16),
            VMEM((CELLS, 2 * C), F32),
            VMEM((2, 8, CHUNK, C), BF16),
            VMEM((ROWS, COLS, C), F32),
            VMEM((ROWS + 2, SPAN, C), BF16),
            VMEM((2, 4, CHUNK, C), BF16),
            VMEM((2, 3, CHUNK, C), BF16),
            VMEM((2, 3, CHUNK, C), BF16),
            VMEM((2, CHUNK + 32, C), F32),
            VMEM((2, 8, 32, C), BF16),
            VMEM((2, 7, 32, C), BF16),
            VMEM((2, 32, C), BF16),
            VMEM((2, ROWS, COLS, C), BF16),
            VMEM((6, COLS, C), BF16),
            dma((5,)),
            dma((8,)),
            dma((8,)),
            dma((2,)),
            dma((2,)),
            dma((2, 3)),
            dma((2, 3)),
            dma((2, 7)),
            dma((2, 7)),
            dma((2, 4)),
            dma((8,)),
            dma((8,)),
            dma((8,)),
        ],
        compiler_params=pltpu.CompilerParams(
            collective_id=0, has_side_effects=True, vmem_limit_bytes=LIMIT
        ),
    )(tokens, cotangent, w_qkv, w_out, w_disco, psi, reach, key_bias.T)


def finish_kernel(mixed_in, input_in, lines_ref, mixed_out, input_out, weight_ref):
    mixed_out[...] = mixed_in[...]
    input_out[...] = input_in[...]
    lat, lon = place()
    total = lines_ref[0].astype(F32)
    for k in range(1, 8):
        total = total + lines_ref[k].astype(F32)
    strips = []
    for row in range(9):
        origin = 3 * (row % 3) + row // 3
        line = jnp.where(lat < 16, total[origin : origin + 1], total[row : row + 1])
        strips += [line[:, 128 * t : 128 * (t + 1)] for t in range(3)]
    turned = [pltpu.roll(strip, 64, 1) for strip in strips[13:]]
    left = lax.broadcasted_iota(jnp.int32, (1, 128), 1) < 64
    first_core = lax.rem(lon, 2) == 0
    for j in range(14):
        later = turned[j] if j == 13 else jnp.where(left, turned[j], turned[j + 1])
        strip = jnp.where(first_core, strips[j], later).reshape(128)
        if j < 13:
            weight_ref[128 * j : 128 * (j + 1)] = strip
        else:
            weight_ref[128 * j : 128 * j + 64] = strip[:64]


def finish(mixed, input_grad, lines):
    vmem = pl.BlockSpec(memory_space=VMEM)
    return pl.pallas_call(
        finish_kernel,
        out_shape=(
            jax.ShapeDtypeStruct((ROWS, COLS, C), BF16),
            jax.ShapeDtypeStruct((ROWS, COLS, C), BF16),
            jax.ShapeDtypeStruct((9 * C // 2,), F32),
        ),
        in_specs=[vmem] * 3,
        out_specs=(vmem,) * 3,
    )(mixed, input_grad, lines)


def on_device(tokens, w_qkv, w_out, w_disco, psi, reach, key_bias, cotangent):
    mixed, input_grad, lines = whole(
        tokens, cotangent, w_qkv, w_out, w_disco, psi, reach, key_bias
    )
    return finish(mixed, input_grad, lines)


def solution(mesh):
    placed = (
        P("lat", "lon", None),
        P(),
        P(),
        P(),
        P("lat", None),
        P("lat"),
        P(),
        P("lat", "lon", None),
    )
    return jax.shard_map(
        on_device,
        mesh=mesh,
        in_specs=placed,
        out_specs=(P("lat", "lon", None), P("lat", "lon", None), P(("lat", "lon"))),
        check_vma=False,
    )
```

```python
import jax
import jax.numpy as jnp
from jax import lax
from jax.experimental import pallas as pl
from jax.experimental.pallas import tpu as pltpu
from jax.sharding import PartitionSpec as P

HEADS = 8
HEAD_DIM = 48
C = 384
ROWS = 4
COLS = 32
SPAN = 3 * COLS
FRAME = (ROWS + 2) * SPAN
CELLS = ROWS * COLS
LATS = 32
LONS = 16
CHUNK = 144
SCALING = HEAD_DIM ** (-0.5)
FAR = -1e30
MESH = pl.DeviceIdType.MESH
BF16 = jnp.bfloat16
F32 = jnp.float32
VMEM = pltpu.VMEM
LIMIT = 56 * 1024 * 1024


def nn(left, right):
    return lax.dot_general(left, right, (((1,), (0,)), ((), ())), preferred_element_type=F32)


def nt(left, right):
    return lax.dot_general(left, right, (((1,), (1,)), ((), ())), preferred_element_type=F32)


def tn(left, right):
    return lax.dot_general(left, right, (((0,), (0,)), ((), ())), preferred_element_type=F32)


def place():
    return lax.axis_index("lat"), lax.axis_index("lon")


def neighbours(lat, lon):
    found = []
    for row_step in (-1, 0, 1):
        for col_step in (-1, 0, 1):
            if row_step or col_step:
                target = (
                    lax.rem(lat + row_step + LATS, LATS),
                    lax.rem(lon + col_step + LONS, LONS),
                )
                found.append((row_step, col_step, target))
    return found


def to_chip(y, z, x, core):
    return (y * 4 + z // 2, x * 4 + lax.rem(z, 2) * 2 + core)


def remote(src, dst, send, recv, target):
    return pltpu.make_async_remote_copy(
        src_ref=src,
        dst_ref=dst,
        send_sem=send,
        recv_sem=recv,
        device_id=target,
        device_id_type=MESH,
    )


def whole_kernel(
    tokens_hbm,
    cot_hbm,
    w_qkv_hbm,
    w_out_hbm,
    w_disco_hbm,
    psi_ref,
    reach_ref,
    bias_ref,
    mixed_hbm,
    input_hbm,
    last_in,
    mixed_ref,
    input_ref,
    frame,
    cot_ref,
    w_qkv,
    w_out,
    w_disco,
    perm_x,
    perm_od,
    turned_own,
    turned_mid,
    turned_edge,
    kv_ref,
    canvas,
    probs_ref,
    low_ref,
    glow_ref,
    shifted,
    mix_in,
    dq_ref,
    gs_ref,
    grads,
    own_ref,
    rim_ref,
    pair_in,
    x_out,
    x_in,
    total_ref,
    pack_ref,
    z_out,
    z_in,
    last_out,
    rim_in,
    line_in,
    load_sem,
    store_sem,
    halo_send,
    halo_recv,
    pair_send,
    pair_recv,
    x_send,
    x_recv,
    z_send,
    z_recv,
    last_send,
    last_recv,
    rim_send,
    rim_recv,
):
    lat, lon = place()
    y, x, core = lat // 4, lon // 4, lax.rem(lon, 2)
    z = lax.rem(lat, 4) * 2 + lax.rem(lon, 4) // 2
    other = 1 - core

    loads = [
        pltpu.make_async_copy(tokens_hbm, frame.at[pl.ds(1, ROWS), pl.ds(COLS, COLS)], load_sem.at[0]),
        pltpu.make_async_copy(w_qkv_hbm, w_qkv, load_sem.at[1]),
        pltpu.make_async_copy(cot_hbm, cot_ref, load_sem.at[2]),
        pltpu.make_async_copy(w_out_hbm, w_out, load_sem.at[3]),
        pltpu.make_async_copy(w_disco_hbm, w_disco, load_sem.at[4]),
    ]
    for load in loads:
        load.start()

    around = neighbours(lat, lon)
    pair_peer = (lat, lon + 1 - 2 * core)
    x_peers = []
    for d in range(1, 4):
        there, back = lax.rem(x + d, 4), lax.rem(x + 4 - d, 4)
        x_peers.append((there, to_chip(y, z, there, core), to_chip(y, z, back, core)))
    z_peers = []
    for d in range(1, 8):
        there, back = lax.rem(z + d, 8), lax.rem(z + 8 - d, 8)
        z_peers.append((there, to_chip(y, there, x, core), to_chip(y, back, x, core)))
    owners = {}
    for job in range(2):
        for half in range(2):
            for to_core in range(2):
                row = (4 * job + half) + 2 * core
                mine = (row == y) & (core == to_core)
                owners[job, half, to_core] = (to_chip(row, z, x, to_core), mine)
    from_core = lax.rem(y, 4) // 2
    sources = []
    for k in range(8):
        mine = (y == k) & (core == from_core)
        sources.append((to_chip(k, z, x, from_core), mine))

    barrier = pltpu.get_barrier_semaphore()

    def hail(target):
        pl.semaphore_signal(barrier, inc=1, device_id=target, device_id_type=MESH)

    for _, _, target in around:
        hail(target)
    hail(pair_peer)
    for _, _, back in x_peers + z_peers:
        hail(back)
    for target, mine in sources:

        @pl.when(jnp.logical_not(mine))
        def _():
            hail(target)

    expected = 8 + 1 + 3 + 7 + 8 - jnp.where(core == from_core, 1, 0)
    pl.semaphore_wait(barrier, expected)

    halo_copies = []
    for idx, (row_step, col_step, target) in enumerate(around):
        if row_step == -1:
            src, dst_rows = tokens_hbm.at[pl.ds(0, 1)], pl.ds(ROWS + 1, 1)
        elif row_step == 1:
            src, dst_rows = tokens_hbm.at[pl.ds(ROWS - 1, 1)], pl.ds(0, 1)
        else:
            src, dst_rows = tokens_hbm, pl.ds(1, ROWS)
        copy = remote(
            src,
            frame.at[dst_rows, pl.ds((1 - col_step) * COLS, COLS)],
            halo_send.at[idx],
            halo_recv.at[idx],
            target,
        )
        copy.start()
        halo_copies.append(copy)

    def ones_where(equal):
        return jnp.where(equal, 1.0, 0.0).astype(BF16)

    pos = lax.broadcasted_iota(jnp.int32, (C, 128), 0)
    lane = lax.broadcasted_iota(jnp.int32, (C, 128), 1)
    pos_z = lax.rem(pos // 6, 8)
    pos_y = (pos // 192) * 2 + lax.rem(pos // 3, 2)
    origin = 3 * (
        pos_y * 32 + (pos_z // 2) * 8 + lax.rem(pos // 48, 4) * 2 + lax.rem(pos_z, 2)
    ) + lax.rem(pos, 3)
    for t in range(3):
        perm_x[:, 128 * t : 128 * (t + 1)] = ones_where(lane + 128 * t == origin)
    pos = lax.broadcasted_iota(jnp.int32, (4 * CHUNK, 128), 0)
    lane = lax.broadcasted_iota(jnp.int32, (4 * CHUNK, 128), 1)
    pos_z = lax.rem(pos // 18, 8)
    origin = (
        288 * lax.rem(pos // 9, 2)
        + 72 * (pos_z // 2)
        + 18 * (pos // 144)
        + 9 * lax.rem(pos_z, 2)
        + lax.rem(pos, 9)
    )
    for t in range(5):
        perm_od[0, :, 128 * t : 128 * (t + 1)] = ones_where(lane + 128 * t == origin)
        perm_od[1, :, 128 * t : 128 * (t + 1)] = ones_where(lane + 128 * t - 64 == origin)

    stack = HEADS * COLS
    head_mask = ones_where(
        lax.broadcasted_iota(jnp.int32, (stack, C), 0) // COLS
        == lax.broadcasted_iota(jnp.int32, (stack, C), 1) // HEAD_DIM
    )
    lane_head = lax.broadcasted_iota(jnp.int32, (COLS, C), 1) // HEAD_DIM
    distance = jnp.abs(
        lax.broadcasted_iota(jnp.int32, (SPAN, stack), 0)
        - COLS
        - lax.rem(lax.broadcasted_iota(jnp.int32, (SPAN, stack), 1), COLS)
    )
    stack_head = lax.broadcasted_iota(jnp.int32, (1, stack), 1) // COLS
    bias_lane = lax.broadcasted_iota(jnp.int32, (HEADS, LATS * ROWS), 1)
    bias_rows = []
    for k in range(ROWS + 2):
        global_row = lat * ROWS - 1 + k
        clamped = jnp.clip(global_row, 0, LATS * ROWS - 1)
        biases = jnp.sum(
            jnp.where(bias_lane == clamped, bias_ref[...], 0.0), axis=1, keepdims=True
        )
        line = jnp.zeros((1, stack), F32)
        for h in range(HEADS):
            line = jnp.where(stack_head == h, biases[h : h + 1], line)
        valid = (global_row >= 0) & (global_row < LATS * ROWS)
        bias_rows.append(jnp.where(valid, line, FAR))

    for load in loads:
        load.wait()
    x_own = frame[1 : ROWS + 1, COLS : 2 * COLS].reshape(CELLS, C)
    cot = cot_ref[...].reshape(CELLS, C)
    queries = nn(x_own, w_qkv[:, :C]).astype(BF16)
    upstream = nt(cot, w_out[...]).astype(BF16)
    gs_ref[...] = nt(cot, w_disco[...]).astype(BF16).astype(F32)
    turned_own[...] = nt(perm_x[...], x_own).astype(BF16)
    canvas[...] = jnp.zeros_like(canvas)

    sides = [idx for idx, (row_step, _, _) in enumerate(around) if row_step == 0]
    for idx in sides:
        halo_copies[idx].wait()
    middle = frame[1 : ROWS + 1].reshape(ROWS * SPAN, C)
    kv_ref[SPAN : SPAN + ROWS * SPAN] = nn(middle, w_qkv[:, C:]).astype(BF16)
    turned_mid[...] = nt(perm_x[...], middle).astype(BF16)
    for idx, copy in enumerate(halo_copies):
        if idx not in sides:
            copy.wait()

    @pl.when(lat == 0)
    def _():
        frame[0] = jnp.zeros((SPAN, C), BF16)

    @pl.when(lat == LATS - 1)
    def _():
        frame[ROWS + 1] = jnp.zeros((SPAN, C), BF16)

    edges = jnp.concatenate([frame[0], frame[ROWS + 1]], axis=0)
    edge_kv = nn(edges, w_qkv[:, C:]).astype(BF16)
    kv_ref[:SPAN] = edge_kv[:SPAN]
    kv_ref[FRAME - SPAN :] = edge_kv[SPAN:]

    for r in range(ROWS + 2):
        wide = frame[r, 16:80].astype(F32)
        shifted[0, r] = pltpu.roll(wide, 1, 0)[16:48]
        shifted[1, r] = wide[16:48]
        shifted[2, r] = pltpu.roll(wide, 63, 0)[16:48]
    for r in range(ROWS):
        for k in range(2):
            total = jnp.zeros((COLS, C), F32)
            for a in range(3):
                for b in range(3):
                    total = total + psi_ref[r, 9 * k + 3 * a + b] * shifted[b, r + a]
            mix_in[r * COLS : (r + 1) * COLS, (k + 1) * C : (k + 2) * C] = total.astype(BF16)

    def fold_heads(weights, channels, rows):
        folded = []
        for g in range(2):
            window = kv_ref[rows, channels + 128 * g : channels + 128 * g + 256]
            wide = tn(weights[:, 128 * g : 128 * (g + 1)], window)
            total = jnp.zeros((COLS, 256), F32)
            for h in range(4):
                total = jnp.where(
                    lane_head[:, 128 * g : 128 * g + 256] == 4 * g + h,
                    wide[h * COLS : (h + 1) * COLS],
                    total,
                )
            folded.append(total)
        first, second = folded
        return jnp.concatenate(
            [first[:, :128], first[:, 128:] + second[:, :128], second[:, 128:]], axis=1
        )

    def key_rows(r):
        return slice(r * SPAN, (r + 3) * SPAN)

    def all_heads(source, r):
        return jnp.concatenate([source[r * COLS : (r + 1) * COLS]] * HEADS, axis=0) * head_mask

    q_heads = [all_heads(queries, r) for r in range(ROWS)]
    u_heads = [all_heads(upstream, r) for r in range(ROWS)]
    for r in range(ROWS):
        outside = jnp.where(distance <= reach_ref[r], 0.0, FAR)
        added = jnp.concatenate([outside + bias_rows[r + a] for a in range(3)], axis=0)
        probs_ref[r] = nt(kv_ref[key_rows(r), :C], q_heads[r]) * SCALING + added
    for r in range(ROWS):
        logits = probs_ref[r]
        probs = jnp.exp(logits - jnp.max(logits, axis=0, keepdims=True))
        probs = probs * (1.0 / jnp.sum(probs, axis=0, keepdims=True))
        probs_ref[r] = probs
        low_ref[r] = probs.astype(BF16)
    for r in range(ROWS):
        mix_in[r * COLS : (r + 1) * COLS, :C] = fold_heads(low_ref[r], C, key_rows(r)).astype(BF16)

    def mix_weights(half):
        window = mix_in[:, pl.ds(pl.multiple_of(512 * half, 128), 640)]
        turned = nt(perm_od[half], window).astype(BF16)
        grads[1, pl.ds(4 * half, 4)] = nn(turned, cot).astype(BF16).reshape(4, CHUNK, C)

    def pair_copy(job, step):
        there = lax.rem(x + step, 4)
        return remote(
            grads.at[job, other * 4 + there],
            pair_in.at[job, there],
            pair_send.at[job, step],
            pair_recv.at[job, step],
            pair_peer,
        )

    def send_pair(job):
        for step in (2, 1, 3, 0):
            pair_copy(job, step).start()

    def x_copy(job, d):
        return remote(
            x_out.at[job, d], x_in.at[job, d], x_send.at[job, d], x_recv.at[job, d], x_peers[d][1]
        )

    def z_copies(job):
        return [
            remote(
                z_out.at[job, there],
                z_in.at[job, d],
                z_send.at[job, d],
                z_recv.at[job, d],
                target,
            )
            for d, (there, target, _) in enumerate(z_peers)
        ]

    def last_copy(job, half, to_core):
        return remote(
            last_out.at[job, pl.ds(half * 32, 32)],
            last_in.at[y],
            last_send.at[job, 2 * half + to_core],
            last_recv.at[y],
            owners[job, half, to_core][0],
        )

    def send_x(job):
        for d in (1, 0, 2):
            there = x_peers[d][0]
            pair_copy(job, d + 1).wait()
            added = grads[job, core * 4 + there].astype(F32) + pair_in[job, there].astype(F32)
            x_out[job, d] = added.astype(BF16)
            x_copy(job, d).start()

    def send_z(job):
        pair_copy(job, 0).wait()
        total = grads[job, core * 4 + x].astype(F32) + pair_in[job, x].astype(F32)
        for d in range(3):
            x_copy(job, d).wait()
            total = total + x_in[job, d].astype(F32)
        total_ref[job, 0:8] = jnp.zeros((8, C), F32)
        total_ref[job, 8 : 8 + CHUNK] = total
        total_ref[job, 8 + CHUNK : 32 + CHUNK] = jnp.zeros((24, C), F32)
        for k in range(8):
            for half in range(2):
                for t in range(3):
                    lanes = slice(128 * t, 128 * (t + 1))
                    to = 64 * k + 32 * half + 9 * t
                    if job == 1:
                        first = 8 + 18 * k + 9 * half
                        pack_ref[job, to : to + 16] = total_ref[job, first : first + 16, lanes]
                    else:
                        for m in range(3):
                            first = 8 + 48 * m + 6 * k + 3 * half
                            pack_ref[job, to + 3 * m : to + 3 * m + 8] = total_ref[
                                job, first : first + 8, lanes
                            ]
        for k in range(8):
            z_out[job, k] = pack_ref[job, 64 * k : 64 * k + 64].astype(BF16)
        for copy in z_copies(job):
            copy.start()

    def send_last(job):
        total = z_out[job, z].astype(F32)
        for d, copy in enumerate(z_copies(job)):
            copy.wait()
            total = total + z_in[job, d].astype(F32)
        last_out[job] = total.astype(BF16)
        for half in range(2):
            for to_core in range(2):
                mine = owners[job, half, to_core][1]

                @pl.when(jnp.logical_not(mine))
                def _():
                    last_copy(job, half, to_core).start()

                @pl.when(mine)
                def _():
                    last_in[y] = last_out[job, half * 32 : half * 32 + 32]

    mix_weights(other)
    send_pair(1)
    mix_weights(core)

    for r in range(ROWS):
        grad_prob = nt(kv_ref[key_rows(r), C:], u_heads[r]).astype(BF16).astype(F32)
        probs = probs_ref[r]
        mean = jnp.sum(probs * grad_prob, axis=0, keepdims=True)
        glow_ref[r] = (probs * (grad_prob - mean)).astype(BF16)
    send_x(1)
    for r in range(ROWS):
        cells = slice(r * COLS, (r + 1) * COLS)
        dq_ref[cells] = (fold_heads(glow_ref[r], 0, key_rows(r)) * SCALING).astype(BF16)
        canvas[key_rows(r), :C] += nn(glow_ref[r], q_heads[r]) * SCALING
        canvas[key_rows(r), C:] += nn(low_ref[r], u_heads[r])

    grad_query = dq_ref[...]
    kv_part = canvas[...].astype(BF16)
    kv_middle = kv_part[SPAN : SPAN + ROWS * SPAN]
    kv_edges = jnp.concatenate([kv_part[:SPAN], kv_part[FRAME - SPAN :]], axis=0)
    turned_edge[...] = nt(perm_x[...], edges).astype(BF16)

    def token_weights(half):
        lines = pl.ds(pl.multiple_of(192 * half, 64), 192)
        query_weight = nn(turned_own[lines], grad_query).astype(BF16)
        kv_weight = nn(turned_mid[lines], kv_middle) + nn(turned_edge[lines], kv_edges)
        kv_weight = kv_weight.astype(BF16)
        for c in range(4):
            part = slice(48 * c, 48 * (c + 1))
            grads[0, 4 * half + c, 0:48] = query_weight[part]
            grads[0, 4 * half + c, 48:96] = kv_weight[part, :C]
            grads[0, 4 * half + c, 96:144] = kv_weight[part, C:]

    token_weights(other)
    send_pair(0)
    token_weights(core)

    canvas[:, :C] = nt(kv_part, w_qkv[:, C:])
    send_x(0)
    query_part = nt(grad_query, w_qkv[:, :C])
    margin = jnp.zeros((16, C), F32)
    for row in range(ROWS + 2):
        spread = jnp.zeros((64, C), F32)
        for b in range(3):
            total = jnp.zeros((COLS, C), F32)
            for a in range(3):
                r = row - a
                if 0 <= r < ROWS:
                    for k in range(2):
                        total = total + (
                            psi_ref[r, 9 * k + 3 * a + b]
                            * gs_ref[r * COLS : (r + 1) * COLS, k * C : (k + 1) * C]
                        )
            total = jnp.concatenate([margin, total, margin], axis=0)
            spread = spread + (total if b == 1 else pltpu.roll(total, 63 if b == 0 else 1, 0))
        canvas[row * SPAN + 16 : row * SPAN + 80, :C] += spread
    rim_ref[...] = canvas[:, :C].astype(BF16).reshape(ROWS + 2, SPAN, C)
    rim_copies = []
    for idx, (row_step, col_step, target) in enumerate(around):
        if row_step == 0:
            src = rim_ref.at[pl.ds(1, ROWS), pl.ds((1 + col_step) * COLS, COLS)]
            dst = rim_in.at[0 if col_step == -1 else 1]
        else:
            row = 0 if row_step == -1 else ROWS + 1
            src = rim_ref.at[row, pl.ds((1 + col_step) * COLS, COLS)]
            dst = line_in.at[(0 if row_step == -1 else 3) + col_step + 1]
        copy = remote(src, dst, rim_send.at[idx], rim_recv.at[idx], target)
        copy.start()
        rim_copies.append(copy)
    for r in range(ROWS):
        at = (r + 1) * SPAN + COLS
        own_ref[r] = canvas[at : at + COLS, :C] + query_part[r * COLS : (r + 1) * COLS]

    send_z(1)
    mixed = nn(mix_in[:, :C], w_out[...]) + nn(mix_in[:, C:], w_disco[...])
    mixed_ref[...] = mixed.astype(BF16).reshape(ROWS, COLS, C)
    mixed_store = pltpu.make_async_copy(mixed_ref, mixed_hbm, store_sem.at[0])
    mixed_store.start()
    send_z(0)
    send_last(1)

    for copy in rim_copies:
        copy.wait()
    above = jnp.where(lat > 0, 1.0, 0.0)
    below = jnp.where(lat < LATS - 1, 1.0, 0.0)
    for r in range(ROWS):
        summed = own_ref[r] + rim_in[0, r].astype(F32) + rim_in[1, r].astype(F32)
        for side in range(3):
            if r == 0:
                summed = summed + above * line_in[3 + side].astype(F32)
            if r == ROWS - 1:
                summed = summed + below * line_in[side].astype(F32)
        input_ref[r] = summed.astype(BF16)
    input_store = pltpu.make_async_copy(input_ref, input_hbm, store_sem.at[1])
    input_store.start()

    send_last(0)
    for k, (source, mine) in enumerate(sources):

        @pl.when(jnp.logical_not(mine))
        def _():
            remote(
                last_out.at[0, pl.ds(0, 32)],
                last_in.at[k],
                last_send.at[0, 0],
                last_recv.at[k],
                source,
            ).wait_recv()

    for (job, half, to_core), (_, mine) in owners.items():

        @pl.when(jnp.logical_not(mine))
        def _():
            last_copy(job, half, to_core).wait_send()

    mixed_store.wait()
    input_store.wait()


def whole(tokens, cotangent, w_qkv, w_out, w_disco, psi, reach, key_bias):
    vmem = pl.BlockSpec(memory_space=VMEM)
    smem = pl.BlockSpec(memory_space=pltpu.SMEM)
    anywhere = pl.BlockSpec(memory_space=pl.ANY)
    dma = pltpu.SemaphoreType.DMA
    return pl.pallas_call(
        whole_kernel,
        out_shape=(
            jax.ShapeDtypeStruct((ROWS, COLS, C), BF16),
            jax.ShapeDtypeStruct((ROWS, COLS, C), BF16),
            jax.ShapeDtypeStruct((8, 32, 128), BF16),
        ),
        in_specs=[anywhere] * 5 + [smem] * 2 + [vmem],
        out_specs=(anywhere, anywhere, vmem),
        scratch_shapes=[
            VMEM((ROWS, COLS, C), BF16),
            VMEM((ROWS, COLS, C), BF16),
            VMEM((ROWS + 2, SPAN, C), BF16),
            VMEM((ROWS, COLS, C), BF16),
            VMEM((C, 3 * C), BF16),
            VMEM((C, C), BF16),
            VMEM((2 * C, C), BF16),
            VMEM((C, C), BF16),
            VMEM((2, 4 * CHUNK, 640), BF16),
            VMEM((C, CELLS), BF16),
            VMEM((C, ROWS * SPAN), BF16),
            VMEM((C, 2 * SPAN), BF16),
            VMEM((FRAME, 2 * C), BF16),
            VMEM((FRAME, 2 * C), F32),
            VMEM((ROWS, 3 * SPAN, HEADS * COLS), F32),
            VMEM((ROWS, 3 * SPAN, HEADS * COLS), BF16),
            VMEM((ROWS, 3 * SPAN, HEADS * COLS), BF16),
            VMEM((3, ROWS + 2, COLS, C), F32),
            VMEM((CELLS, 3 * C), BF16),
            VMEM((CELLS, C), BF16),
            VMEM((CELLS, 2 * C), F32),
            VMEM((2, 8, CHUNK, C), BF16),
            VMEM((ROWS, COLS, C), F32),
            VMEM((ROWS + 2, SPAN, C), BF16),
            VMEM((2, 4, CHUNK, C), BF16),
            VMEM((2, 3, CHUNK, C), BF16),
            VMEM((2, 3, CHUNK, C), BF16),
            VMEM((2, CHUNK + 32, C), F32),
            VMEM((2, 8 * 64 + 16, 128), F32),
            VMEM((2, 8, 64, 128), BF16),
            VMEM((2, 7, 64, 128), BF16),
            VMEM((2, 64, 128), BF16),
            VMEM((2, ROWS, COLS, C), BF16),
            VMEM((6, COLS, C), BF16),
            dma((5,)),
            dma((2,)),
            dma((8,)),
            dma((8,)),
            dma((2, 4)),
            dma((2, 4)),
            dma((2, 3)),
            dma((2, 3)),
            dma((2, 7)),
            dma((2, 7)),
            dma((2, 4)),
            dma((8,)),
            dma((8,)),
            dma((8,)),
        ],
        compiler_params=pltpu.CompilerParams(
            collective_id=0, has_side_effects=True, vmem_limit_bytes=LIMIT
        ),
    )(tokens, cotangent, w_qkv, w_out, w_disco, psi, reach, key_bias.T)


def finish_kernel(mixed_in, input_in, lines_ref, mixed_out, input_out, weight_ref):
    mixed_out[...] = mixed_in[...]
    input_out[...] = input_in[...]
    lat, lon = place()
    total = lines_ref[0].astype(F32)
    for k in range(1, 8):
        total = total + lines_ref[k].astype(F32)
    strips = []
    for row in range(9):
        origin = 3 * (row % 3) + row // 3
        for t in range(3):
            at, late = 9 * t + origin, 9 * t + row
            strips.append(jnp.where(lat < 16, total[at : at + 1], total[late : late + 1]))
    turned = [pltpu.roll(strip, 64, 1) for strip in strips[13:]]
    left = lax.broadcasted_iota(jnp.int32, (1, 128), 1) < 64
    first_core = lax.rem(lon, 2) == 0
    for j in range(14):
        later = turned[j] if j == 13 else jnp.where(left, turned[j], turned[j + 1])
        strip = jnp.where(first_core, strips[j], later).reshape(128)
        if j < 13:
            weight_ref[128 * j : 128 * (j + 1)] = strip
        else:
            weight_ref[128 * j : 128 * j + 64] = strip[:64]


def finish(mixed, input_grad, lines):
    vmem = pl.BlockSpec(memory_space=VMEM)
    return pl.pallas_call(
        finish_kernel,
        out_shape=(
            jax.ShapeDtypeStruct((ROWS, COLS, C), BF16),
            jax.ShapeDtypeStruct((ROWS, COLS, C), BF16),
            jax.ShapeDtypeStruct((9 * C // 2,), F32),
        ),
        in_specs=[vmem] * 3,
        out_specs=(vmem,) * 3,
    )(mixed, input_grad, lines)


def on_device(tokens, w_qkv, w_out, w_disco, psi, reach, key_bias, cotangent):
    mixed, input_grad, lines = whole(
        tokens, cotangent, w_qkv, w_out, w_disco, psi, reach, key_bias
    )
    return finish(mixed, input_grad, lines)


def solution(mesh):
    placed = (
        P("lat", "lon", None),
        P(),
        P(),
        P(),
        P("lat", None),
        P("lat"),
        P(),
        P("lat", "lon", None),
    )
    return jax.shard_map(
        on_device,
        mesh=mesh,
        in_specs=placed,
        out_specs=(P("lat", "lon", None), P("lat", "lon", None), P(("lat", "lon"))),
        check_vma=False,
    )
```

```python
import jax
import jax.numpy as jnp
from jax import lax
from jax.experimental import pallas as pl
from jax.experimental.pallas import tpu as pltpu
from jax.sharding import PartitionSpec as P

HEADS = 8
HEAD_DIM = 48
C = 384
ROWS = 4
COLS = 32
SPAN = 3 * COLS
FRAME = (ROWS + 2) * SPAN
CELLS = ROWS * COLS
LATS = 32
LONS = 16
CHUNK = 144
SCALING = HEAD_DIM ** (-0.5)
FAR = -1e30
MESH = pl.DeviceIdType.MESH
BF16 = jnp.bfloat16
F32 = jnp.float32
VMEM = pltpu.VMEM
LIMIT = 56 * 1024 * 1024


def nn(left, right):
    return lax.dot_general(left, right, (((1,), (0,)), ((), ())), preferred_element_type=F32)


def nt(left, right):
    return lax.dot_general(left, right, (((1,), (1,)), ((), ())), preferred_element_type=F32)


def tn(left, right):
    return lax.dot_general(left, right, (((0,), (0,)), ((), ())), preferred_element_type=F32)


def place():
    return lax.axis_index("lat"), lax.axis_index("lon")


def neighbours(lat, lon):
    found = []
    for row_step in (-1, 0, 1):
        for col_step in (-1, 0, 1):
            if row_step or col_step:
                target = (
                    lax.rem(lat + row_step + LATS, LATS),
                    lax.rem(lon + col_step + LONS, LONS),
                )
                found.append((row_step, col_step, target))
    return found


def to_chip(y, z, x, core):
    return (y * 4 + z // 2, x * 4 + lax.rem(z, 2) * 2 + core)


def remote(src, dst, send, recv, target):
    return pltpu.make_async_remote_copy(
        src_ref=src,
        dst_ref=dst,
        send_sem=send,
        recv_sem=recv,
        device_id=target,
        device_id_type=MESH,
    )


def whole_kernel(
    tokens_hbm,
    cot_hbm,
    w_qkv_hbm,
    w_out_hbm,
    w_disco_hbm,
    psi_ref,
    reach_ref,
    bias_ref,
    mixed_hbm,
    input_hbm,
    last_in,
    mixed_ref,
    input_ref,
    frame,
    cot_ref,
    w_qkv,
    w_out,
    w_disco,
    perm_x,
    perm_od,
    turned_own,
    turned_mid,
    turned_edge,
    kv_ref,
    canvas,
    probs_ref,
    low_ref,
    glow_ref,
    shifted,
    mix_in,
    dq_ref,
    gs_ref,
    grads,
    own_ref,
    rim_ref,
    pair_in,
    x_out,
    x_in,
    total_ref,
    pack_ref,
    z_out,
    z_in,
    last_out,
    rim_in,
    line_in,
    far_sem,
    load_sem,
    store_sem,
    halo_send,
    halo_recv,
    pair_send,
    pair_recv,
    x_send,
    x_recv,
    z_send,
    z_recv,
    last_send,
    last_recv,
    rim_send,
    rim_recv,
):
    lat, lon = place()
    y, x, core = lat // 4, lon // 4, lax.rem(lon, 2)
    z = lax.rem(lat, 4) * 2 + lax.rem(lon, 4) // 2
    other = 1 - core

    loads = [
        pltpu.make_async_copy(tokens_hbm, frame.at[pl.ds(1, ROWS), pl.ds(COLS, COLS)], load_sem.at[0]),
        pltpu.make_async_copy(w_qkv_hbm, w_qkv, load_sem.at[1]),
        pltpu.make_async_copy(cot_hbm, cot_ref, load_sem.at[2]),
        pltpu.make_async_copy(w_out_hbm, w_out, load_sem.at[3]),
        pltpu.make_async_copy(w_disco_hbm, w_disco, load_sem.at[4]),
    ]
    for load in loads:
        load.start()

    around = neighbours(lat, lon)
    pair_peer = (lat, lon + 1 - 2 * core)
    x_peers = []
    for d in range(1, 4):
        there, back = lax.rem(x + d, 4), lax.rem(x + 4 - d, 4)
        x_peers.append((there, to_chip(y, z, there, core), to_chip(y, z, back, core)))
    z_peers = []
    for d in range(1, 8):
        there, back = lax.rem(z + d, 8), lax.rem(z + 8 - d, 8)
        z_peers.append((there, to_chip(y, there, x, core), to_chip(y, back, x, core)))
    owners = {}
    for job in range(2):
        for half in range(2):
            for to_core in range(2):
                row = (4 * job + half) + 2 * core
                mine = (row == y) & (core == to_core)
                owners[job, half, to_core] = (to_chip(row, z, x, to_core), mine)
    from_core = lax.rem(y, 4) // 2
    sources = []
    for k in range(8):
        mine = (y == k) & (core == from_core)
        sources.append((to_chip(k, z, x, from_core), mine))

    barrier = pltpu.get_barrier_semaphore()
    east = (lat, lax.rem(lon + 1, LONS))
    west = (lat, lax.rem(lon + LONS - 1, LONS))
    north = (lax.rem(lat + LATS - 1, LATS), lon)
    south = (lax.rem(lat + 1, LATS), lon)
    near = [east, west, north, south, pair_peer] + [back for _, _, back in x_peers]
    for step in (1, 2, 6, 7):
        near.append(to_chip(y, lax.rem(z + step, 8), x, core))
        near += [to_chip(lax.rem(y + step, 8), z, x, c) for c in (core, other)]
    for target in near:
        pl.semaphore_signal(barrier, inc=1, device_id=target, device_id_type=MESH)
    pl.semaphore_wait(barrier, len(near))

    def halo_copy(idx, src, rows, cols, target):
        dst = frame.at[rows, cols]
        copy = remote(src, dst, halo_send.at[idx], halo_recv.at[idx], target)
        copy.start()
        return copy

    left, centre, right = (pl.ds(COLS * part, COLS) for part in range(3))
    first, last = pl.ds(0, 1), pl.ds(ROWS - 1, 1)
    above_row, below_row = pl.ds(0, 1), pl.ds(ROWS + 1, 1)
    halo_copies = [
        halo_copy(0, tokens_hbm, pl.ds(1, ROWS), left, east),
        halo_copy(1, tokens_hbm, pl.ds(1, ROWS), right, west),
        halo_copy(2, tokens_hbm.at[first], below_row, centre, north),
        halo_copy(3, tokens_hbm.at[last], above_row, centre, south),
    ]
    for step in (2, 6):
        for target in (
            to_chip(y, lax.rem(z + step, 8), x, core),
            to_chip(lax.rem(y + step, 8), z, x, core),
        ):
            pl.semaphore_signal(far_sem, inc=1, device_id=target, device_id_type=MESH)

    def ones_where(equal):
        return jnp.where(equal, 1.0, 0.0).astype(BF16)

    pos = lax.broadcasted_iota(jnp.int32, (C, 128), 0)
    lane = lax.broadcasted_iota(jnp.int32, (C, 128), 1)
    pos_z = lax.rem(pos // 6, 8)
    pos_y = (pos // 192) * 2 + lax.rem(pos // 3, 2)
    origin = 3 * (
        pos_y * 32 + (pos_z // 2) * 8 + lax.rem(pos // 48, 4) * 2 + lax.rem(pos_z, 2)
    ) + lax.rem(pos, 3)
    for t in range(3):
        perm_x[:, 128 * t : 128 * (t + 1)] = ones_where(lane + 128 * t == origin)
    pos = lax.broadcasted_iota(jnp.int32, (4 * CHUNK, 128), 0)
    lane = lax.broadcasted_iota(jnp.int32, (4 * CHUNK, 128), 1)
    pos_z = lax.rem(pos // 18, 8)
    origin = (
        288 * lax.rem(pos // 9, 2)
        + 72 * (pos_z // 2)
        + 18 * (pos // 144)
        + 9 * lax.rem(pos_z, 2)
        + lax.rem(pos, 9)
    )
    for t in range(5):
        perm_od[0, :, 128 * t : 128 * (t + 1)] = ones_where(lane + 128 * t == origin)
        perm_od[1, :, 128 * t : 128 * (t + 1)] = ones_where(lane + 128 * t - 64 == origin)

    stack = HEADS * COLS
    head_mask = ones_where(
        lax.broadcasted_iota(jnp.int32, (stack, C), 0) // COLS
        == lax.broadcasted_iota(jnp.int32, (stack, C), 1) // HEAD_DIM
    )
    lane_head = lax.broadcasted_iota(jnp.int32, (COLS, C), 1) // HEAD_DIM
    distance = jnp.abs(
        lax.broadcasted_iota(jnp.int32, (SPAN, stack), 0)
        - COLS
        - lax.rem(lax.broadcasted_iota(jnp.int32, (SPAN, stack), 1), COLS)
    )
    stack_head = lax.broadcasted_iota(jnp.int32, (1, stack), 1) // COLS
    bias_lane = lax.broadcasted_iota(jnp.int32, (HEADS, LATS * ROWS), 1)
    bias_rows = []
    for k in range(ROWS + 2):
        global_row = lat * ROWS - 1 + k
        clamped = jnp.clip(global_row, 0, LATS * ROWS - 1)
        biases = jnp.sum(
            jnp.where(bias_lane == clamped, bias_ref[...], 0.0), axis=1, keepdims=True
        )
        line = jnp.zeros((1, stack), F32)
        for h in range(HEADS):
            line = jnp.where(stack_head == h, biases[h : h + 1], line)
        valid = (global_row >= 0) & (global_row < LATS * ROWS)
        bias_rows.append(jnp.where(valid, line, FAR))

    for load in loads:
        load.wait()
    x_own = frame[1 : ROWS + 1, COLS : 2 * COLS].reshape(CELLS, C)
    cot = cot_ref[...].reshape(CELLS, C)
    queries = nn(x_own, w_qkv[:, :C]).astype(BF16)
    upstream = nt(cot, w_out[...]).astype(BF16)
    gs_ref[...] = nt(cot, w_disco[...]).astype(BF16).astype(F32)
    turned_own[...] = nt(perm_x[...], x_own).astype(BF16)
    canvas[...] = jnp.zeros_like(canvas)

    for idx, cols in ((0, left), (1, right)):
        halo_copies[idx].wait()
        halo_copies.append(halo_copy(4 + idx, frame.at[pl.ds(1, 1), cols], below_row, cols, north))
        halo_copies.append(halo_copy(6 + idx, frame.at[pl.ds(ROWS, 1), cols], above_row, cols, south))
    middle = frame[1 : ROWS + 1].reshape(ROWS * SPAN, C)
    kv_ref[SPAN : SPAN + ROWS * SPAN] = nn(middle, w_qkv[:, C:]).astype(BF16)
    turned_mid[...] = nt(perm_x[...], middle).astype(BF16)
    for copy in halo_copies[2:]:
        copy.wait()

    @pl.when(lat == 0)
    def _():
        frame[0] = jnp.zeros((SPAN, C), BF16)

    @pl.when(lat == LATS - 1)
    def _():
        frame[ROWS + 1] = jnp.zeros((SPAN, C), BF16)

    edges = jnp.concatenate([frame[0], frame[ROWS + 1]], axis=0)
    edge_kv = nn(edges, w_qkv[:, C:]).astype(BF16)
    kv_ref[:SPAN] = edge_kv[:SPAN]
    kv_ref[FRAME - SPAN :] = edge_kv[SPAN:]

    for r in range(ROWS + 2):
        wide = frame[r, 16:80].astype(F32)
        shifted[0, r] = pltpu.roll(wide, 1, 0)[16:48]
        shifted[1, r] = wide[16:48]
        shifted[2, r] = pltpu.roll(wide, 63, 0)[16:48]
    for r in range(ROWS):
        for k in range(2):
            total = jnp.zeros((COLS, C), F32)
            for a in range(3):
                for b in range(3):
                    total = total + psi_ref[r, 9 * k + 3 * a + b] * shifted[b, r + a]
            mix_in[r * COLS : (r + 1) * COLS, (k + 1) * C : (k + 2) * C] = total.astype(BF16)

    def fold_heads(weights, channels, rows):
        folded = []
        for g in range(2):
            window = kv_ref[rows, channels + 128 * g : channels + 128 * g + 256]
            wide = tn(weights[:, 128 * g : 128 * (g + 1)], window)
            total = jnp.zeros((COLS, 256), F32)
            for h in range(4):
                total = jnp.where(
                    lane_head[:, 128 * g : 128 * g + 256] == 4 * g + h,
                    wide[h * COLS : (h + 1) * COLS],
                    total,
                )
            folded.append(total)
        first, second = folded
        return jnp.concatenate(
            [first[:, :128], first[:, 128:] + second[:, :128], second[:, 128:]], axis=1
        )

    def key_rows(r):
        return slice(r * SPAN, (r + 3) * SPAN)

    def all_heads(source, r):
        return jnp.concatenate([source[r * COLS : (r + 1) * COLS]] * HEADS, axis=0) * head_mask

    q_heads = [all_heads(queries, r) for r in range(ROWS)]
    u_heads = [all_heads(upstream, r) for r in range(ROWS)]
    for r in range(ROWS):
        outside = jnp.where(distance <= reach_ref[r], 0.0, FAR)
        added = jnp.concatenate([outside + bias_rows[r + a] for a in range(3)], axis=0)
        probs_ref[r] = nt(kv_ref[key_rows(r), :C], q_heads[r]) * SCALING + added
    for r in range(ROWS):
        logits = probs_ref[r]
        probs = jnp.exp(logits - jnp.max(logits, axis=0, keepdims=True))
        probs = probs * (1.0 / jnp.sum(probs, axis=0, keepdims=True))
        probs_ref[r] = probs
        low_ref[r] = probs.astype(BF16)
    for r in range(ROWS):
        mix_in[r * COLS : (r + 1) * COLS, :C] = fold_heads(low_ref[r], C, key_rows(r)).astype(BF16)

    def mix_weights(half):
        window = mix_in[:, pl.ds(pl.multiple_of(512 * half, 128), 640)]
        turned = nt(perm_od[half], window).astype(BF16)
        grads[1, pl.ds(4 * half, 4)] = nn(turned, cot).astype(BF16).reshape(4, CHUNK, C)

    def pair_copy(job, step):
        there = lax.rem(x + step, 4)
        return remote(
            grads.at[job, other * 4 + there],
            pair_in.at[job, there],
            pair_send.at[job, step],
            pair_recv.at[job, step],
            pair_peer,
        )

    def send_pair(job):
        for step in (2, 1, 3, 0):
            pair_copy(job, step).start()

    def x_copy(job, d):
        return remote(
            x_out.at[job, d], x_in.at[job, d], x_send.at[job, d], x_recv.at[job, d], x_peers[d][1]
        )

    def z_copies(job):
        return [
            remote(
                z_out.at[job, there],
                z_in.at[job, d],
                z_send.at[job, d],
                z_recv.at[job, d],
                target,
            )
            for d, (there, target, _) in enumerate(z_peers)
        ]

    def last_copy(job, half, to_core):
        return remote(
            last_out.at[job, pl.ds(half * 32, 32)],
            last_in.at[y],
            last_send.at[job, 2 * half + to_core],
            last_recv.at[y],
            owners[job, half, to_core][0],
        )

    def send_x(job):
        for d in (1, 0, 2):
            there = x_peers[d][0]
            pair_copy(job, d + 1).wait()
            added = grads[job, core * 4 + there].astype(F32) + pair_in[job, there].astype(F32)
            x_out[job, d] = added.astype(BF16)
            x_copy(job, d).start()

    def send_z(job):
        pair_copy(job, 0).wait()
        total = grads[job, core * 4 + x].astype(F32) + pair_in[job, x].astype(F32)
        for d in range(3):
            x_copy(job, d).wait()
            total = total + x_in[job, d].astype(F32)
        total_ref[job, 0:8] = jnp.zeros((8, C), F32)
        total_ref[job, 8 : 8 + CHUNK] = total
        total_ref[job, 8 + CHUNK : 32 + CHUNK] = jnp.zeros((24, C), F32)
        for k in range(8):
            for half in range(2):
                for t in range(3):
                    lanes = slice(128 * t, 128 * (t + 1))
                    to = 64 * k + 32 * half + 9 * t
                    if job == 1:
                        first = 8 + 18 * k + 9 * half
                        pack_ref[job, to : to + 16] = total_ref[job, first : first + 16, lanes]
                    else:
                        for m in range(3):
                            first = 8 + 48 * m + 6 * k + 3 * half
                            pack_ref[job, to + 3 * m : to + 3 * m + 8] = total_ref[
                                job, first : first + 8, lanes
                            ]
        for k in range(8):
            z_out[job, k] = pack_ref[job, 64 * k : 64 * k + 64].astype(BF16)
        for copy in z_copies(job):
            copy.start()

    def send_last(job):
        total = z_out[job, z].astype(F32)
        for d, copy in enumerate(z_copies(job)):
            copy.wait()
            total = total + z_in[job, d].astype(F32)
        last_out[job] = total.astype(BF16)
        for half in range(2):
            for to_core in range(2):
                mine = owners[job, half, to_core][1]

                @pl.when(jnp.logical_not(mine))
                def _():
                    last_copy(job, half, to_core).start()

                @pl.when(mine)
                def _():
                    last_in[y] = last_out[job, half * 32 : half * 32 + 32]

    mix_weights(other)
    send_pair(1)
    mix_weights(core)

    for r in range(ROWS):
        grad_prob = nt(kv_ref[key_rows(r), C:], u_heads[r]).astype(BF16).astype(F32)
        probs = probs_ref[r]
        mean = jnp.sum(probs * grad_prob, axis=0, keepdims=True)
        glow_ref[r] = (probs * (grad_prob - mean)).astype(BF16)
    send_x(1)
    for r in range(ROWS):
        cells = slice(r * COLS, (r + 1) * COLS)
        dq_ref[cells] = (fold_heads(glow_ref[r], 0, key_rows(r)) * SCALING).astype(BF16)
        canvas[key_rows(r), :C] += nn(glow_ref[r], q_heads[r]) * SCALING
        canvas[key_rows(r), C:] += nn(low_ref[r], u_heads[r])

    grad_query = dq_ref[...]
    kv_part = canvas[...].astype(BF16)
    kv_middle = kv_part[SPAN : SPAN + ROWS * SPAN]
    kv_edges = jnp.concatenate([kv_part[:SPAN], kv_part[FRAME - SPAN :]], axis=0)
    turned_edge[...] = nt(perm_x[...], edges).astype(BF16)

    def token_weights(half):
        lines = pl.ds(pl.multiple_of(192 * half, 64), 192)
        query_weight = nn(turned_own[lines], grad_query).astype(BF16)
        kv_weight = nn(turned_mid[lines], kv_middle) + nn(turned_edge[lines], kv_edges)
        kv_weight = kv_weight.astype(BF16)
        for c in range(4):
            part = slice(48 * c, 48 * (c + 1))
            grads[0, 4 * half + c, 0:48] = query_weight[part]
            grads[0, 4 * half + c, 48:96] = kv_weight[part, :C]
            grads[0, 4 * half + c, 96:144] = kv_weight[part, C:]

    token_weights(other)
    send_pair(0)
    token_weights(core)

    canvas[:, :C] = nt(kv_part, w_qkv[:, C:])
    send_x(0)
    query_part = nt(grad_query, w_qkv[:, :C])
    margin = jnp.zeros((16, C), F32)
    for row in range(ROWS + 2):
        spread = jnp.zeros((64, C), F32)
        for b in range(3):
            total = jnp.zeros((COLS, C), F32)
            for a in range(3):
                r = row - a
                if 0 <= r < ROWS:
                    for k in range(2):
                        total = total + (
                            psi_ref[r, 9 * k + 3 * a + b]
                            * gs_ref[r * COLS : (r + 1) * COLS, k * C : (k + 1) * C]
                        )
            total = jnp.concatenate([margin, total, margin], axis=0)
            spread = spread + (total if b == 1 else pltpu.roll(total, 63 if b == 0 else 1, 0))
        canvas[row * SPAN + 16 : row * SPAN + 80, :C] += spread
    rim_ref[...] = canvas[:, :C].astype(BF16).reshape(ROWS + 2, SPAN, C)
    rim_copies = []
    for idx, (row_step, col_step, target) in enumerate(around):
        if row_step == 0:
            src = rim_ref.at[pl.ds(1, ROWS), pl.ds((1 + col_step) * COLS, COLS)]
            dst = rim_in.at[0 if col_step == -1 else 1]
        else:
            row = 0 if row_step == -1 else ROWS + 1
            src = rim_ref.at[row, pl.ds((1 + col_step) * COLS, COLS)]
            dst = line_in.at[(0 if row_step == -1 else 3) + col_step + 1]
        copy = remote(src, dst, rim_send.at[idx], rim_recv.at[idx], target)
        copy.start()
        rim_copies.append(copy)
    for r in range(ROWS):
        at = (r + 1) * SPAN + COLS
        own_ref[r] = canvas[at : at + COLS, :C] + query_part[r * COLS : (r + 1) * COLS]

    pl.semaphore_wait(far_sem, 4)
    send_z(1)
    mixed = nn(mix_in[:, :C], w_out[...]) + nn(mix_in[:, C:], w_disco[...])
    mixed_ref[...] = mixed.astype(BF16).reshape(ROWS, COLS, C)
    mixed_store = pltpu.make_async_copy(mixed_ref, mixed_hbm, store_sem.at[0])
    mixed_store.start()
    send_z(0)
    send_last(1)

    for copy in rim_copies:
        copy.wait()
    above = jnp.where(lat > 0, 1.0, 0.0)
    below = jnp.where(lat < LATS - 1, 1.0, 0.0)
    for r in range(ROWS):
        summed = own_ref[r] + rim_in[0, r].astype(F32) + rim_in[1, r].astype(F32)
        for side in range(3):
            if r == 0:
                summed = summed + above * line_in[3 + side].astype(F32)
            if r == ROWS - 1:
                summed = summed + below * line_in[side].astype(F32)
        input_ref[r] = summed.astype(BF16)
    input_store = pltpu.make_async_copy(input_ref, input_hbm, store_sem.at[1])
    input_store.start()

    send_last(0)
    for k, (source, mine) in enumerate(sources):

        @pl.when(jnp.logical_not(mine))
        def _():
            remote(
                last_out.at[0, pl.ds(0, 32)],
                last_in.at[k],
                last_send.at[0, 0],
                last_recv.at[k],
                source,
            ).wait_recv()

    for (job, half, to_core), (_, mine) in owners.items():

        @pl.when(jnp.logical_not(mine))
        def _():
            last_copy(job, half, to_core).wait_send()

    mixed_store.wait()
    input_store.wait()


def whole(tokens, cotangent, w_qkv, w_out, w_disco, psi, reach, key_bias):
    vmem = pl.BlockSpec(memory_space=VMEM)
    smem = pl.BlockSpec(memory_space=pltpu.SMEM)
    anywhere = pl.BlockSpec(memory_space=pl.ANY)
    dma = pltpu.SemaphoreType.DMA
    return pl.pallas_call(
        whole_kernel,
        out_shape=(
            jax.ShapeDtypeStruct((ROWS, COLS, C), BF16),
            jax.ShapeDtypeStruct((ROWS, COLS, C), BF16),
            jax.ShapeDtypeStruct((8, 32, 128), BF16),
        ),
        in_specs=[anywhere] * 5 + [smem] * 2 + [vmem],
        out_specs=(anywhere, anywhere, vmem),
        scratch_shapes=[
            VMEM((ROWS, COLS, C), BF16),
            VMEM((ROWS, COLS, C), BF16),
            VMEM((ROWS + 2, SPAN, C), BF16),
            VMEM((ROWS, COLS, C), BF16),
            VMEM((C, 3 * C), BF16),
            VMEM((C, C), BF16),
            VMEM((2 * C, C), BF16),
            VMEM((C, C), BF16),
            VMEM((2, 4 * CHUNK, 640), BF16),
            VMEM((C, CELLS), BF16),
            VMEM((C, ROWS * SPAN), BF16),
            VMEM((C, 2 * SPAN), BF16),
            VMEM((FRAME, 2 * C), BF16),
            VMEM((FRAME, 2 * C), F32),
            VMEM((ROWS, 3 * SPAN, HEADS * COLS), F32),
            VMEM((ROWS, 3 * SPAN, HEADS * COLS), BF16),
            VMEM((ROWS, 3 * SPAN, HEADS * COLS), BF16),
            VMEM((3, ROWS + 2, COLS, C), F32),
            VMEM((CELLS, 3 * C), BF16),
            VMEM((CELLS, C), BF16),
            VMEM((CELLS, 2 * C), F32),
            VMEM((2, 8, CHUNK, C), BF16),
            VMEM((ROWS, COLS, C), F32),
            VMEM((ROWS + 2, SPAN, C), BF16),
            VMEM((2, 4, CHUNK, C), BF16),
            VMEM((2, 3, CHUNK, C), BF16),
            VMEM((2, 3, CHUNK, C), BF16),
            VMEM((2, CHUNK + 32, C), F32),
            VMEM((2, 8 * 64 + 16, 128), F32),
            VMEM((2, 8, 64, 128), BF16),
            VMEM((2, 7, 64, 128), BF16),
            VMEM((2, 64, 128), BF16),
            VMEM((2, ROWS, COLS, C), BF16),
            VMEM((6, COLS, C), BF16),
            pltpu.SemaphoreType.REGULAR,
            dma((5,)),
            dma((2,)),
            dma((8,)),
            dma((8,)),
            dma((2, 4)),
            dma((2, 4)),
            dma((2, 3)),
            dma((2, 3)),
            dma((2, 7)),
            dma((2, 7)),
            dma((2, 4)),
            dma((8,)),
            dma((8,)),
            dma((8,)),
        ],
        compiler_params=pltpu.CompilerParams(
            collective_id=0, has_side_effects=True, vmem_limit_bytes=LIMIT
        ),
    )(tokens, cotangent, w_qkv, w_out, w_disco, psi, reach, key_bias.T)


def finish_kernel(mixed_in, input_in, lines_ref, mixed_out, input_out, weight_ref):
    mixed_out[...] = mixed_in[...]
    input_out[...] = input_in[...]
    lat, lon = place()
    total = lines_ref[0].astype(F32)
    for k in range(1, 8):
        total = total + lines_ref[k].astype(F32)
    strips = []
    for row in range(9):
        origin = 3 * (row % 3) + row // 3
        for t in range(3):
            at, late = 9 * t + origin, 9 * t + row
            strips.append(jnp.where(lat < 16, total[at : at + 1], total[late : late + 1]))
    turned = [pltpu.roll(strip, 64, 1) for strip in strips[13:]]
    left = lax.broadcasted_iota(jnp.int32, (1, 128), 1) < 64
    first_core = lax.rem(lon, 2) == 0
    for j in range(14):
        later = turned[j] if j == 13 else jnp.where(left, turned[j], turned[j + 1])
        strip = jnp.where(first_core, strips[j], later).reshape(128)
        if j < 13:
            weight_ref[128 * j : 128 * (j + 1)] = strip
        else:
            weight_ref[128 * j : 128 * j + 64] = strip[:64]


def finish(mixed, input_grad, lines):
    vmem = pl.BlockSpec(memory_space=VMEM)
    return pl.pallas_call(
        finish_kernel,
        out_shape=(
            jax.ShapeDtypeStruct((ROWS, COLS, C), BF16),
            jax.ShapeDtypeStruct((ROWS, COLS, C), BF16),
            jax.ShapeDtypeStruct((9 * C // 2,), F32),
        ),
        in_specs=[vmem] * 3,
        out_specs=(vmem,) * 3,
    )(mixed, input_grad, lines)


def on_device(tokens, w_qkv, w_out, w_disco, psi, reach, key_bias, cotangent):
    mixed, input_grad, lines = whole(
        tokens, cotangent, w_qkv, w_out, w_disco, psi, reach, key_bias
    )
    return finish(mixed, input_grad, lines)


def solution(mesh):
    placed = (
        P("lat", "lon", None),
        P(),
        P(),
        P(),
        P("lat", None),
        P("lat"),
        P(),
        P("lat", "lon", None),
    )
    return jax.shard_map(
        on_device,
        mesh=mesh,
        in_specs=placed,
        out_specs=(P("lat", "lon", None), P("lat", "lon", None), P(("lat", "lon"))),
        check_vma=False,
    )
```

```python
import jax
import jax.numpy as jnp
from jax import lax
from jax.experimental import pallas as pl
from jax.experimental.pallas import tpu as pltpu
from jax.sharding import PartitionSpec as P

HEADS = 8
HEAD_DIM = 48
C = 384
ROWS = 4
COLS = 32
SPAN = 3 * COLS
FRAME = (ROWS + 2) * SPAN
CELLS = ROWS * COLS
LATS = 32
LONS = 16
CHUNK = 144
SCALING = HEAD_DIM ** (-0.5)
FAR = -1e30
MESH = pl.DeviceIdType.MESH
BF16 = jnp.bfloat16
F32 = jnp.float32
VMEM = pltpu.VMEM
LIMIT = 56 * 1024 * 1024


def nn(left, right):
    return lax.dot_general(left, right, (((1,), (0,)), ((), ())), preferred_element_type=F32)


def nt(left, right):
    return lax.dot_general(left, right, (((1,), (1,)), ((), ())), preferred_element_type=F32)


def tn(left, right):
    return lax.dot_general(left, right, (((0,), (0,)), ((), ())), preferred_element_type=F32)


def place():
    return lax.axis_index("lat"), lax.axis_index("lon")


def neighbours(lat, lon):
    found = []
    for row_step in (-1, 0, 1):
        for col_step in (-1, 0, 1):
            if row_step or col_step:
                target = (
                    lax.rem(lat + row_step + LATS, LATS),
                    lax.rem(lon + col_step + LONS, LONS),
                )
                found.append((row_step, col_step, target))
    return found


def to_chip(y, z, x, core):
    return (y * 4 + z // 2, x * 4 + lax.rem(z, 2) * 2 + core)


def remote(src, dst, send, recv, target):
    return pltpu.make_async_remote_copy(
        src_ref=src,
        dst_ref=dst,
        send_sem=send,
        recv_sem=recv,
        device_id=target,
        device_id_type=MESH,
    )


def whole_kernel(
    tokens_hbm,
    cot_hbm,
    w_qkv_hbm,
    w_out_hbm,
    w_disco_hbm,
    psi_ref,
    reach_ref,
    bias_ref,
    mixed_hbm,
    input_hbm,
    last_in,
    mixed_ref,
    input_ref,
    frame,
    cots,
    slices,
    slices_in,
    w_qkv,
    w_out,
    w_disco,
    perm_x,
    perm_od,
    turned_own,
    turned_mid,
    turned_edge,
    kv_ref,
    canvas,
    probs_ref,
    low_ref,
    glow_ref,
    shifted,
    mix_in,
    dq_ref,
    gs_ref,
    grads,
    own_ref,
    rim_ref,
    pair_in,
    x_out,
    x_in,
    total_ref,
    pack_ref,
    z_out,
    z_in,
    last_out,
    rim_in,
    line_in,
    far_sem,
    load_sem,
    store_sem,
    cot_send,
    cot_recv,
    swap_send,
    swap_recv,
    slice_send,
    slice_recv,
    halo_send,
    halo_recv,
    pair_send,
    pair_recv,
    x_send,
    x_recv,
    z_send,
    z_recv,
    last_send,
    last_recv,
    rim_send,
    rim_recv,
):
    lat, lon = place()
    y, x, core = lat // 4, lon // 4, lax.rem(lon, 2)
    z = lax.rem(lat, 4) * 2 + lax.rem(lon, 4) // 2
    other = 1 - core
    slot = core * 4 + x

    loads = [
        pltpu.make_async_copy(tokens_hbm, frame.at[pl.ds(1, ROWS), pl.ds(COLS, COLS)], load_sem.at[0]),
        pltpu.make_async_copy(w_qkv_hbm, w_qkv, load_sem.at[1]),
        pltpu.make_async_copy(cot_hbm, cots.at[slot], load_sem.at[2]),
        pltpu.make_async_copy(w_out_hbm, w_out, load_sem.at[3]),
        pltpu.make_async_copy(w_disco_hbm, w_disco, load_sem.at[4]),
    ]
    for load in loads:
        load.start()

    around = neighbours(lat, lon)
    pair_peer = (lat, lon + 1 - 2 * core)
    x_peers = []
    for d in range(1, 4):
        there, back = lax.rem(x + d, 4), lax.rem(x + 4 - d, 4)
        x_peers.append((there, to_chip(y, z, there, core), to_chip(y, z, back, core)))
    z_peers = []
    for d in range(1, 8):
        there, back = lax.rem(z + d, 8), lax.rem(z + 8 - d, 8)
        z_peers.append((there, to_chip(y, there, x, core), to_chip(y, back, x, core)))
    owners = {}
    for job in range(2):
        for half in range(2):
            for to_core in range(2):
                row = (4 * job + half) + 2 * core
                mine = (row == y) & (core == to_core)
                owners[job, half, to_core] = (to_chip(row, z, x, to_core), mine)
    from_core = lax.rem(y, 4) // 2
    sources = []
    for k in range(8):
        mine = (y == k) & (core == from_core)
        sources.append((to_chip(k, z, x, from_core), mine))

    barrier = pltpu.get_barrier_semaphore()
    east = (lat, lax.rem(lon + 1, LONS))
    west = (lat, lax.rem(lon + LONS - 1, LONS))
    north = (lax.rem(lat + LATS - 1, LATS), lon)
    south = (lax.rem(lat + 1, LATS), lon)
    near = [east, west, north, south, pair_peer]
    for step in (1, 2, 3):
        near += [to_chip(y, z, lax.rem(x + step, 4), c) for c in (core, other)]
    for step in (1, 2, 6, 7):
        near.append(to_chip(y, lax.rem(z + step, 8), x, core))
        near += [to_chip(lax.rem(y + step, 8), z, x, c) for c in (core, other)]
    for target in near:
        pl.semaphore_signal(barrier, inc=1, device_id=target, device_id_type=MESH)
    pl.semaphore_wait(barrier, len(near))

    def halo_copy(idx, src, rows, cols, target):
        dst = frame.at[rows, cols]
        copy = remote(src, dst, halo_send.at[idx], halo_recv.at[idx], target)
        copy.start()
        return copy

    left, centre, right = (pl.ds(COLS * part, COLS) for part in range(3))
    first, last = pl.ds(0, 1), pl.ds(ROWS - 1, 1)
    above_row, below_row = pl.ds(0, 1), pl.ds(ROWS + 1, 1)
    halo_copies = [
        halo_copy(0, tokens_hbm.at[first], below_row, centre, north),
        halo_copy(1, tokens_hbm.at[last], above_row, centre, south),
        halo_copy(2, tokens_hbm, pl.ds(1, ROWS), left, east),
        halo_copy(3, tokens_hbm, pl.ds(1, ROWS), right, west),
    ]
    for step in (2, 6):
        for target in (
            to_chip(y, lax.rem(z + step, 8), x, core),
            to_chip(lax.rem(y + step, 8), z, x, core),
        ):
            pl.semaphore_signal(far_sem, inc=1, device_id=target, device_id_type=MESH)

    cot_copies = []
    for d, (_, target, _) in enumerate(x_peers):
        copy = remote(cot_hbm, cots.at[slot], cot_send.at[d], cot_recv.at[d], target)
        copy.start()
        cot_copies.append(copy)

    def ones_where(equal):
        return jnp.where(equal, 1.0, 0.0).astype(BF16)

    pos = lax.broadcasted_iota(jnp.int32, (C, 128), 0)
    lane = lax.broadcasted_iota(jnp.int32, (C, 128), 1)
    pos_z = lax.rem(pos // 6, 8)
    pos_y = (pos // 192) * 2 + lax.rem(pos // 3, 2)
    origin = 3 * (
        pos_y * 32 + (pos_z // 2) * 8 + lax.rem(pos // 48, 4) * 2 + lax.rem(pos_z, 2)
    ) + lax.rem(pos, 3)
    for t in range(3):
        perm_x[:, 128 * t : 128 * (t + 1)] = ones_where(lane + 128 * t == origin)
    pos = lax.broadcasted_iota(jnp.int32, (4 * CHUNK, 128), 0)
    lane = lax.broadcasted_iota(jnp.int32, (4 * CHUNK, 128), 1)
    pos_z = lax.rem(pos // 18, 8)
    origin = (
        288 * lax.rem(pos // 9, 2)
        + 72 * (pos_z // 2)
        + 18 * (pos // 144)
        + 9 * lax.rem(pos_z, 2)
        + lax.rem(pos, 9)
    )
    for t in range(5):
        perm_od[0, :, 128 * t : 128 * (t + 1)] = ones_where(lane + 128 * t == origin)
        perm_od[1, :, 128 * t : 128 * (t + 1)] = ones_where(lane + 128 * t - 64 == origin)

    stack = HEADS * COLS
    head_mask = ones_where(
        lax.broadcasted_iota(jnp.int32, (stack, C), 0) // COLS
        == lax.broadcasted_iota(jnp.int32, (stack, C), 1) // HEAD_DIM
    )
    lane_head = lax.broadcasted_iota(jnp.int32, (COLS, C), 1) // HEAD_DIM
    distance = jnp.abs(
        lax.broadcasted_iota(jnp.int32, (SPAN, stack), 0)
        - COLS
        - lax.rem(lax.broadcasted_iota(jnp.int32, (SPAN, stack), 1), COLS)
    )
    stack_head = lax.broadcasted_iota(jnp.int32, (1, stack), 1) // COLS
    bias_lane = lax.broadcasted_iota(jnp.int32, (HEADS, LATS * ROWS), 1)
    bias_rows = []
    for k in range(ROWS + 2):
        global_row = lat * ROWS - 1 + k
        clamped = jnp.clip(global_row, 0, LATS * ROWS - 1)
        biases = jnp.sum(
            jnp.where(bias_lane == clamped, bias_ref[...], 0.0), axis=1, keepdims=True
        )
        line = jnp.zeros((1, stack), F32)
        for h in range(HEADS):
            line = jnp.where(stack_head == h, biases[h : h + 1], line)
        valid = (global_row >= 0) & (global_row < LATS * ROWS)
        bias_rows.append(jnp.where(valid, line, FAR))

    for load in loads:
        load.wait()
    x_own = frame[1 : ROWS + 1, COLS : 2 * COLS].reshape(CELLS, C)
    cot = cots[slot].reshape(CELLS, C)
    queries = nn(x_own, w_qkv[:, :C]).astype(BF16)
    upstream = nt(cot, w_out[...]).astype(BF16)
    for idx, row in ((0, below_row), (1, above_row)):
        halo_copies[idx].wait()
        halo_copies.append(halo_copy(4 + idx, frame.at[row, centre], row, left, east))
        halo_copies.append(halo_copy(6 + idx, frame.at[row, centre], row, right, west))
    gs_ref[...] = nt(cot, w_disco[...]).astype(BF16).astype(F32)
    turned_own[...] = nt(perm_x[...], x_own).astype(BF16)
    canvas[...] = jnp.zeros_like(canvas)

    for copy in halo_copies[2:4]:
        copy.wait()
    middle = frame[1 : ROWS + 1].reshape(ROWS * SPAN, C)
    kv_ref[SPAN : SPAN + ROWS * SPAN] = nn(middle, w_qkv[:, C:]).astype(BF16)
    turned_mid[...] = nt(perm_x[...], middle).astype(BF16)
    for copy in halo_copies[4:]:
        copy.wait()

    @pl.when(lat == 0)
    def _():
        frame[0] = jnp.zeros((SPAN, C), BF16)

    @pl.when(lat == LATS - 1)
    def _():
        frame[ROWS + 1] = jnp.zeros((SPAN, C), BF16)

    edges = jnp.concatenate([frame[0], frame[ROWS + 1]], axis=0)
    edge_kv = nn(edges, w_qkv[:, C:]).astype(BF16)
    kv_ref[:SPAN] = edge_kv[:SPAN]
    kv_ref[FRAME - SPAN :] = edge_kv[SPAN:]

    for r in range(ROWS + 2):
        wide = frame[r, 16:80].astype(F32)
        shifted[0, r] = pltpu.roll(wide, 1, 0)[16:48]
        shifted[1, r] = wide[16:48]
        shifted[2, r] = pltpu.roll(wide, 63, 0)[16:48]
    for r in range(ROWS):
        for k in range(2):
            total = jnp.zeros((COLS, C), F32)
            for a in range(3):
                for b in range(3):
                    total = total + psi_ref[r, 9 * k + 3 * a + b] * shifted[b, r + a]
            mix_in[r * COLS : (r + 1) * COLS, (k + 1) * C : (k + 2) * C] = total.astype(BF16)

    def fold_heads(weights, channels, rows):
        folded = []
        for g in range(2):
            window = kv_ref[rows, channels + 128 * g : channels + 128 * g + 256]
            wide = tn(weights[:, 128 * g : 128 * (g + 1)], window)
            total = jnp.zeros((COLS, 256), F32)
            for h in range(4):
                total = jnp.where(
                    lane_head[:, 128 * g : 128 * g + 256] == 4 * g + h,
                    wide[h * COLS : (h + 1) * COLS],
                    total,
                )
            folded.append(total)
        first, second = folded
        return jnp.concatenate(
            [first[:, :128], first[:, 128:] + second[:, :128], second[:, 128:]], axis=1
        )

    def key_rows(r):
        return slice(r * SPAN, (r + 3) * SPAN)

    def all_heads(source, r):
        return jnp.concatenate([source[r * COLS : (r + 1) * COLS]] * HEADS, axis=0) * head_mask

    q_heads = [all_heads(queries, r) for r in range(ROWS)]
    u_heads = [all_heads(upstream, r) for r in range(ROWS)]
    for r in range(ROWS):
        outside = jnp.where(distance <= reach_ref[r], 0.0, FAR)
        added = jnp.concatenate([outside + bias_rows[r + a] for a in range(3)], axis=0)
        probs_ref[r] = nt(kv_ref[key_rows(r), :C], q_heads[r]) * SCALING + added
    for r in range(ROWS):
        logits = probs_ref[r]
        probs = jnp.exp(logits - jnp.max(logits, axis=0, keepdims=True))
        probs = probs * (1.0 / jnp.sum(probs, axis=0, keepdims=True))
        probs_ref[r] = probs
        low_ref[r] = probs.astype(BF16)
    for r in range(ROWS):
        mix_in[r * COLS : (r + 1) * COLS, :C] = fold_heads(low_ref[r], C, key_rows(r)).astype(BF16)

    for half in range(2):
        window = mix_in[:, 512 * half : 512 * half + 640]
        turned = nt(perm_od[half], window).astype(BF16)
        slices[4 * half : 4 * half + 4] = turned.reshape(4, CHUNK, CELLS)
    slice_copies = []
    for d in (2, 1, 3, 0):
        for c in range(2):
            if d or c:
                there = lax.rem(x + d, 4)
                to_core = other if c else core
                copy = remote(
                    slices.at[to_core * 4 + there],
                    slices_in.at[slot],
                    slice_send.at[2 * d + c],
                    slice_recv.at[2 * d + c],
                    to_chip(y, z, there, to_core),
                )
                copy.start()
                slice_copies.append(copy)
    slices_in[slot] = slices[slot]
    swaps = []
    for copy in cot_copies:
        copy.wait()
    for step in range(4):
        held = core * 4 + lax.rem(x + step, 4)
        copy = remote(cots.at[held], cots.at[held], swap_send.at[step], swap_recv.at[step], pair_peer)
        copy.start()
        swaps.append(copy)

    def pair_copy(job, step):
        there = lax.rem(x + step, 4)
        return remote(
            grads.at[job, other * 4 + there],
            pair_in.at[job, there],
            pair_send.at[job, step],
            pair_recv.at[job, step],
            pair_peer,
        )

    def send_pair(job):
        for step in (2, 1, 3, 0):
            pair_copy(job, step).start()

    def x_copy(job, d):
        return remote(
            x_out.at[job, d], x_in.at[job, d], x_send.at[job, d], x_recv.at[job, d], x_peers[d][1]
        )

    def z_copies(job):
        return [
            remote(
                z_out.at[job, there],
                z_in.at[job, d],
                z_send.at[job, d],
                z_recv.at[job, d],
                target,
            )
            for d, (there, target, _) in enumerate(z_peers)
        ]

    def last_copy(job, half, to_core):
        return remote(
            last_out.at[job, pl.ds(half * 32, 32)],
            last_in.at[y],
            last_send.at[job, 2 * half + to_core],
            last_recv.at[y],
            owners[job, half, to_core][0],
        )

    def send_x(job):
        for d in (1, 0, 2):
            there = x_peers[d][0]
            pair_copy(job, d + 1).wait()
            added = grads[job, core * 4 + there].astype(F32) + pair_in[job, there].astype(F32)
            x_out[job, d] = added.astype(BF16)
            x_copy(job, d).start()

    def send_z(job):
        if job == 1:
            for copy in swaps + slice_copies:
                copy.wait()
            whole_slice = jnp.concatenate([slices_in[k] for k in range(8)], axis=1)
            total = nn(whole_slice, cots[...].reshape(8 * CELLS, C))
        else:
            pair_copy(job, 0).wait()
            total = grads[job, slot].astype(F32) + pair_in[job, x].astype(F32)
            for d in range(3):
                x_copy(job, d).wait()
                total = total + x_in[job, d].astype(F32)
        total_ref[job, 0:8] = jnp.zeros((8, C), F32)
        total_ref[job, 8 : 8 + CHUNK] = total
        total_ref[job, 8 + CHUNK : 32 + CHUNK] = jnp.zeros((24, C), F32)
        for k in range(8):
            for half in range(2):
                for t in range(3):
                    lanes = slice(128 * t, 128 * (t + 1))
                    to = 64 * k + 32 * half + 9 * t
                    if job == 1:
                        first = 8 + 18 * k + 9 * half
                        pack_ref[job, to : to + 16] = total_ref[job, first : first + 16, lanes]
                    else:
                        for m in range(3):
                            first = 8 + 48 * m + 6 * k + 3 * half
                            pack_ref[job, to + 3 * m : to + 3 * m + 8] = total_ref[
                                job, first : first + 8, lanes
                            ]
        for k in range(8):
            z_out[job, k] = pack_ref[job, 64 * k : 64 * k + 64].astype(BF16)
        for copy in z_copies(job):
            copy.start()

    def send_last(job):
        total = z_out[job, z].astype(F32)
        for d, copy in enumerate(z_copies(job)):
            copy.wait()
            total = total + z_in[job, d].astype(F32)
        last_out[job] = total.astype(BF16)
        for half in range(2):
            for to_core in range(2):
                mine = owners[job, half, to_core][1]

                @pl.when(jnp.logical_not(mine))
                def _():
                    last_copy(job, half, to_core).start()

                @pl.when(mine)
                def _():
                    last_in[y] = last_out[job, half * 32 : half * 32 + 32]

    for r in range(ROWS):
        grad_prob = nt(kv_ref[key_rows(r), C:], u_heads[r]).astype(BF16).astype(F32)
        probs = probs_ref[r]
        mean = jnp.sum(probs * grad_prob, axis=0, keepdims=True)
        glow_ref[r] = (probs * (grad_prob - mean)).astype(BF16)
    for r in range(ROWS):
        cells = slice(r * COLS, (r + 1) * COLS)
        dq_ref[cells] = (fold_heads(glow_ref[r], 0, key_rows(r)) * SCALING).astype(BF16)
        canvas[key_rows(r), :C] += nn(glow_ref[r], q_heads[r]) * SCALING
        canvas[key_rows(r), C:] += nn(low_ref[r], u_heads[r])

    grad_query = dq_ref[...]
    kv_part = canvas[...].astype(BF16)
    kv_middle = kv_part[SPAN : SPAN + ROWS * SPAN]
    kv_edges = jnp.concatenate([kv_part[:SPAN], kv_part[FRAME - SPAN :]], axis=0)
    turned_edge[...] = nt(perm_x[...], edges).astype(BF16)

    def token_weights(half):
        lines = pl.ds(pl.multiple_of(192 * half, 64), 192)
        query_weight = nn(turned_own[lines], grad_query).astype(BF16)
        kv_weight = nn(turned_mid[lines], kv_middle) + nn(turned_edge[lines], kv_edges)
        kv_weight = kv_weight.astype(BF16)
        for c in range(4):
            part = slice(48 * c, 48 * (c + 1))
            grads[0, 4 * half + c, 0:48] = query_weight[part]
            grads[0, 4 * half + c, 48:96] = kv_weight[part, :C]
            grads[0, 4 * half + c, 96:144] = kv_weight[part, C:]

    token_weights(other)
    send_pair(0)
    token_weights(core)

    canvas[:, :C] = nt(kv_part, w_qkv[:, C:])
    send_x(0)
    query_part = nt(grad_query, w_qkv[:, :C])
    margin = jnp.zeros((16, C), F32)
    for row in range(ROWS + 2):
        spread = jnp.zeros((64, C), F32)
        for b in range(3):
            total = jnp.zeros((COLS, C), F32)
            for a in range(3):
                r = row - a
                if 0 <= r < ROWS:
                    for k in range(2):
                        total = total + (
                            psi_ref[r, 9 * k + 3 * a + b]
                            * gs_ref[r * COLS : (r + 1) * COLS, k * C : (k + 1) * C]
                        )
            total = jnp.concatenate([margin, total, margin], axis=0)
            spread = spread + (total if b == 1 else pltpu.roll(total, 63 if b == 0 else 1, 0))
        canvas[row * SPAN + 16 : row * SPAN + 80, :C] += spread
    rim_ref[...] = canvas[:, :C].astype(BF16).reshape(ROWS + 2, SPAN, C)
    rim_copies = []
    for idx, (row_step, col_step, target) in enumerate(around):
        if row_step == 0:
            src = rim_ref.at[pl.ds(1, ROWS), pl.ds((1 + col_step) * COLS, COLS)]
            dst = rim_in.at[0 if col_step == -1 else 1]
        else:
            row = 0 if row_step == -1 else ROWS + 1
            src = rim_ref.at[row, pl.ds((1 + col_step) * COLS, COLS)]
            dst = line_in.at[(0 if row_step == -1 else 3) + col_step + 1]
        copy = remote(src, dst, rim_send.at[idx], rim_recv.at[idx], target)
        copy.start()
        rim_copies.append(copy)
    for r in range(ROWS):
        at = (r + 1) * SPAN + COLS
        own_ref[r] = canvas[at : at + COLS, :C] + query_part[r * COLS : (r + 1) * COLS]

    pl.semaphore_wait(far_sem, 4)
    send_z(1)
    mixed = nn(mix_in[:, :C], w_out[...]) + nn(mix_in[:, C:], w_disco[...])
    mixed_ref[...] = mixed.astype(BF16).reshape(ROWS, COLS, C)
    mixed_store = pltpu.make_async_copy(mixed_ref, mixed_hbm, store_sem.at[0])
    mixed_store.start()
    send_z(0)
    send_last(1)

    for copy in rim_copies:
        copy.wait()
    above = jnp.where(lat > 0, 1.0, 0.0)
    below = jnp.where(lat < LATS - 1, 1.0, 0.0)
    for r in range(ROWS):
        summed = own_ref[r] + rim_in[0, r].astype(F32) + rim_in[1, r].astype(F32)
        for side in range(3):
            if r == 0:
                summed = summed + above * line_in[3 + side].astype(F32)
            if r == ROWS - 1:
                summed = summed + below * line_in[side].astype(F32)
        input_ref[r] = summed.astype(BF16)
    input_store = pltpu.make_async_copy(input_ref, input_hbm, store_sem.at[1])
    input_store.start()

    send_last(0)
    for k, (source, mine) in enumerate(sources):

        @pl.when(jnp.logical_not(mine))
        def _():
            remote(
                last_out.at[0, pl.ds(0, 32)],
                last_in.at[k],
                last_send.at[0, 0],
                last_recv.at[k],
                source,
            ).wait_recv()

    for (job, half, to_core), (_, mine) in owners.items():

        @pl.when(jnp.logical_not(mine))
        def _():
            last_copy(job, half, to_core).wait_send()

    mixed_store.wait()
    input_store.wait()


def whole(tokens, cotangent, w_qkv, w_out, w_disco, psi, reach, key_bias):
    vmem = pl.BlockSpec(memory_space=VMEM)
    smem = pl.BlockSpec(memory_space=pltpu.SMEM)
    anywhere = pl.BlockSpec(memory_space=pl.ANY)
    dma = pltpu.SemaphoreType.DMA
    return pl.pallas_call(
        whole_kernel,
        out_shape=(
            jax.ShapeDtypeStruct((ROWS, COLS, C), BF16),
            jax.ShapeDtypeStruct((ROWS, COLS, C), BF16),
            jax.ShapeDtypeStruct((8, 32, 128), BF16),
        ),
        in_specs=[anywhere] * 5 + [smem] * 2 + [vmem],
        out_specs=(anywhere, anywhere, vmem),
        scratch_shapes=[
            VMEM((ROWS, COLS, C), BF16),
            VMEM((ROWS, COLS, C), BF16),
            VMEM((ROWS + 2, SPAN, C), BF16),
            VMEM((8, ROWS, COLS, C), BF16),
            VMEM((8, CHUNK, CELLS), BF16),
            VMEM((8, CHUNK, CELLS), BF16),
            VMEM((C, 3 * C), BF16),
            VMEM((C, C), BF16),
            VMEM((2 * C, C), BF16),
            VMEM((C, C), BF16),
            VMEM((2, 4 * CHUNK, 640), BF16),
            VMEM((C, CELLS), BF16),
            VMEM((C, ROWS * SPAN), BF16),
            VMEM((C, 2 * SPAN), BF16),
            VMEM((FRAME, 2 * C), BF16),
            VMEM((FRAME, 2 * C), F32),
            VMEM((ROWS, 3 * SPAN, HEADS * COLS), F32),
            VMEM((ROWS, 3 * SPAN, HEADS * COLS), BF16),
            VMEM((ROWS, 3 * SPAN, HEADS * COLS), BF16),
            VMEM((3, ROWS + 2, COLS, C), F32),
            VMEM((CELLS, 3 * C), BF16),
            VMEM((CELLS, C), BF16),
            VMEM((CELLS, 2 * C), F32),
            VMEM((1, 8, CHUNK, C), BF16),
            VMEM((ROWS, COLS, C), F32),
            VMEM((ROWS + 2, SPAN, C), BF16),
            VMEM((1, 4, CHUNK, C), BF16),
            VMEM((1, 3, CHUNK, C), BF16),
            VMEM((1, 3, CHUNK, C), BF16),
            VMEM((2, CHUNK + 32, C), F32),
            VMEM((2, 8 * 64 + 16, 128), F32),
            VMEM((2, 8, 64, 128), BF16),
            VMEM((2, 7, 64, 128), BF16),
            VMEM((2, 64, 128), BF16),
            VMEM((2, ROWS, COLS, C), BF16),
            VMEM((6, COLS, C), BF16),
            pltpu.SemaphoreType.REGULAR,
            dma((5,)),
            dma((2,)),
            dma((3,)),
            dma((3,)),
            dma((4,)),
            dma((4,)),
            dma((8,)),
            dma((8,)),
            dma((8,)),
            dma((8,)),
            dma((1, 4)),
            dma((1, 4)),
            dma((1, 3)),
            dma((1, 3)),
            dma((2, 7)),
            dma((2, 7)),
            dma((2, 4)),
            dma((8,)),
            dma((8,)),
            dma((8,)),
        ],
        compiler_params=pltpu.CompilerParams(
            collective_id=0, has_side_effects=True, vmem_limit_bytes=LIMIT
        ),
    )(tokens, cotangent, w_qkv, w_out, w_disco, psi, reach, key_bias.T)


def finish_kernel(mixed_in, input_in, lines_ref, mixed_out, input_out, weight_ref):
    mixed_out[...] = mixed_in[...]
    input_out[...] = input_in[...]
    lat, lon = place()
    total = lines_ref[0].astype(F32)
    for k in range(1, 8):
        total = total + lines_ref[k].astype(F32)
    strips = []
    for row in range(9):
        origin = 3 * (row % 3) + row // 3
        for t in range(3):
            at, late = 9 * t + origin, 9 * t + row
            strips.append(jnp.where(lat < 16, total[at : at + 1], total[late : late + 1]))
    turned = [pltpu.roll(strip, 64, 1) for strip in strips[13:]]
    left = lax.broadcasted_iota(jnp.int32, (1, 128), 1) < 64
    first_core = lax.rem(lon, 2) == 0
    for j in range(14):
        later = turned[j] if j == 13 else jnp.where(left, turned[j], turned[j + 1])
        strip = jnp.where(first_core, strips[j], later).reshape(128)
        if j < 13:
            weight_ref[128 * j : 128 * (j + 1)] = strip
        else:
            weight_ref[128 * j : 128 * j + 64] = strip[:64]


def finish(mixed, input_grad, lines):
    vmem = pl.BlockSpec(memory_space=VMEM)
    return pl.pallas_call(
        finish_kernel,
        out_shape=(
            jax.ShapeDtypeStruct((ROWS, COLS, C), BF16),
            jax.ShapeDtypeStruct((ROWS, COLS, C), BF16),
            jax.ShapeDtypeStruct((9 * C // 2,), F32),
        ),
        in_specs=[vmem] * 3,
        out_specs=(vmem,) * 3,
    )(mixed, input_grad, lines)


def on_device(tokens, w_qkv, w_out, w_disco, psi, reach, key_bias, cotangent):
    mixed, input_grad, lines = whole(
        tokens, cotangent, w_qkv, w_out, w_disco, psi, reach, key_bias
    )
    return finish(mixed, input_grad, lines)


def solution(mesh):
    placed = (
        P("lat", "lon", None),
        P(),
        P(),
        P(),
        P("lat", None),
        P("lat"),
        P(),
        P("lat", "lon", None),
    )
    return jax.shard_map(
        on_device,
        mesh=mesh,
        in_specs=placed,
        out_specs=(P("lat", "lon", None), P("lat", "lon", None), P(("lat", "lon"))),
        check_vma=False,
    )
```

```python
import jax
import jax.numpy as jnp
from jax import lax
from jax.experimental import pallas as pl
from jax.experimental.pallas import tpu as pltpu
from jax.sharding import PartitionSpec as P

HEADS = 8
HEAD_DIM = 48
C = 384
ROWS = 4
COLS = 32
SPAN = 3 * COLS
FRAME = (ROWS + 2) * SPAN
CELLS = ROWS * COLS
LATS = 32
LONS = 16
CHUNK = 144
SCALING = HEAD_DIM ** (-0.5)
FAR = -1e30
MESH = pl.DeviceIdType.MESH
BF16 = jnp.bfloat16
F32 = jnp.float32
VMEM = pltpu.VMEM
LIMIT = 56 * 1024 * 1024


def nn(left, right):
    return lax.dot_general(left, right, (((1,), (0,)), ((), ())), preferred_element_type=F32)


def nt(left, right):
    return lax.dot_general(left, right, (((1,), (1,)), ((), ())), preferred_element_type=F32)


def tn(left, right):
    return lax.dot_general(left, right, (((0,), (0,)), ((), ())), preferred_element_type=F32)


def place():
    return lax.axis_index("lat"), lax.axis_index("lon")


def neighbours(lat, lon):
    found = []
    for row_step in (-1, 0, 1):
        for col_step in (-1, 0, 1):
            if row_step or col_step:
                target = (
                    lax.rem(lat + row_step + LATS, LATS),
                    lax.rem(lon + col_step + LONS, LONS),
                )
                found.append((row_step, col_step, target))
    return found


def to_chip(y, z, x, core):
    return (y * 4 + z // 2, x * 4 + lax.rem(z, 2) * 2 + core)


def remote(src, dst, send, recv, target):
    return pltpu.make_async_remote_copy(
        src_ref=src,
        dst_ref=dst,
        send_sem=send,
        recv_sem=recv,
        device_id=target,
        device_id_type=MESH,
    )


def whole_kernel(
    tokens_hbm,
    cot_hbm,
    w_qkv_hbm,
    w_out_hbm,
    w_disco_hbm,
    psi_ref,
    reach_ref,
    bias_ref,
    mixed_hbm,
    input_hbm,
    last_in,
    mixed_ref,
    input_ref,
    frame,
    cots,
    slices,
    slices_in,
    w_qkv,
    w_out,
    w_disco,
    perm_x,
    perm_od,
    turned_own,
    turned_mid,
    turned_edge,
    kv_ref,
    canvas,
    probs_ref,
    low_ref,
    glow_ref,
    shifted,
    mix_in,
    dq_ref,
    gs_ref,
    grads,
    own_ref,
    rim_ref,
    pair_in,
    x_out,
    x_in,
    total_ref,
    pack_ref,
    z_out,
    z_in,
    last_out,
    rim_in,
    line_in,
    far_sem,
    load_sem,
    store_sem,
    cot_send,
    cot_recv,
    swap_send,
    swap_recv,
    slice_send,
    slice_recv,
    halo_send,
    halo_recv,
    pair_send,
    pair_recv,
    x_send,
    x_recv,
    z_send,
    z_recv,
    last_send,
    last_recv,
    rim_send,
    rim_recv,
):
    lat, lon = place()
    y, x, core = lat // 4, lon // 4, lax.rem(lon, 2)
    z = lax.rem(lat, 4) * 2 + lax.rem(lon, 4) // 2
    other = 1 - core
    slot = core * 4 + x

    loads = [
        pltpu.make_async_copy(tokens_hbm, frame.at[pl.ds(1, ROWS), pl.ds(COLS, COLS)], load_sem.at[0]),
        pltpu.make_async_copy(w_qkv_hbm, w_qkv, load_sem.at[1]),
        pltpu.make_async_copy(cot_hbm, cots.at[slot], load_sem.at[2]),
        pltpu.make_async_copy(w_out_hbm, w_out, load_sem.at[3]),
        pltpu.make_async_copy(w_disco_hbm, w_disco, load_sem.at[4]),
    ]
    for load in loads:
        load.start()

    around = neighbours(lat, lon)
    pair_peer = (lat, lon + 1 - 2 * core)
    x_peers = []
    for d in range(1, 4):
        there, back = lax.rem(x + d, 4), lax.rem(x + 4 - d, 4)
        x_peers.append((there, to_chip(y, z, there, core), to_chip(y, z, back, core)))
    z_peers = []
    for d in range(1, 8):
        there, back = lax.rem(z + d, 8), lax.rem(z + 8 - d, 8)
        z_peers.append((there, to_chip(y, there, x, core), to_chip(y, back, x, core)))
    owners = {}
    for job in range(2):
        for half in range(2):
            for to_core in range(2):
                row = (4 * job + half) + 2 * core
                mine = (row == y) & (core == to_core)
                owners[job, half, to_core] = (to_chip(row, z, x, to_core), mine)
    from_core = lax.rem(y, 4) // 2
    sources = []
    for k in range(8):
        mine = (y == k) & (core == from_core)
        sources.append((to_chip(k, z, x, from_core), mine))

    barrier = pltpu.get_barrier_semaphore()
    east = (lat, lax.rem(lon + 1, LONS))
    west = (lat, lax.rem(lon + LONS - 1, LONS))
    north = (lax.rem(lat + LATS - 1, LATS), lon)
    south = (lax.rem(lat + 1, LATS), lon)
    near = [north, south, east, west, pair_peer]
    for step in (1, 2, 3):
        near += [to_chip(y, z, lax.rem(x + step, 4), c) for c in (core, other)]
    for step in (1, 2, 6, 7):
        near.append(to_chip(y, lax.rem(z + step, 8), x, core))
        near += [to_chip(lax.rem(y + step, 8), z, x, c) for c in (core, other)]
    for target in near:
        pl.semaphore_signal(barrier, inc=1, device_id=target, device_id_type=MESH)
    pl.semaphore_wait(barrier, len(near))

    def halo_copy(idx, src, rows, cols, target):
        dst = frame.at[rows, cols]
        copy = remote(src, dst, halo_send.at[idx], halo_recv.at[idx], target)
        copy.start()
        return copy

    left, centre, right = (pl.ds(COLS * part, COLS) for part in range(3))
    first, last = pl.ds(0, 1), pl.ds(ROWS - 1, 1)
    above_row, below_row = pl.ds(0, 1), pl.ds(ROWS + 1, 1)
    halo_copies = [
        halo_copy(0, tokens_hbm.at[first], below_row, centre, north),
        halo_copy(1, tokens_hbm.at[last], above_row, centre, south),
        halo_copy(2, tokens_hbm, pl.ds(1, ROWS), left, east),
        halo_copy(3, tokens_hbm, pl.ds(1, ROWS), right, west),
    ]
    for step in (2, 6):
        for target in (
            to_chip(y, lax.rem(z + step, 8), x, core),
            to_chip(lax.rem(y + step, 8), z, x, core),
        ):
            pl.semaphore_signal(far_sem, inc=1, device_id=target, device_id_type=MESH)

    cot_copies = []
    for d, (_, target, _) in enumerate(x_peers):
        copy = remote(cot_hbm, cots.at[slot], cot_send.at[d], cot_recv.at[d], target)
        copy.start()
        cot_copies.append(copy)

    def ones_where(equal):
        return jnp.where(equal, 1.0, 0.0).astype(BF16)

    pos = lax.broadcasted_iota(jnp.int32, (C, 128), 0)
    lane = lax.broadcasted_iota(jnp.int32, (C, 128), 1)
    pos_z = lax.rem(pos // 6, 8)
    pos_y = (pos // 192) * 2 + lax.rem(pos // 3, 2)
    origin = 3 * (
        pos_y * 32 + (pos_z // 2) * 8 + lax.rem(pos // 48, 4) * 2 + lax.rem(pos_z, 2)
    ) + lax.rem(pos, 3)
    for t in range(3):
        perm_x[:, 128 * t : 128 * (t + 1)] = ones_where(lane + 128 * t == origin)
    pos = lax.broadcasted_iota(jnp.int32, (4 * CHUNK, 128), 0)
    lane = lax.broadcasted_iota(jnp.int32, (4 * CHUNK, 128), 1)
    pos_z = lax.rem(pos // 18, 8)
    origin = (
        288 * lax.rem(pos // 9, 2)
        + 72 * (pos_z // 2)
        + 18 * (pos // 144)
        + 9 * lax.rem(pos_z, 2)
        + lax.rem(pos, 9)
    )
    for t in range(5):
        perm_od[0, :, 128 * t : 128 * (t + 1)] = ones_where(lane + 128 * t == origin)
        perm_od[1, :, 128 * t : 128 * (t + 1)] = ones_where(lane + 128 * t - 64 == origin)

    stack = HEADS * COLS
    head_mask = ones_where(
        lax.broadcasted_iota(jnp.int32, (stack, C), 0) // COLS
        == lax.broadcasted_iota(jnp.int32, (stack, C), 1) // HEAD_DIM
    )
    lane_head = lax.broadcasted_iota(jnp.int32, (COLS, C), 1) // HEAD_DIM
    distance = jnp.abs(
        lax.broadcasted_iota(jnp.int32, (SPAN, stack), 0)
        - COLS
        - lax.rem(lax.broadcasted_iota(jnp.int32, (SPAN, stack), 1), COLS)
    )
    stack_head = lax.broadcasted_iota(jnp.int32, (1, stack), 1) // COLS
    bias_lane = lax.broadcasted_iota(jnp.int32, (HEADS, LATS * ROWS), 1)
    bias_rows = []
    for k in range(ROWS + 2):
        global_row = lat * ROWS - 1 + k
        clamped = jnp.clip(global_row, 0, LATS * ROWS - 1)
        biases = jnp.sum(
            jnp.where(bias_lane == clamped, bias_ref[...], 0.0), axis=1, keepdims=True
        )
        line = jnp.zeros((1, stack), F32)
        for h in range(HEADS):
            line = jnp.where(stack_head == h, biases[h : h + 1], line)
        valid = (global_row >= 0) & (global_row < LATS * ROWS)
        bias_rows.append(jnp.where(valid, line, FAR))

    for load in loads:
        load.wait()
    x_own = frame[1 : ROWS + 1, COLS : 2 * COLS].reshape(CELLS, C)
    cot = cots[slot].reshape(CELLS, C)
    queries = nn(x_own, w_qkv[:, :C]).astype(BF16)
    upstream = nt(cot, w_out[...]).astype(BF16)
    for idx, row in ((0, below_row), (1, above_row)):
        halo_copies[idx].wait()
        halo_copies.append(halo_copy(4 + idx, frame.at[row, centre], row, left, east))
        halo_copies.append(halo_copy(6 + idx, frame.at[row, centre], row, right, west))
    gs_ref[...] = nt(cot, w_disco[...]).astype(BF16).astype(F32)
    turned_own[...] = nt(perm_x[...], x_own).astype(BF16)

    for copy in halo_copies[2:4]:
        copy.wait()
    middle = frame[1 : ROWS + 1].reshape(ROWS * SPAN, C)
    kv_ref[SPAN : SPAN + ROWS * SPAN] = nn(middle, w_qkv[:, C:]).astype(BF16)
    turned_mid[...] = nt(perm_x[...], middle).astype(BF16)
    for copy in halo_copies[4:]:
        copy.wait()

    @pl.when(lat == 0)
    def _():
        frame[0] = jnp.zeros((SPAN, C), BF16)

    @pl.when(lat == LATS - 1)
    def _():
        frame[ROWS + 1] = jnp.zeros((SPAN, C), BF16)

    edges = jnp.concatenate([frame[0], frame[ROWS + 1]], axis=0)
    edge_kv = nn(edges, w_qkv[:, C:]).astype(BF16)
    kv_ref[:SPAN] = edge_kv[:SPAN]
    kv_ref[FRAME - SPAN :] = edge_kv[SPAN:]

    for r in range(ROWS + 2):
        wide = frame[r, 16:80].astype(F32)
        shifted[0, r] = pltpu.roll(wide, 1, 0)[16:48]
        shifted[1, r] = wide[16:48]
        shifted[2, r] = pltpu.roll(wide, 63, 0)[16:48]
    for r in range(ROWS):
        for k in range(2):
            total = jnp.zeros((COLS, C), F32)
            for a in range(3):
                for b in range(3):
                    total = total + psi_ref[r, 9 * k + 3 * a + b] * shifted[b, r + a]
            mix_in[r * COLS : (r + 1) * COLS, (k + 1) * C : (k + 2) * C] = total.astype(BF16)

    def fold_heads(weights, channels, rows):
        folded = []
        for g in range(2):
            window = kv_ref[rows, channels + 128 * g : channels + 128 * g + 256]
            wide = tn(weights[:, 128 * g : 128 * (g + 1)], window)
            total = jnp.zeros((COLS, 256), F32)
            for h in range(4):
                total = jnp.where(
                    lane_head[:, 128 * g : 128 * g + 256] == 4 * g + h,
                    wide[h * COLS : (h + 1) * COLS],
                    total,
                )
            folded.append(total)
        first, second = folded
        return jnp.concatenate(
            [first[:, :128], first[:, 128:] + second[:, :128], second[:, 128:]], axis=1
        )

    def key_rows(r):
        return slice(r * SPAN, (r + 3) * SPAN)

    def all_heads(source, r):
        return jnp.concatenate([source[r * COLS : (r + 1) * COLS]] * HEADS, axis=0) * head_mask

    q_heads = [all_heads(queries, r) for r in range(ROWS)]
    u_heads = [all_heads(upstream, r) for r in range(ROWS)]
    for r in range(ROWS):
        outside = jnp.where(distance <= reach_ref[r], 0.0, FAR)
        added = jnp.concatenate([outside + bias_rows[r + a] for a in range(3)], axis=0)
        probs_ref[r] = nt(kv_ref[key_rows(r), :C], q_heads[r]) * SCALING + added
    for r in range(ROWS):
        logits = probs_ref[r]
        probs = jnp.exp(logits - jnp.max(logits, axis=0, keepdims=True))
        probs = probs * (1.0 / jnp.sum(probs, axis=0, keepdims=True))
        probs_ref[r] = probs
        low_ref[r] = probs.astype(BF16)
    for r in range(ROWS):
        mix_in[r * COLS : (r + 1) * COLS, :C] = fold_heads(low_ref[r], C, key_rows(r)).astype(BF16)

    for half in range(2):
        window = mix_in[:, 512 * half : 512 * half + 640]
        turned = nt(perm_od[half], window).astype(BF16)
        slices[4 * half : 4 * half + 4] = turned.reshape(4, CHUNK, CELLS)
    slice_copies = []
    for d in (2, 1, 3, 0):
        for c in range(2):
            if d or c:
                there = lax.rem(x + d, 4)
                to_core = other if c else core
                copy = remote(
                    slices.at[to_core * 4 + there],
                    slices_in.at[slot],
                    slice_send.at[2 * d + c],
                    slice_recv.at[2 * d + c],
                    to_chip(y, z, there, to_core),
                )
                copy.start()
                slice_copies.append(copy)
    slices_in[slot] = slices[slot]
    swaps = []
    for copy in cot_copies:
        copy.wait()
    for step in range(4):
        held = core * 4 + lax.rem(x + step, 4)
        copy = remote(cots.at[held], cots.at[held], swap_send.at[step], swap_recv.at[step], pair_peer)
        copy.start()
        swaps.append(copy)

    def pair_copy(job, step):
        there = lax.rem(x + step, 4)
        return remote(
            grads.at[job, other * 4 + there],
            pair_in.at[job, there],
            pair_send.at[job, step],
            pair_recv.at[job, step],
            pair_peer,
        )

    def send_pair(job):
        for step in (2, 1, 3, 0):
            pair_copy(job, step).start()

    def x_copy(job, d):
        return remote(
            x_out.at[job, d], x_in.at[job, d], x_send.at[job, d], x_recv.at[job, d], x_peers[d][1]
        )

    def z_copies(job):
        return [
            remote(
                z_out.at[job, there],
                z_in.at[job, d],
                z_send.at[job, d],
                z_recv.at[job, d],
                target,
            )
            for d, (there, target, _) in enumerate(z_peers)
        ]

    def last_copy(job, half, to_core):
        return remote(
            last_out.at[job, pl.ds(half * 32, 32)],
            last_in.at[y],
            last_send.at[job, 2 * half + to_core],
            last_recv.at[y],
            owners[job, half, to_core][0],
        )

    def send_x(job):
        for d in (1, 0, 2):
            there = x_peers[d][0]
            pair_copy(job, d + 1).wait()
            added = grads[job, core * 4 + there].astype(F32) + pair_in[job, there].astype(F32)
            x_out[job, d] = added.astype(BF16)
            x_copy(job, d).start()

    def send_z(job):
        if job == 1:
            for copy in swaps + slice_copies:
                copy.wait()
            whole_slice = jnp.concatenate([slices_in[k] for k in range(8)], axis=1)
            total = nn(whole_slice, cots[...].reshape(8 * CELLS, C))
        else:
            pair_copy(job, 0).wait()
            total = grads[job, slot].astype(F32) + pair_in[job, x].astype(F32)
            for d in (0, 2, 1):
                x_copy(job, d).wait()
                total = total + x_in[job, d].astype(F32)
        total_ref[job, 0:8] = jnp.zeros((8, C), F32)
        total_ref[job, 8 : 8 + CHUNK] = total
        total_ref[job, 8 + CHUNK : 32 + CHUNK] = jnp.zeros((24, C), F32)
        for k in range(8):
            for half in range(2):
                for t in range(3):
                    lanes = slice(128 * t, 128 * (t + 1))
                    to = 64 * k + 32 * half + 9 * t
                    if job == 1:
                        first = 8 + 18 * k + 9 * half
                        pack_ref[job, to : to + 16] = total_ref[job, first : first + 16, lanes]
                    else:
                        for m in range(3):
                            first = 8 + 48 * m + 6 * k + 3 * half
                            pack_ref[job, to + 3 * m : to + 3 * m + 8] = total_ref[
                                job, first : first + 8, lanes
                            ]
        for k in range(8):
            z_out[job, k] = pack_ref[job, 64 * k : 64 * k + 64].astype(BF16)
        for copy in z_copies(job):
            copy.start()

    def send_last(job):
        total = z_out[job, z].astype(F32)
        for d, copy in enumerate(z_copies(job)):
            copy.wait()
            total = total + z_in[job, d].astype(F32)
        last_out[job] = total.astype(BF16)
        for half in range(2):
            for to_core in range(2):
                mine = owners[job, half, to_core][1]

                @pl.when(jnp.logical_not(mine))
                def _():
                    last_copy(job, half, to_core).start()

                @pl.when(mine)
                def _():
                    last_in[y] = last_out[job, half * 32 : half * 32 + 32]

    for r in range(ROWS):
        grad_prob = nt(kv_ref[key_rows(r), C:], u_heads[r]).astype(BF16).astype(F32)
        probs = probs_ref[r]
        mean = jnp.sum(probs * grad_prob, axis=0, keepdims=True)
        glow_ref[r] = (probs * (grad_prob - mean)).astype(BF16)
    for r in range(ROWS):
        cells = slice(r * COLS, (r + 1) * COLS)
        dq_ref[cells] = (fold_heads(glow_ref[r], 0, key_rows(r)) * SCALING).astype(BF16)
        both = jnp.concatenate([nn(glow_ref[r], q_heads[r]), nn(low_ref[r], u_heads[r])], axis=1)
        if r == 0:
            canvas[key_rows(0)] = both
        else:
            begun = slice(r * SPAN, (r + 2) * SPAN)
            canvas[begun] += both[: 2 * SPAN]
            canvas[(r + 2) * SPAN : (r + 3) * SPAN] = both[2 * SPAN :]

    grad_query = dq_ref[...]
    kv_part = jnp.concatenate([canvas[:, :C] * SCALING, canvas[:, C:]], axis=1).astype(BF16)
    kv_middle = kv_part[SPAN : SPAN + ROWS * SPAN]
    kv_edges = jnp.concatenate([kv_part[:SPAN], kv_part[FRAME - SPAN :]], axis=0)
    turned_edge[...] = nt(perm_x[...], edges).astype(BF16)

    def token_weights(half):
        lines = pl.ds(pl.multiple_of(192 * half, 64), 192)
        query_weight = nn(turned_own[lines], grad_query).astype(BF16)
        kv_weight = nn(turned_mid[lines], kv_middle) + nn(turned_edge[lines], kv_edges)
        kv_weight = kv_weight.astype(BF16)
        for c in range(4):
            part = slice(48 * c, 48 * (c + 1))
            grads[0, 4 * half + c, 0:48] = query_weight[part]
            grads[0, 4 * half + c, 48:96] = kv_weight[part, :C]
            grads[0, 4 * half + c, 96:144] = kv_weight[part, C:]

    token_weights(other)
    send_pair(0)
    token_weights(core)

    canvas[:, :C] = nt(kv_part, w_qkv[:, C:])
    send_x(0)
    query_part = nt(grad_query, w_qkv[:, :C])
    margin = jnp.zeros((16, C), F32)
    for row in range(ROWS + 2):
        spread = jnp.zeros((64, C), F32)
        for b in range(3):
            total = jnp.zeros((COLS, C), F32)
            for a in range(3):
                r = row - a
                if 0 <= r < ROWS:
                    for k in range(2):
                        total = total + (
                            psi_ref[r, 9 * k + 3 * a + b]
                            * gs_ref[r * COLS : (r + 1) * COLS, k * C : (k + 1) * C]
                        )
            total = jnp.concatenate([margin, total, margin], axis=0)
            spread = spread + (total if b == 1 else pltpu.roll(total, 63 if b == 0 else 1, 0))
        canvas[row * SPAN + 16 : row * SPAN + 80, :C] += spread
    rim_ref[...] = canvas[:, :C].astype(BF16).reshape(ROWS + 2, SPAN, C)
    rim_copies = []
    for idx, (row_step, col_step, target) in enumerate(around):
        if row_step == 0:
            src = rim_ref.at[pl.ds(1, ROWS), pl.ds((1 + col_step) * COLS, COLS)]
            dst = rim_in.at[0 if col_step == -1 else 1]
        else:
            row = 0 if row_step == -1 else ROWS + 1
            src = rim_ref.at[row, pl.ds((1 + col_step) * COLS, COLS)]
            dst = line_in.at[(0 if row_step == -1 else 3) + col_step + 1]
        copy = remote(src, dst, rim_send.at[idx], rim_recv.at[idx], target)
        if row_step:
            copy.start()
        rim_copies.append(copy)
    for r in range(ROWS):
        at = (r + 1) * SPAN + COLS
        own_ref[r] = canvas[at : at + COLS, :C] + query_part[r * COLS : (r + 1) * COLS]

    pl.semaphore_wait(far_sem, 4)
    send_z(1)
    mixed = nn(mix_in[:, :C], w_out[...]) + nn(mix_in[:, C:], w_disco[...])
    mixed_ref[...] = mixed.astype(BF16).reshape(ROWS, COLS, C)
    mixed_store = pltpu.make_async_copy(mixed_ref, mixed_hbm, store_sem.at[0])
    mixed_store.start()
    send_z(0)
    for idx, (row_step, _, _) in enumerate(around):
        if row_step == 0:
            rim_copies[idx].start()
    send_last(1)

    send_last(0)

    for copy in rim_copies:
        copy.wait()
    above = jnp.where(lat > 0, 1.0, 0.0)
    below = jnp.where(lat < LATS - 1, 1.0, 0.0)
    for r in range(ROWS):
        summed = own_ref[r] + rim_in[0, r].astype(F32) + rim_in[1, r].astype(F32)
        for side in range(3):
            if r == 0:
                summed = summed + above * line_in[3 + side].astype(F32)
            if r == ROWS - 1:
                summed = summed + below * line_in[side].astype(F32)
        input_ref[r] = summed.astype(BF16)
    input_store = pltpu.make_async_copy(input_ref, input_hbm, store_sem.at[1])
    input_store.start()

    for k, (source, mine) in enumerate(sources):

        @pl.when(jnp.logical_not(mine))
        def _():
            remote(
                last_out.at[0, pl.ds(0, 32)],
                last_in.at[k],
                last_send.at[0, 0],
                last_recv.at[k],
                source,
            ).wait_recv()

    for (job, half, to_core), (_, mine) in owners.items():

        @pl.when(jnp.logical_not(mine))
        def _():
            last_copy(job, half, to_core).wait_send()

    mixed_store.wait()
    input_store.wait()


def whole(tokens, cotangent, w_qkv, w_out, w_disco, psi, reach, key_bias):
    vmem = pl.BlockSpec(memory_space=VMEM)
    smem = pl.BlockSpec(memory_space=pltpu.SMEM)
    anywhere = pl.BlockSpec(memory_space=pl.ANY)
    dma = pltpu.SemaphoreType.DMA
    return pl.pallas_call(
        whole_kernel,
        out_shape=(
            jax.ShapeDtypeStruct((ROWS, COLS, C), BF16),
            jax.ShapeDtypeStruct((ROWS, COLS, C), BF16),
            jax.ShapeDtypeStruct((8, 32, 128), BF16),
        ),
        in_specs=[anywhere] * 5 + [smem] * 2 + [vmem],
        out_specs=(anywhere, anywhere, vmem),
        scratch_shapes=[
            VMEM((ROWS, COLS, C), BF16),
            VMEM((ROWS, COLS, C), BF16),
            VMEM((ROWS + 2, SPAN, C), BF16),
            VMEM((8, ROWS, COLS, C), BF16),
            VMEM((8, CHUNK, CELLS), BF16),
            VMEM((8, CHUNK, CELLS), BF16),
            VMEM((C, 3 * C), BF16),
            VMEM((C, C), BF16),
            VMEM((2 * C, C), BF16),
            VMEM((C, C), BF16),
            VMEM((2, 4 * CHUNK, 640), BF16),
            VMEM((C, CELLS), BF16),
            VMEM((C, ROWS * SPAN), BF16),
            VMEM((C, 2 * SPAN), BF16),
            VMEM((FRAME, 2 * C), BF16),
            VMEM((FRAME, 2 * C), F32),
            VMEM((ROWS, 3 * SPAN, HEADS * COLS), F32),
            VMEM((ROWS, 3 * SPAN, HEADS * COLS), BF16),
            VMEM((ROWS, 3 * SPAN, HEADS * COLS), BF16),
            VMEM((3, ROWS + 2, COLS, C), F32),
            VMEM((CELLS, 3 * C), BF16),
            VMEM((CELLS, C), BF16),
            VMEM((CELLS, 2 * C), F32),
            VMEM((1, 8, CHUNK, C), BF16),
            VMEM((ROWS, COLS, C), F32),
            VMEM((ROWS + 2, SPAN, C), BF16),
            VMEM((1, 4, CHUNK, C), BF16),
            VMEM((1, 3, CHUNK, C), BF16),
            VMEM((1, 3, CHUNK, C), BF16),
            VMEM((2, CHUNK + 32, C), F32),
            VMEM((2, 8 * 64 + 16, 128), F32),
            VMEM((2, 8, 64, 128), BF16),
            VMEM((2, 7, 64, 128), BF16),
            VMEM((2, 64, 128), BF16),
            VMEM((2, ROWS, COLS, C), BF16),
            VMEM((6, COLS, C), BF16),
            pltpu.SemaphoreType.REGULAR,
            dma((5,)),
            dma((2,)),
            dma((3,)),
            dma((3,)),
            dma((4,)),
            dma((4,)),
            dma((8,)),
            dma((8,)),
            dma((8,)),
            dma((8,)),
            dma((1, 4)),
            dma((1, 4)),
            dma((1, 3)),
            dma((1, 3)),
            dma((2, 7)),
            dma((2, 7)),
            dma((2, 4)),
            dma((8,)),
            dma((8,)),
            dma((8,)),
        ],
        compiler_params=pltpu.CompilerParams(
            collective_id=0, has_side_effects=True, vmem_limit_bytes=LIMIT
        ),
    )(tokens, cotangent, w_qkv, w_out, w_disco, psi, reach, key_bias.T)


def finish_kernel(mixed_in, input_in, lines_ref, mixed_out, input_out, weight_ref):
    mixed_out[...] = mixed_in[...]
    input_out[...] = input_in[...]
    lat, lon = place()
    total = lines_ref[0].astype(F32)
    for k in range(1, 8):
        total = total + lines_ref[k].astype(F32)
    strips = []
    for row in range(9):
        origin = 3 * (row % 3) + row // 3
        for t in range(3):
            at, late = 9 * t + origin, 9 * t + row
            strips.append(jnp.where(lat < 16, total[at : at + 1], total[late : late + 1]))
    turned = [pltpu.roll(strip, 64, 1) for strip in strips[13:]]
    left = lax.broadcasted_iota(jnp.int32, (1, 128), 1) < 64
    first_core = lax.rem(lon, 2) == 0
    for j in range(14):
        later = turned[j] if j == 13 else jnp.where(left, turned[j], turned[j + 1])
        strip = jnp.where(first_core, strips[j], later).reshape(128)
        if j < 13:
            weight_ref[128 * j : 128 * (j + 1)] = strip
        else:
            weight_ref[128 * j : 128 * j + 64] = strip[:64]


def finish(mixed, input_grad, lines):
    vmem = pl.BlockSpec(memory_space=VMEM)
    return pl.pallas_call(
        finish_kernel,
        out_shape=(
            jax.ShapeDtypeStruct((ROWS, COLS, C), BF16),
            jax.ShapeDtypeStruct((ROWS, COLS, C), BF16),
            jax.ShapeDtypeStruct((9 * C // 2,), F32),
        ),
        in_specs=[vmem] * 3,
        out_specs=(vmem,) * 3,
    )(mixed, input_grad, lines)


def on_device(tokens, w_qkv, w_out, w_disco, psi, reach, key_bias, cotangent):
    mixed, input_grad, lines = whole(
        tokens, cotangent, w_qkv, w_out, w_disco, psi, reach, key_bias
    )
    return finish(mixed, input_grad, lines)


def solution(mesh):
    placed = (
        P("lat", "lon", None),
        P(),
        P(),
        P(),
        P("lat", None),
        P("lat"),
        P(),
        P("lat", "lon", None),
    )
    return jax.shard_map(
        on_device,
        mesh=mesh,
        in_specs=placed,
        out_specs=(P("lat", "lon", None), P("lat", "lon", None), P(("lat", "lon"))),
        check_vma=False,
    )
```

```python
import jax
import jax.numpy as jnp
from jax import lax
from jax.experimental import pallas as pl
from jax.experimental.pallas import tpu as pltpu
from jax.sharding import PartitionSpec as P

HEADS = 8
HEAD_DIM = 48
C = 384
ROWS = 4
COLS = 32
SPAN = 3 * COLS
FRAME = (ROWS + 2) * SPAN
CELLS = ROWS * COLS
LATS = 32
LONS = 16
CHUNK = 144
SCALING = HEAD_DIM ** (-0.5)
FAR = -1e30
MESH = pl.DeviceIdType.MESH
BF16 = jnp.bfloat16
F32 = jnp.float32
VMEM = pltpu.VMEM
LIMIT = 56 * 1024 * 1024


def nn(left, right):
    return lax.dot_general(left, right, (((1,), (0,)), ((), ())), preferred_element_type=F32)


def nt(left, right):
    return lax.dot_general(left, right, (((1,), (1,)), ((), ())), preferred_element_type=F32)


def tn(left, right):
    return lax.dot_general(left, right, (((0,), (0,)), ((), ())), preferred_element_type=F32)


def place():
    return lax.axis_index("lat"), lax.axis_index("lon")


def neighbours(lat, lon):
    found = []
    for row_step in (-1, 0, 1):
        for col_step in (-1, 0, 1):
            if row_step or col_step:
                target = (
                    lax.rem(lat + row_step + LATS, LATS),
                    lax.rem(lon + col_step + LONS, LONS),
                )
                found.append((row_step, col_step, target))
    return found


def to_chip(y, z, x, core):
    return (y * 4 + z // 2, x * 4 + lax.rem(z, 2) * 2 + core)


def remote(src, dst, send, recv, target):
    return pltpu.make_async_remote_copy(
        src_ref=src,
        dst_ref=dst,
        send_sem=send,
        recv_sem=recv,
        device_id=target,
        device_id_type=MESH,
    )


def whole_kernel(
    tokens_hbm,
    cot_hbm,
    w_qkv_hbm,
    w_out_hbm,
    w_disco_hbm,
    psi_ref,
    reach_ref,
    bias_ref,
    mixed_hbm,
    input_hbm,
    last_in,
    mixed_ref,
    input_ref,
    frame,
    cots,
    slices,
    slices_in,
    w_qkv,
    w_out,
    w_disco,
    perm_x,
    perm_od,
    turned_own,
    turned_mid,
    turned_edge,
    kv_ref,
    canvas,
    probs_ref,
    low_ref,
    glow_ref,
    shifted,
    mix_in,
    dq_ref,
    gs_ref,
    grads,
    own_ref,
    rim_ref,
    pair_in,
    x_out,
    x_in,
    total_ref,
    pack_ref,
    z_out,
    z_in,
    last_out,
    rim_in,
    line_in,
    far_sem,
    load_sem,
    store_sem,
    cot_send,
    cot_recv,
    swap_send,
    swap_recv,
    slice_send,
    slice_recv,
    halo_send,
    halo_recv,
    pair_send,
    pair_recv,
    x_send,
    x_recv,
    z_send,
    z_recv,
    last_send,
    last_recv,
    rim_send,
    rim_recv,
):
    lat, lon = place()
    y, x, core = lat // 4, lon // 4, lax.rem(lon, 2)
    z = lax.rem(lat, 4) * 2 + lax.rem(lon, 4) // 2
    other = 1 - core
    slot = core * 4 + x

    loads = [
        pltpu.make_async_copy(tokens_hbm, frame.at[pl.ds(1, ROWS), pl.ds(COLS, COLS)], load_sem.at[0]),
        pltpu.make_async_copy(w_qkv_hbm, w_qkv, load_sem.at[1]),
        pltpu.make_async_copy(cot_hbm, cots.at[slot], load_sem.at[2]),
        pltpu.make_async_copy(w_out_hbm, w_out, load_sem.at[3]),
        pltpu.make_async_copy(w_disco_hbm, w_disco, load_sem.at[4]),
    ]
    for load in loads:
        load.start()

    around = neighbours(lat, lon)
    pair_peer = (lat, lon + 1 - 2 * core)
    x_peers = []
    for d in range(1, 4):
        there, back = lax.rem(x + d, 4), lax.rem(x + 4 - d, 4)
        x_peers.append((there, to_chip(y, z, there, core), to_chip(y, z, back, core)))
    z_peers = []
    for d in range(1, 8):
        there, back = lax.rem(z + d, 8), lax.rem(z + 8 - d, 8)
        z_peers.append((there, to_chip(y, there, x, core), to_chip(y, back, x, core)))
    owners = {}
    for job in range(2):
        for half in range(2):
            for to_core in range(2):
                row = (4 * job + half) + 2 * core
                mine = (row == y) & (core == to_core)
                owners[job, half, to_core] = (to_chip(row, z, x, to_core), mine)
    from_core = lax.rem(y, 4) // 2
    sources = []
    for k in range(8):
        mine = (y == k) & (core == from_core)
        sources.append((to_chip(k, z, x, from_core), mine))

    barrier = pltpu.get_barrier_semaphore()
    east = (lat, lax.rem(lon + 1, LONS))
    west = (lat, lax.rem(lon + LONS - 1, LONS))
    north = (lax.rem(lat + LATS - 1, LATS), lon)
    south = (lax.rem(lat + 1, LATS), lon)
    near = [north, south, east, west, pair_peer]
    for step in (1, 2, 3):
        near += [to_chip(y, z, lax.rem(x + step, 4), c) for c in (core, other)]
    for step in (1, 2, 6, 7):
        near.append(to_chip(y, lax.rem(z + step, 8), x, core))
        near += [to_chip(lax.rem(y + step, 8), z, x, c) for c in (core, other)]
    for target in near:
        pl.semaphore_signal(barrier, inc=1, device_id=target, device_id_type=MESH)
    pl.semaphore_wait(barrier, len(near))

    def halo_copy(idx, src, rows, cols, target):
        dst = frame.at[rows, cols]
        copy = remote(src, dst, halo_send.at[idx], halo_recv.at[idx], target)
        copy.start()
        return copy

    left, centre, right = (pl.ds(COLS * part, COLS) for part in range(3))
    first, last = pl.ds(0, 1), pl.ds(ROWS - 1, 1)
    above_row, below_row = pl.ds(0, 1), pl.ds(ROWS + 1, 1)
    halo_copies = [
        halo_copy(0, tokens_hbm.at[first], below_row, centre, north),
        halo_copy(1, tokens_hbm.at[last], above_row, centre, south),
    ]
    cot_copies = []
    for d, (_, target, _) in enumerate(x_peers):
        copy = remote(cot_hbm, cots.at[slot], cot_send.at[d], cot_recv.at[d], target)
        copy.start()
        cot_copies.append(copy)
    halo_copies += [
        halo_copy(2, tokens_hbm, pl.ds(1, ROWS), left, east),
        halo_copy(3, tokens_hbm, pl.ds(1, ROWS), right, west),
    ]
    for step in (2, 6):
        for target in (
            to_chip(y, lax.rem(z + step, 8), x, core),
            to_chip(lax.rem(y + step, 8), z, x, core),
        ):
            pl.semaphore_signal(far_sem, inc=1, device_id=target, device_id_type=MESH)

    def ones_where(equal):
        return jnp.where(equal, 1.0, 0.0).astype(BF16)

    pos = lax.broadcasted_iota(jnp.int32, (C, 128), 0)
    lane = lax.broadcasted_iota(jnp.int32, (C, 128), 1)
    pos_z = lax.rem(pos // 6, 8)
    pos_y = (pos // 192) * 2 + lax.rem(pos // 3, 2)
    origin = 3 * (
        pos_y * 32 + (pos_z // 2) * 8 + lax.rem(pos // 48, 4) * 2 + lax.rem(pos_z, 2)
    ) + lax.rem(pos, 3)
    for t in range(3):
        perm_x[:, 128 * t : 128 * (t + 1)] = ones_where(lane + 128 * t == origin)
    pos = lax.broadcasted_iota(jnp.int32, (4 * CHUNK, 128), 0)
    lane = lax.broadcasted_iota(jnp.int32, (4 * CHUNK, 128), 1)
    pos_z = lax.rem(pos // 18, 8)
    origin = (
        288 * lax.rem(pos // 9, 2)
        + 72 * (pos_z // 2)
        + 18 * (pos // 144)
        + 9 * lax.rem(pos_z, 2)
        + lax.rem(pos, 9)
    )
    for t in range(5):
        perm_od[0, :, 128 * t : 128 * (t + 1)] = ones_where(lane + 128 * t == origin)
        perm_od[1, :, 128 * t : 128 * (t + 1)] = ones_where(lane + 128 * t - 64 == origin)

    stack = HEADS * COLS
    head_mask = ones_where(
        lax.broadcasted_iota(jnp.int32, (stack, C), 0) // COLS
        == lax.broadcasted_iota(jnp.int32, (stack, C), 1) // HEAD_DIM
    )
    lane_head = lax.broadcasted_iota(jnp.int32, (COLS, C), 1) // HEAD_DIM
    distance = jnp.abs(
        lax.broadcasted_iota(jnp.int32, (SPAN, stack), 0)
        - COLS
        - lax.rem(lax.broadcasted_iota(jnp.int32, (SPAN, stack), 1), COLS)
    )
    stack_head = lax.broadcasted_iota(jnp.int32, (1, stack), 1) // COLS
    bias_lane = lax.broadcasted_iota(jnp.int32, (HEADS, LATS * ROWS), 1)
    bias_rows = []
    for k in range(ROWS + 2):
        global_row = lat * ROWS - 1 + k
        clamped = jnp.clip(global_row, 0, LATS * ROWS - 1)
        biases = jnp.sum(
            jnp.where(bias_lane == clamped, bias_ref[...], 0.0), axis=1, keepdims=True
        )
        line = jnp.zeros((1, stack), F32)
        for h in range(HEADS):
            line = jnp.where(stack_head == h, biases[h : h + 1], line)
        valid = (global_row >= 0) & (global_row < LATS * ROWS)
        bias_rows.append(jnp.where(valid, line, FAR))

    for load in loads:
        load.wait()
    x_own = frame[1 : ROWS + 1, COLS : 2 * COLS].reshape(CELLS, C)
    cot = cots[slot].reshape(CELLS, C)
    queries = nn(x_own, w_qkv[:, :C]).astype(BF16)
    upstream = nt(cot, w_out[...]).astype(BF16)
    for idx, row in ((0, below_row), (1, above_row)):
        halo_copies[idx].wait()
        halo_copies.append(halo_copy(4 + idx, frame.at[row, centre], row, left, east))
        halo_copies.append(halo_copy(6 + idx, frame.at[row, centre], row, right, west))
    gs_ref[...] = nt(cot, w_disco[...]).astype(BF16).astype(F32)
    turned_own[...] = nt(perm_x[...], x_own).astype(BF16)

    for copy in halo_copies[2:4]:
        copy.wait()
    middle = frame[1 : ROWS + 1].reshape(ROWS * SPAN, C)
    kv_ref[SPAN : SPAN + ROWS * SPAN] = nn(middle, w_qkv[:, C:]).astype(BF16)
    turned_mid[...] = nt(perm_x[...], middle).astype(BF16)
    for copy in halo_copies[4:]:
        copy.wait()

    @pl.when(lat == 0)
    def _():
        frame[0] = jnp.zeros((SPAN, C), BF16)

    @pl.when(lat == LATS - 1)
    def _():
        frame[ROWS + 1] = jnp.zeros((SPAN, C), BF16)

    edges = jnp.concatenate([frame[0], frame[ROWS + 1]], axis=0)
    edge_kv = nn(edges, w_qkv[:, C:]).astype(BF16)
    kv_ref[:SPAN] = edge_kv[:SPAN]
    kv_ref[FRAME - SPAN :] = edge_kv[SPAN:]

    for r in range(ROWS + 2):
        wide = frame[r, 16:80].astype(F32)
        shifted[0, r] = pltpu.roll(wide, 1, 0)[16:48]
        shifted[1, r] = wide[16:48]
        shifted[2, r] = pltpu.roll(wide, 63, 0)[16:48]
    for r in range(ROWS):
        for k in range(2):
            total = jnp.zeros((COLS, C), F32)
            for a in range(3):
                for b in range(3):
                    total = total + psi_ref[r, 9 * k + 3 * a + b] * shifted[b, r + a]
            mix_in[r * COLS : (r + 1) * COLS, (k + 1) * C : (k + 2) * C] = total.astype(BF16)

    def fold_heads(weights, channels, rows):
        folded = []
        for g in range(2):
            window = kv_ref[rows, channels + 128 * g : channels + 128 * g + 256]
            wide = tn(weights[:, 128 * g : 128 * (g + 1)], window)
            total = jnp.zeros((COLS, 256), F32)
            for h in range(4):
                total = jnp.where(
                    lane_head[:, 128 * g : 128 * g + 256] == 4 * g + h,
                    wide[h * COLS : (h + 1) * COLS],
                    total,
                )
            folded.append(total)
        first, second = folded
        return jnp.concatenate(
            [first[:, :128], first[:, 128:] + second[:, :128], second[:, 128:]], axis=1
        )

    def key_rows(r):
        return slice(r * SPAN, (r + 3) * SPAN)

    def all_heads(source, r):
        return jnp.concatenate([source[r * COLS : (r + 1) * COLS]] * HEADS, axis=0) * head_mask

    q_heads = [all_heads(queries, r) for r in range(ROWS)]
    u_heads = [all_heads(upstream, r) for r in range(ROWS)]
    for r in range(ROWS):
        outside = jnp.where(distance <= reach_ref[r], 0.0, FAR)
        added = jnp.concatenate([outside + bias_rows[r + a] for a in range(3)], axis=0)
        probs_ref[r] = nt(kv_ref[key_rows(r), :C], q_heads[r]) * SCALING + added
    for r in range(ROWS):
        logits = probs_ref[r]
        probs = jnp.exp(logits - jnp.max(logits, axis=0, keepdims=True))
        probs = probs * (1.0 / jnp.sum(probs, axis=0, keepdims=True))
        probs_ref[r] = probs
        low_ref[r] = probs.astype(BF16)
    for r in range(ROWS):
        mix_in[r * COLS : (r + 1) * COLS, :C] = fold_heads(low_ref[r], C, key_rows(r)).astype(BF16)

    for half in range(2):
        window = mix_in[:, 512 * half : 512 * half + 640]
        turned = nt(perm_od[half], window).astype(BF16)
        slices[4 * half : 4 * half + 4] = turned.reshape(4, CHUNK, CELLS)
    slice_copies = []
    for d in (2, 1, 3, 0):
        for c in range(2):
            if d or c:
                there = lax.rem(x + d, 4)
                to_core = other if c else core
                copy = remote(
                    slices.at[to_core * 4 + there],
                    slices_in.at[slot],
                    slice_send.at[2 * d + c],
                    slice_recv.at[2 * d + c],
                    to_chip(y, z, there, to_core),
                )
                copy.start()
                slice_copies.append(copy)
    slices_in[slot] = slices[slot]
    swaps = []
    for copy in cot_copies:
        copy.wait()
    for step in range(4):
        held = core * 4 + lax.rem(x + step, 4)
        copy = remote(cots.at[held], cots.at[held], swap_send.at[step], swap_recv.at[step], pair_peer)
        copy.start()
        swaps.append(copy)

    def pair_copy(job, step):
        there = lax.rem(x + step, 4)
        return remote(
            grads.at[job, other * 4 + there],
            pair_in.at[job, there],
            pair_send.at[job, step],
            pair_recv.at[job, step],
            pair_peer,
        )

    def send_pair(job):
        for step in (2, 1, 3, 0):
            pair_copy(job, step).start()

    def x_copy(job, d):
        return remote(
            x_out.at[job, d], x_in.at[job, d], x_send.at[job, d], x_recv.at[job, d], x_peers[d][1]
        )

    def z_copies(job):
        return [
            remote(
                z_out.at[job, there],
                z_in.at[job, d],
                z_send.at[job, d],
                z_recv.at[job, d],
                target,
            )
            for d, (there, target, _) in enumerate(z_peers)
        ]

    def last_copy(job, half, to_core):
        return remote(
            last_out.at[job, pl.ds(half * 32, 32)],
            last_in.at[y],
            last_send.at[job, 2 * half + to_core],
            last_recv.at[y],
            owners[job, half, to_core][0],
        )

    def send_x(job):
        for d in (1, 0, 2):
            there = x_peers[d][0]
            pair_copy(job, d + 1).wait()
            added = grads[job, core * 4 + there].astype(F32) + pair_in[job, there].astype(F32)
            x_out[job, d] = added.astype(BF16)
            x_copy(job, d).start()

    def send_z(job):
        if job == 1:
            for copy in swaps + slice_copies:
                copy.wait()
            whole_slice = jnp.concatenate([slices_in[k] for k in range(8)], axis=1)
            total = nn(whole_slice, cots[...].reshape(8 * CELLS, C))
        else:
            pair_copy(job, 0).wait()
            total = grads[job, slot].astype(F32) + pair_in[job, x].astype(F32)
            for d in (0, 2, 1):
                x_copy(job, d).wait()
                total = total + x_in[job, d].astype(F32)
        total_ref[job, 0:8] = jnp.zeros((8, C), F32)
        total_ref[job, 8 : 8 + CHUNK] = total
        total_ref[job, 8 + CHUNK : 32 + CHUNK] = jnp.zeros((24, C), F32)
        for k in range(8):
            for half in range(2):
                for t in range(3):
                    lanes = slice(128 * t, 128 * (t + 1))
                    to = 64 * k + 32 * half + 9 * t
                    if job == 1:
                        first = 8 + 18 * k + 9 * half
                        pack_ref[job, to : to + 16] = total_ref[job, first : first + 16, lanes]
                    else:
                        for m in range(3):
                            first = 8 + 48 * m + 6 * k + 3 * half
                            pack_ref[job, to + 3 * m : to + 3 * m + 8] = total_ref[
                                job, first : first + 8, lanes
                            ]
        for k in range(8):
            z_out[job, k] = pack_ref[job, 64 * k : 64 * k + 64].astype(BF16)
        for copy in z_copies(job):
            copy.start()

    def send_last(job):
        total = z_out[job, z].astype(F32)
        for d, copy in enumerate(z_copies(job)):
            copy.wait()
            total = total + z_in[job, d].astype(F32)
        last_out[job] = total.astype(BF16)
        for half in range(2):
            for to_core in range(2):
                mine = owners[job, half, to_core][1]

                @pl.when(jnp.logical_not(mine))
                def _():
                    last_copy(job, half, to_core).start()

                @pl.when(mine)
                def _():
                    last_in[y] = last_out[job, half * 32 : half * 32 + 32]

    for r in range(ROWS):
        grad_prob = nt(kv_ref[key_rows(r), C:], u_heads[r]).astype(BF16).astype(F32)
        probs = probs_ref[r]
        mean = jnp.sum(probs * grad_prob, axis=0, keepdims=True)
        glow_ref[r] = (probs * (grad_prob - mean)).astype(BF16)
    for r in range(ROWS):
        cells = slice(r * COLS, (r + 1) * COLS)
        dq_ref[cells] = (fold_heads(glow_ref[r], 0, key_rows(r)) * SCALING).astype(BF16)
        both = jnp.concatenate([nn(glow_ref[r], q_heads[r]), nn(low_ref[r], u_heads[r])], axis=1)
        if r == 0:
            canvas[key_rows(0)] = both
        else:
            begun = slice(r * SPAN, (r + 2) * SPAN)
            canvas[begun] += both[: 2 * SPAN]
            canvas[(r + 2) * SPAN : (r + 3) * SPAN] = both[2 * SPAN :]

    grad_query = dq_ref[...]
    kv_part = jnp.concatenate([canvas[:, :C] * SCALING, canvas[:, C:]], axis=1).astype(BF16)
    kv_middle = kv_part[SPAN : SPAN + ROWS * SPAN]
    kv_edges = jnp.concatenate([kv_part[:SPAN], kv_part[FRAME - SPAN :]], axis=0)
    turned_edge[...] = nt(perm_x[...], edges).astype(BF16)

    def token_weights(half):
        lines = pl.ds(pl.multiple_of(192 * half, 64), 192)
        query_weight = nn(turned_own[lines], grad_query).astype(BF16)
        kv_weight = nn(turned_mid[lines], kv_middle) + nn(turned_edge[lines], kv_edges)
        kv_weight = kv_weight.astype(BF16)
        for c in range(4):
            part = slice(48 * c, 48 * (c + 1))
            grads[0, 4 * half + c, 0:48] = query_weight[part]
            grads[0, 4 * half + c, 48:96] = kv_weight[part, :C]
            grads[0, 4 * half + c, 96:144] = kv_weight[part, C:]

    token_weights(other)
    send_pair(0)
    token_weights(core)

    send_x(0)
    canvas[:, :C] = nt(kv_part, w_qkv[:, C:])
    query_part = nt(grad_query, w_qkv[:, :C])
    margin = jnp.zeros((16, C), F32)
    for row in range(ROWS + 2):
        spread = jnp.zeros((64, C), F32)
        for b in range(3):
            total = jnp.zeros((COLS, C), F32)
            for a in range(3):
                r = row - a
                if 0 <= r < ROWS:
                    for k in range(2):
                        total = total + (
                            psi_ref[r, 9 * k + 3 * a + b]
                            * gs_ref[r * COLS : (r + 1) * COLS, k * C : (k + 1) * C]
                        )
            total = jnp.concatenate([margin, total, margin], axis=0)
            spread = spread + (total if b == 1 else pltpu.roll(total, 63 if b == 0 else 1, 0))
        canvas[row * SPAN + 16 : row * SPAN + 80, :C] += spread
    rim_ref[...] = canvas[:, :C].astype(BF16).reshape(ROWS + 2, SPAN, C)
    rim_copies = []
    for idx, (row_step, col_step, target) in enumerate(around):
        if row_step == 0:
            src = rim_ref.at[pl.ds(1, ROWS), pl.ds((1 + col_step) * COLS, COLS)]
            dst = rim_in.at[0 if col_step == -1 else 1]
        else:
            row = 0 if row_step == -1 else ROWS + 1
            src = rim_ref.at[row, pl.ds((1 + col_step) * COLS, COLS)]
            dst = line_in.at[(0 if row_step == -1 else 3) + col_step + 1]
        copy = remote(src, dst, rim_send.at[idx], rim_recv.at[idx], target)
        if row_step:
            copy.start()
        rim_copies.append(copy)
    for r in range(ROWS):
        at = (r + 1) * SPAN + COLS
        own_ref[r] = canvas[at : at + COLS, :C] + query_part[r * COLS : (r + 1) * COLS]

    pl.semaphore_wait(far_sem, 4)
    send_z(1)
    mixed = nn(mix_in[:, :C], w_out[...]) + nn(mix_in[:, C:], w_disco[...])
    mixed_ref[...] = mixed.astype(BF16).reshape(ROWS, COLS, C)
    mixed_store = pltpu.make_async_copy(mixed_ref, mixed_hbm, store_sem.at[0])
    mixed_store.start()
    send_z(0)
    for idx, (row_step, _, _) in enumerate(around):
        if row_step == 0:
            rim_copies[idx].start()
    send_last(1)

    send_last(0)

    for copy in rim_copies:
        copy.wait()
    above = jnp.where(lat > 0, 1.0, 0.0)
    below = jnp.where(lat < LATS - 1, 1.0, 0.0)
    for r in range(ROWS):
        summed = own_ref[r] + rim_in[0, r].astype(F32) + rim_in[1, r].astype(F32)
        for side in range(3):
            if r == 0:
                summed = summed + above * line_in[3 + side].astype(F32)
            if r == ROWS - 1:
                summed = summed + below * line_in[side].astype(F32)
        input_ref[r] = summed.astype(BF16)
    input_store = pltpu.make_async_copy(input_ref, input_hbm, store_sem.at[1])
    input_store.start()

    for k, (source, mine) in enumerate(sources):

        @pl.when(jnp.logical_not(mine))
        def _():
            remote(
                last_out.at[0, pl.ds(0, 32)],
                last_in.at[k],
                last_send.at[0, 0],
                last_recv.at[k],
                source,
            ).wait_recv()

    for (job, half, to_core), (_, mine) in owners.items():

        @pl.when(jnp.logical_not(mine))
        def _():
            last_copy(job, half, to_core).wait_send()

    mixed_store.wait()
    input_store.wait()


def whole(tokens, cotangent, w_qkv, w_out, w_disco, psi, reach, key_bias):
    vmem = pl.BlockSpec(memory_space=VMEM)
    smem = pl.BlockSpec(memory_space=pltpu.SMEM)
    anywhere = pl.BlockSpec(memory_space=pl.ANY)
    dma = pltpu.SemaphoreType.DMA
    return pl.pallas_call(
        whole_kernel,
        out_shape=(
            jax.ShapeDtypeStruct((ROWS, COLS, C), BF16),
            jax.ShapeDtypeStruct((ROWS, COLS, C), BF16),
            jax.ShapeDtypeStruct((8, 32, 128), BF16),
        ),
        in_specs=[anywhere] * 5 + [smem] * 2 + [vmem],
        out_specs=(anywhere, anywhere, vmem),
        scratch_shapes=[
            VMEM((ROWS, COLS, C), BF16),
            VMEM((ROWS, COLS, C), BF16),
            VMEM((ROWS + 2, SPAN, C), BF16),
            VMEM((8, ROWS, COLS, C), BF16),
            VMEM((8, CHUNK, CELLS), BF16),
            VMEM((8, CHUNK, CELLS), BF16),
            VMEM((C, 3 * C), BF16),
            VMEM((C, C), BF16),
            VMEM((2 * C, C), BF16),
            VMEM((C, C), BF16),
            VMEM((2, 4 * CHUNK, 640), BF16),
            VMEM((C, CELLS), BF16),
            VMEM((C, ROWS * SPAN), BF16),
            VMEM((C, 2 * SPAN), BF16),
            VMEM((FRAME, 2 * C), BF16),
            VMEM((FRAME, 2 * C), F32),
            VMEM((ROWS, 3 * SPAN, HEADS * COLS), F32),
            VMEM((ROWS, 3 * SPAN, HEADS * COLS), BF16),
            VMEM((ROWS, 3 * SPAN, HEADS * COLS), BF16),
            VMEM((3, ROWS + 2, COLS, C), F32),
            VMEM((CELLS, 3 * C), BF16),
            VMEM((CELLS, C), BF16),
            VMEM((CELLS, 2 * C), F32),
            VMEM((1, 8, CHUNK, C), BF16),
            VMEM((ROWS, COLS, C), F32),
            VMEM((ROWS + 2, SPAN, C), BF16),
            VMEM((1, 4, CHUNK, C), BF16),
            VMEM((1, 3, CHUNK, C), BF16),
            VMEM((1, 3, CHUNK, C), BF16),
            VMEM((2, CHUNK + 32, C), F32),
            VMEM((2, 8 * 64 + 16, 128), F32),
            VMEM((2, 8, 64, 128), BF16),
            VMEM((2, 7, 64, 128), BF16),
            VMEM((2, 64, 128), BF16),
            VMEM((2, ROWS, COLS, C), BF16),
            VMEM((6, COLS, C), BF16),
            pltpu.SemaphoreType.REGULAR,
            dma((5,)),
            dma((2,)),
            dma((3,)),
            dma((3,)),
            dma((4,)),
            dma((4,)),
            dma((8,)),
            dma((8,)),
            dma((8,)),
            dma((8,)),
            dma((1, 4)),
            dma((1, 4)),
            dma((1, 3)),
            dma((1, 3)),
            dma((2, 7)),
            dma((2, 7)),
            dma((2, 4)),
            dma((8,)),
            dma((8,)),
            dma((8,)),
        ],
        compiler_params=pltpu.CompilerParams(
            collective_id=0, has_side_effects=True, vmem_limit_bytes=LIMIT
        ),
    )(tokens, cotangent, w_qkv, w_out, w_disco, psi, reach, key_bias.T)


def finish_kernel(mixed_in, input_in, lines_ref, mixed_out, input_out, weight_ref):
    mixed_out[...] = mixed_in[...]
    input_out[...] = input_in[...]
    lat, lon = place()
    total = lines_ref[0].astype(F32)
    for k in range(1, 8):
        total = total + lines_ref[k].astype(F32)
    strips = []
    for row in range(9):
        origin = 3 * (row % 3) + row // 3
        for t in range(3):
            at, late = 9 * t + origin, 9 * t + row
            strips.append(jnp.where(lat < 16, total[at : at + 1], total[late : late + 1]))
    turned = [pltpu.roll(strip, 64, 1) for strip in strips[13:]]
    left = lax.broadcasted_iota(jnp.int32, (1, 128), 1) < 64
    first_core = lax.rem(lon, 2) == 0
    for j in range(14):
        later = turned[j] if j == 13 else jnp.where(left, turned[j], turned[j + 1])
        strip = jnp.where(first_core, strips[j], later).reshape(128)
        if j < 13:
            weight_ref[128 * j : 128 * (j + 1)] = strip
        else:
            weight_ref[128 * j : 128 * j + 64] = strip[:64]


def finish(mixed, input_grad, lines):
    vmem = pl.BlockSpec(memory_space=VMEM)
    return pl.pallas_call(
        finish_kernel,
        out_shape=(
            jax.ShapeDtypeStruct((ROWS, COLS, C), BF16),
            jax.ShapeDtypeStruct((ROWS, COLS, C), BF16),
            jax.ShapeDtypeStruct((9 * C // 2,), F32),
        ),
        in_specs=[vmem] * 3,
        out_specs=(vmem,) * 3,
    )(mixed, input_grad, lines)


def on_device(tokens, w_qkv, w_out, w_disco, psi, reach, key_bias, cotangent):
    mixed, input_grad, lines = whole(
        tokens, cotangent, w_qkv, w_out, w_disco, psi, reach, key_bias
    )
    return finish(mixed, input_grad, lines)


def solution(mesh):
    placed = (
        P("lat", "lon", None),
        P(),
        P(),
        P(),
        P("lat", None),
        P("lat"),
        P(),
        P("lat", "lon", None),
    )
    return jax.shard_map(
        on_device,
        mesh=mesh,
        in_specs=placed,
        out_specs=(P("lat", "lon", None), P("lat", "lon", None), P(("lat", "lon"))),
        check_vma=False,
    )
```
